32 devices in a mesh: wide: 8 (over z, y), narrow: 4 (over x, core).
Axes of the slice: x: 2, y: 2, z: 4, core: 2. Of those that a mesh axis runs over, the one named last changes fastest.
Arguments:
- kept_tokens: bfloat16 [32, 32, 7, 1152], P(('wide', 'narrow')), may hold values from -6 to 6
- keep_mask: int32 [32, 256], P(('wide', 'narrow')), may hold values from 0 to 1, as said below
- conditioning: float32 [32, 1152], P(('wide', 'narrow')), may hold values from -6 to 6
- ada_weight: float32 [1152, 6912], P(('wide', 'narrow')), may hold values from -0.1875 to 0.1875
- ada_bias: float32 [6912], P(('wide', 'narrow')), may hold values from -3 to 3
- qkv_weight: float32 [1152, 3456], P(('wide', 'narrow')), may hold values from -0.1875 to 0.1875
- out_weight: float32 [1152, 1152], P(('wide', 'narrow')), may hold values from -0.75 to 0.75
- up_weight: float32 [1152, 4608], P(('wide', 'narrow')), may hold values from -0.1875 to 0.1875
- down_weight: float32 [4608, 1152], P(('wide', 'narrow')), may hold values from -0.09375 to 0.09375
- position_bias: float32 [16, 31, 31], replicated, may hold values from -5 to 5
- mask_token: float32 [1152], P(('wide', 'narrow')), may hold values from -5 to 5
- cotangent: bfloat16 [8192, 1152], P(('wide', 'narrow')), may hold values from -6 to 6
Outputs:
- block_out: bfloat16 [8192, 1152], P(('wide', 'narrow'))
- grad_kept: bfloat16 [32, 32, 7, 1152], P(('wide', 'narrow'))
- grad_cond: float32 [32, 1152], P(('wide', 'narrow'))
- grad_ada_weight: float32 [1152, 6912], P(('wide', 'narrow'))
- grad_ada_bias: float32 [6912], P(('wide', 'narrow'))
- grad_qkv_weight: float32 [1152, 3456], P(('wide', 'narrow'))
- grad_out_weight: float32 [1152, 1152], P(('wide', 'narrow'))
- grad_up_weight: float32 [1152, 4608], P(('wide', 'narrow'))
- grad_down_weight: float32 [4608, 1152], P(('wide', 'narrow'))
- grad_position_bias: float32 [16, 31, 31], replicated
- grad_mask_token: float32 [1152], P(('wide', 'narrow'))
The draws below stay inside these ranges and needn't reach their ends.
Inputs may be any that keep to these rules, and one draw needn't show every extreme that they name: `keep_mask`: each image masks between 48 and 104 of its 256 tokens; the 1 images of one device keep at most 208 tokens together, and some device keeps exactly 208.
All inputs are finite; a program needn't handle non-finite values.
Results may differ from the reference program's by a relative error of at most 0.014.
The reference program's roundings to bfloat16 on the way count: a program that leaves them out, or rounds other values in their place, can miss the bound.
Values may be sent and summed in bfloat16 or wider, within the bound.
A program may use at most 384 MiB of HBM per device.

```python
import math
import jax
import jax.numpy as jnp
from jax import lax

D = 1152
HEADS = 16
HEAD_DIM = 72
FF = 4608
GRID = 16
PATCHES = 256
OFFSETS = 31
IMG_DEV = 1
IMAGES = 32
TOKENS = 8192
MASK_LO = 48
MASK_HI = 104
CAP = 7
N_WIDE = 8
N_NARROW = 4


def draw_keep_mask(key, part):
    base = jax.random.fold_in(key, 11)
    count_key, order_key, pick_key = jax.random.split(base, 3)
    masked = jax.random.randint(count_key, (IMAGES,), MASK_LO, MASK_HI + 1)
    holders = IMAGES // IMG_DEV
    chosen = jax.random.randint(pick_key, (), 0, holders)
    owner = jnp.arange(IMAGES, dtype=jnp.int32) // IMG_DEV
    masked = jnp.where(owner == chosen, MASK_LO, masked)
    image_keys = jax.random.split(order_key, IMAGES)
    orders = jax.vmap(lambda one_key: jax.random.permutation(one_key, PATCHES))(image_keys)
    places = jnp.argsort(orders, axis=1, stable=True)
    return (places >= masked[:, None]).astype(jnp.int32)


def shard_levels(rng, dims, shards, low, high):
    loudness = 1.0
    for dim, shards_of in shards:
        steps = jax.random.uniform(jax.random.fold_in(jax.random.fold_in(rng, 6), dim), (shards_of,), jnp.float32, low / len(shards), high / len(shards))
        loudness = loudness * jnp.repeat(jnp.exp(steps), dims[dim] // shards_of).reshape((-1,) + (1,) * (len(dims) - 1 - dim))
    return loudness


def gaussian(rng, shape, spread, bound, cuts=(), held_as=jnp.bfloat16):
    factor_of = shard_levels(rng, shape, cuts, -0.22, 0.18) if cuts else 1.0
    drawn = jax.random.normal(rng, shape, jnp.float32) * spread * factor_of
    return jnp.minimum(jnp.maximum(drawn, -bound), bound).astype(held_as)


def setup_inputs(seed: int = 0) -> dict:
    arg_keys = jax.random.split(jax.random.key(seed), 13)
    return {
        "kept_tokens": gaussian(arg_keys[0], (N_WIDE * N_NARROW, N_WIDE * N_NARROW, CAP, D), 1.0, 6.0, ((0, 32),)),
        "keep_mask": draw_keep_mask(jax.random.fold_in(arg_keys[12], 71), 0),
        "conditioning": gaussian(arg_keys[2], (IMAGES, D), 1.0, 6.0, ((0, 32),), jnp.float32),
        "ada_weight": gaussian(arg_keys[3], (D, 6 * D), D ** -0.5, 0.1875, ((0, 32),), jnp.float32),
        "ada_bias": gaussian(arg_keys[4], (6 * D,), 0.5, 3.0, ((0, 32),), jnp.float32),
        "qkv_weight": gaussian(arg_keys[5], (D, 3 * D), D ** -0.5, 0.1875, ((0, 32),), jnp.float32),
        "out_weight": gaussian(arg_keys[6], (D, D), (D // 16) ** -0.5, 0.75, ((0, 32),), jnp.float32),
        "up_weight": gaussian(arg_keys[7], (D, FF), D ** -0.5, 0.1875, ((0, 32),), jnp.float32),
        "down_weight": gaussian(arg_keys[8], (FF, D), FF ** -0.5, 0.09375, ((0, 32),), jnp.float32),
        "position_bias": gaussian(arg_keys[9], (HEADS, OFFSETS, OFFSETS), 1.0, 5.0, (), jnp.float32),
        "mask_token": gaussian(arg_keys[10], (D,), 1.0, 5.0, ((0, 32),), jnp.float32),
        "cotangent": gaussian(arg_keys[11], (TOKENS, D), 1.0, 6.0, ((0, 32),)),
    }


EPSILON = 1e-06

@jax.custom_vjp
def low(v):
    return lax.optimization_barrier(v.astype(jnp.bfloat16)).astype(jnp.float32)

@jax.custom_vjp
def low_back(v):
    return v

def low_keep(v):
    return (low(v), None)

def low_pass(kept, grad):
    return (grad,)

def back_keep(v):
    return (v, None)

def back_low(kept, grad):
    return (low(grad),)
low.defvjp(low_keep, low_pass)
low_back.defvjp(back_keep, back_low)

def matmul(left, right):
    return jnp.dot(left, right, precision=lax.Precision.HIGHEST, preferred_element_type=jnp.float32)

def layer_norm(stream):
    center = stream - lax.optimization_barrier(jnp.mean(stream, axis=-1, keepdims=True))
    variance = lax.optimization_barrier(jnp.mean(center * center, axis=-1, keepdims=True))
    return center * lax.rsqrt(variance + EPSILON)

def expand_bias(table):
    places = jnp.arange(PATCHES, dtype=jnp.int32)
    rows_y = places // GRID
    cols_x = places % GRID
    index_y = (rows_y[:, None] - rows_y[None, :] + GRID - 1).astype(jnp.int32)
    index_x = (cols_x[:, None] - cols_x[None, :] + GRID - 1).astype(jnp.int32)
    return table[:, index_y, index_x]

def group_forward(params, received, keep_group, cond_group):
    ada_weight, ada_bias, qkv_weight, out_weight, up_weight, down_weight, position_bias, mask_token = params
    images = cond_group.shape[0]
    count = images * PATCHES
    devices = N_WIDE * N_NARROW
    keep_float = keep_group.astype(jnp.float32)
    ranks = jnp.cumsum(keep_group) - 1
    target = ranks % devices * CAP + ranks // devices
    columns = jnp.arange(devices * CAP, dtype=jnp.int32)
    selector = jnp.where((keep_group[:, None] == 1) & (target[:, None] == columns[None, :]), 1.0, 0.0).astype(jnp.float32)
    stream_in = matmul(selector, received) + (1.0 - keep_float)[:, None] * mask_token[None, :]
    stream_in = stream_in.reshape(images, PATCHES, D)
    modulation = low_back(matmul(low(jax.nn.silu(cond_group)), ada_weight) + ada_bias[None, :])
    shift_one, scale_one, gate_one, shift_two, scale_two, gate_two = jnp.split(modulation[:, None, :], 6, axis=-1)
    normed_one = low(layer_norm(stream_in) * (1.0 + scale_one) + shift_one).reshape(count, D)
    projected = low_back(low(matmul(normed_one, qkv_weight))).reshape(images, PATCHES, 3, HEADS, HEAD_DIM)
    queries = projected[:, :, 0]
    key_rows = projected[:, :, 1]
    value_rows = projected[:, :, 2]
    scale = 1.0 / math.sqrt(HEAD_DIM)
    scores = jnp.einsum('iqhd,ikhd->ihqk', queries, key_rows, precision=lax.Precision.HIGHEST)
    scores = low_back(scores * scale + expand_bias(position_bias)[None])
    att_weights = jax.nn.softmax(scores, axis=-1)
    mixed = jnp.einsum('ihqk,ikhd->iqhd', low(att_weights), value_rows, precision=lax.Precision.HIGHEST)
    mixed = low_back(low(mixed)).reshape(count, D)
    branch = low_back(matmul(mixed, out_weight)).reshape(images, PATCHES, D)
    stream_mid = stream_in + gate_one * branch
    normed_two = low(layer_norm(stream_mid) * (1.0 + scale_two) + shift_two).reshape(count, D)
    hidden = low_back(matmul(normed_two, up_weight))
    activated = low(jax.nn.gelu(hidden, approximate=True))
    down = low_back(matmul(activated, down_weight)).reshape(images, PATCHES, D)
    return (stream_mid + gate_two * down).reshape(count, D)

def reference(kept_tokens, keep_mask, conditioning, ada_weight, ada_bias, qkv_weight, out_weight, up_weight, down_weight, position_bias, mask_token, cotangent):
    devices = N_WIDE * N_NARROW
    groups = IMAGES // IMG_DEV

    def forward(kept, cond, *params):
        lowered = tuple((low(weight) for weight in params[:6])) + (params[6], low(params[7]))
        received = jnp.transpose(low_back(kept), (1, 0, 2, 3)).reshape(groups, devices * CAP, D)
        keep_groups = keep_mask.reshape(groups, IMG_DEV * PATCHES)
        cond_groups = cond.reshape(groups, IMG_DEV, D)

        def one_group(inputs):
            return group_forward(lowered, inputs[0], inputs[1], inputs[2])
        outputs = lax.map(jax.checkpoint(one_group), (received, keep_groups, cond_groups))
        return outputs.reshape(TOKENS, D)
    floats = tuple((item.astype(jnp.float32) for item in (kept_tokens, conditioning, ada_weight, ada_bias, qkv_weight, out_weight, up_weight, down_weight, position_bias, mask_token)))
    result, pull = jax.vjp(forward, *floats)
    grads = pull(cotangent.astype(jnp.float32))
    return (result.astype(jnp.bfloat16), grads[0].astype(jnp.bfloat16), grads[1], grads[2], grads[3], grads[4], grads[5], grads[6], grads[7], grads[8], grads[9])
```

```python
import functools
import math

import jax
import jax.numpy as jnp
from jax import lax
from jax.experimental import pallas as pl
from jax.experimental.pallas import tpu as pltpu
from jax.sharding import PartitionSpec as P

D = 1152
HEADS = 16
HEAD_DIM = 72
FF = 4608
GRID = 16
PATCHES = 256


EPSILON = 1e-06


def layer_norm(stream):
    center = stream - jnp.mean(stream, axis=-1, keepdims=True)
    variance = jnp.mean(center * center, axis=-1, keepdims=True)
    return center * lax.rsqrt(variance + EPSILON)


def modulate(stream, shift, scale):
    return layer_norm(stream) * (1.0 + scale) + shift


def offset_picker(grid):
    places = jnp.arange(grid, dtype=jnp.int32)
    spread = jnp.arange(2 * grid - 1, dtype=jnp.int32)
    return (
        places[:, None, None] - places[None, :, None] + grid - 1 == spread[None, None, :]
    ).astype(jnp.float32)


def expand_bias(table, grid):
    picker = offset_picker(grid)
    partial_rows = jnp.einsum("yka,had->hykd", picker, table, precision=lax.Precision.HIGHEST)
    expanded = jnp.einsum("hykd,xjd->hyxkj", partial_rows, picker, precision=lax.Precision.HIGHEST)
    return expanded.reshape(table.shape[0], grid * grid, grid * grid)


def bias_adjoint(grad_bias, grid):
    picker = offset_picker(grid)
    shaped = grad_bias.reshape(grad_bias.shape[0], grid, grid, grid, grid)
    partial_rows = jnp.einsum("hyxkj,xjd->hykd", shaped, picker, precision=lax.Precision.HIGHEST)
    return jnp.einsum("hykd,yka->had", partial_rows, picker, precision=lax.Precision.HIGHEST)


def gelu_tanh(value):
    return jax.nn.gelu(value, approximate=True)


MESH = pl.DeviceIdType.MESH
LAG = 1
ROWS = 144

PARTS = ((0, 80, "zxy"), (80, 64, "zyx"))

def rels(zc):
    return [(rz, ry, rx) for rz in range(zc) for ry in range(2) for rx in range(2)]

def place():
    wide = lax.axis_index("wide")
    narrow = lax.axis_index("narrow")
    return wide // 2, wide % 2, narrow // 2, narrow % 2

def arrive_dim(rel, order):
    val = {"z": rel[0], "y": rel[1], "x": rel[2]}
    last = -1
    for i, dname in enumerate(order):
        if val[dname]:
            last = i
    return last

def gather_kernel(zc, groups, src, out, send_sem, recv_sem, sib_send, sib_recv, own_sem):
    z, y, x, c = place()
    wcount = 2 * zc
    def dev(rz, ry, rx, cc):
        return (lax.rem(z + rz, zc) * 2 + (y + ry) % 2, ((x + rx) % 2) * 2 + cc)
    def unit_of(g, rel, cc):
        w = lax.rem(z + zc - rel[0], zc) * 2 + (y + rel[1]) % 2
        n = ((x + rel[2]) % 2) * 2 + cc
        return w * 4 + n if g == 2 else n * wcount + w
    peers = [(k, 0, 0) for k in range(1, zc)] + [(0, 1, 0), (0, 0, 1)]
    barrier = pltpu.get_barrier_semaphore()
    for p in peers:
        pl.semaphore_signal(barrier, inc=1, device_id=dev(*p, c), device_id_type=MESH)
    pl.semaphore_signal(barrier, inc=1, device_id=dev(0, 0, 0, 1 - c), device_id_type=MESH)
    pl.semaphore_wait(barrier, len(peers) + 1)
    allrel = rels(zc)
    ridx = {r: i for i, r in enumerate(allrel)}

    def add(a, b):
        return ((a[0] + b[0]) % zc, (a[1] + b[1]) % 2, (a[2] + b[2]) % 2)

    def forward(g, p, rel):
        r0, rows, order = PARTS[p]
        at = arrive_dim(rel, order)
        first = rel == (0, 0, 0)
        u = unit_of(g, rel, c)
        block = src.at[g, pl.ds(r0, rows)] if first else out.at[g, u, pl.ds(r0, rows)]
        for dname in order[at + 1:]:
            hops = {"z": [(k, 0, 0) for k in range(1, zc)], "y": [(0, 1, 0)], "x": [(0, 0, 1)]}[dname]
            for h in hops:
                there = add(rel, h)
                pltpu.make_async_remote_copy(
                    src_ref=block, dst_ref=out.at[g, u, pl.ds(r0, rows)],
                    send_sem=send_sem.at[g, p], recv_sem=recv_sem.at[g, p, ridx[there]],
                    device_id=dev(*h, c), device_id_type=MESH).start()
        pltpu.make_async_remote_copy(
            src_ref=block, dst_ref=out.at[g, u, pl.ds(r0, rows)],
            send_sem=sib_send.at[g, p], recv_sem=sib_recv.at[g, p],
            device_id=dev(0, 0, 0, 1 - c), device_id_type=MESH).start()

    def wait_bytes(sem, g, p, units):
        r0, rows, _ = PARTS[p]
        ref = out.at[g, pl.ds(0, units), pl.ds(r0, rows)]
        pltpu.make_async_copy(ref, ref, sem).wait()

    def depth(rel):
        return sum(1 for v in rel if v)
    own = [pltpu.make_async_copy(src.at[g], out.at[g, unit_of(g, (0, 0, 0), c)], own_sem.at[g]) for g in groups]
    for g in groups:
        for p in range(len(PARTS)):
            forward(g, p, (0, 0, 0))
    for cp in own:
        cp.start()
    for g in groups:
        for dd in (1, 2, 3):
            for rel in allrel:
                if depth(rel) != dd:
                    continue
                for p in range(len(PARTS)):
                    r0, rows, order = PARTS[p]
                    ref = out.at[g, 0, pl.ds(r0, rows)]
                    pltpu.make_async_copy(ref, ref, recv_sem.at[g, p, ridx[rel]]).wait()
                    forward(g, p, rel)
        for p in range(len(PARTS)):
            wait_bytes(sib_recv.at[g, p], g, p, 4 * zc)
            wait_bytes(send_sem.at[g, p], g, p, 4 * zc - 1)
            wait_bytes(sib_send.at[g, p], g, p, 4 * zc)
    for cp in own:
        cp.wait()

def gather(src, zc):
    ng = src.shape[0]
    np_ = len(PARTS)
    return pl.pallas_call(
        functools.partial(gather_kernel, zc, range(ng)),
        out_shape=jax.ShapeDtypeStruct((ng, 8 * zc, ROWS, D), jnp.bfloat16),
        in_specs=[pl.BlockSpec(memory_space=pl.ANY)],
        out_specs=pl.BlockSpec(memory_space=pl.ANY),
        scratch_shapes=[
            pltpu.SemaphoreType.DMA((ng, np_)),
            pltpu.SemaphoreType.DMA((ng, np_, 4 * zc)),
            pltpu.SemaphoreType.DMA((ng, np_)),
            pltpu.SemaphoreType.DMA((ng, np_)),
            pltpu.SemaphoreType.DMA((ng,)),
        ],
        compiler_params=pltpu.CompilerParams(collective_id=1, has_side_effects=True),
        name="gather_weights",
    )(src)

def reduce_plan(zc, order):
    dims = order[::-1]
    at = {"z": 0, "y": 1, "x": 2}
    live = rels(zc)
    slots, phases = {}, []
    for j, dname in enumerate(dims):
        sends = [r for r in live if r[at[dname]]]
        live = [r for r in live if not r[at[dname]]]
        hops = range(1, zc) if dname == "z" else (1,)
        for r in live:
            for k in hops:
                slots[r, j, k] = len(slots)
        phases.append((dname, sends, live, list(hops)))
    return phases, slots

def reduce_kernel(zc, groups, gp, out, rbuf, send_sem, recv_sem):
    z, y, x, c = place()
    wcount = 2 * zc
    at = {"z": 0, "y": 1, "x": 2}
    def dev(rz, ry, rx, cc):
        return (lax.rem(z + rz, zc) * 2 + (y + ry) % 2, ((x + rx) % 2) * 2 + cc)
    def unit_of(rel):
        return ((x + rel[2]) % 2) * wcount + lax.rem(z + rel[0], zc) * 2 + (y + rel[1]) % 2
    peers = [(k, 0, 0) for k in range(1, zc)] + [(0, 1, 0), (0, 0, 1)]
    barrier = pltpu.get_barrier_semaphore()
    for p in peers:
        pl.semaphore_signal(barrier, inc=1, device_id=dev(*p, c), device_id_type=MESH)
    pl.semaphore_wait(barrier, len(peers))
    plans = [reduce_plan(zc, part[2]) for part in PARTS]
    lastslot = {}

    def partial(g, p, rel):
        r0, rows, _ = PARTS[p]
        if (g, p, rel) in lastslot:
            return rbuf.at[g, lastslot[g, p, rel], pl.ds(r0, rows)]
        return gp.at[g, unit_of(rel), pl.ds(r0, rows)]

    def send(g, p, j, rel):
        r0, rows, _ = PARTS[p]
        dname = plans[p][0][j][0]
        k = rel[at[dname]]
        hop = tuple(k if i == at[dname] else 0 for i in range(3))
        there = tuple(0 if i == at[dname] else rel[i] for i in range(3))
        slot = plans[p][1][there, j, k]
        pltpu.make_async_remote_copy(
            src_ref=partial(g, p, rel), dst_ref=rbuf.at[g, slot, pl.ds(r0, rows)],
            send_sem=send_sem.at[g, p], recv_sem=recv_sem.at[g, p, slot],
            device_id=dev(*hop, c), device_id_type=MESH).start()

    def receive(g, p, j, rel, final):
        r0, rows, _ = PARTS[p]
        hops = plans[p][0][j][3]
        slots = [plans[p][1][rel, j, k] for k in hops]
        for s in slots:
            ref = rbuf.at[g, s, pl.ds(r0, rows)]
            pltpu.make_async_copy(ref, ref, recv_sem.at[g, p, s]).wait()
        mine = partial(g, p, rel)
        def body(i, _):
            rr = pl.ds(pl.multiple_of(i * 16, 16), 16)
            total = mine[rr].astype(jnp.float32)
            for s in slots:
                total += rbuf[g, s, pl.ds(pl.multiple_of(r0 + i * 16, 16), 16)].astype(jnp.float32)
            if final:
                out[g, pl.ds(pl.multiple_of(r0 + i * 16, 16), 16)] = total
            else:
                rbuf[g, slots[0], pl.ds(pl.multiple_of(r0 + i * 16, 16), 16)] = total.astype(jnp.bfloat16)
            return 0
        lax.fori_loop(0, rows // 16, body, 0)
        lastslot[g, p, rel] = slots[0]

    zorder = list(range(1, zc)) + [0]
    items = [(g, k) for g in groups for k in zorder]

    def stage(j, g, k):
        for p in range(len(PARTS)):
            phases = plans[p][0]
            lowered = [r for r in phases[j - 1][2] if r[0] == k] if j else []
            sends = [r for r in phases[j][1] if r[0] == k] if j < 3 else []
            for rel in lowered:
                if rel in sends:
                    receive(g, p, j - 1, rel, False)
                    send(g, p, j, rel)
            for rel in lowered:
                if rel not in sends:
                    receive(g, p, j - 1, rel, j == 3)
            if j == 0:
                for rel in sends:
                    send(g, p, 0, rel)

    for t in range(len(items) + 3 * LAG):
        for j in range(4):
            i = t - j * LAG
            if 0 <= i < len(items):
                stage(j, *items[i])
    for g in groups:
        for p in range(len(PARTS)):
            r0, rows, _ = PARTS[p]
            ref = rbuf.at[g, :, pl.ds(r0, rows)]
            pltpu.make_async_copy(ref, ref, send_sem.at[g, p]).wait()

def reduce_units(gp, zc):
    ng = gp.shape[0]
    np_ = len(PARTS)
    return pl.pallas_call(
        functools.partial(reduce_kernel, zc, tuple(reversed(range(ng)))),
        out_shape=jax.ShapeDtypeStruct((ng, ROWS, D), jnp.float32),
        in_specs=[pl.BlockSpec(memory_space=pltpu.VMEM)],
        out_specs=pl.BlockSpec(memory_space=pltpu.VMEM),
        scratch_shapes=[
            pltpu.VMEM((ng, 4 * zc - 1, ROWS, D), jnp.bfloat16),
            pltpu.SemaphoreType.DMA((ng, np_)),
            pltpu.SemaphoreType.DMA((ng, np_, 4 * zc - 1)),
        ],
        compiler_params=pltpu.CompilerParams(collective_id=2, has_side_effects=True, vmem_limit_bytes=56 * 1024 * 1024),
        name="reduce_grads",
    )(gp)

AXES = ("wide", "narrow")


def running_rank(keep_flat):
    count = keep_flat.shape[0]
    lower = (lax.broadcasted_iota(jnp.int32, (count, count), 0) >= lax.broadcasted_iota(jnp.int32, (count, count), 1))
    total = jnp.dot(lower.astype(jnp.bfloat16), keep_flat.astype(jnp.bfloat16)[:, None], preferred_element_type=jnp.float32)
    return total[:, 0].astype(jnp.int32) - 1


def per_device(kept_tokens, keep_mask, conditioning, ada_weight, ada_bias, qkv_weight, out_weight, up_weight, down_weight, position_bias, mask_token, cotangent):
    wide_count = lax.axis_size("wide")
    narrow_count = lax.axis_size("narrow")
    devices = wide_count * narrow_count
    slots = kept_tokens.shape[2]
    images = conditioning.shape[0]
    count = images * PATCHES
    rows = qkv_weight.shape[0]
    fast = narrow_count == 4 and wide_count % 2 == 0 and rows * narrow_count == ROWS and images == 1
    me = lax.axis_index(AXES)
    core = lax.axis_index("narrow") % 2
    factor = 1.0 / math.sqrt(HEAD_DIM)
    low_type = jnp.bfloat16
    wide_type = jnp.float32
    silu_cond = jax.nn.silu(conditioning).astype(low_type)
    small = jnp.concatenate([silu_cond.reshape(-1), ada_bias.astype(low_type), mask_token.astype(low_type)])
    smalls = lax.all_gather(small, AXES, axis=0, tiled=False)
    silu_all = smalls[:, : images * D].reshape(devices * images, D)
    bias_full = smalls[:, images * D : images * D + ada_bias.shape[0]].reshape(-1)
    token_full = smalls[:, images * D + ada_bias.shape[0] :].reshape(-1)
    ada_low = ada_weight.astype(low_type)
    silu_part = lax.dynamic_slice_in_dim(silu_all, me * rows, rows, axis=1)
    mod_part = jnp.dot(silu_part, ada_low, preferred_element_type=wide_type)
    mod_parts = lax.all_to_all(mod_part.reshape(devices, images, 6 * D), AXES, split_axis=0, concat_axis=0, tiled=True)
    modulation = jnp.sum(mod_parts, axis=0) + bias_full.astype(wide_type)[None, :]
    if fast:
        attn_src = jnp.concatenate([qkv_weight.reshape(rows, 3, D), out_weight.reshape(rows, 1, D)], axis=1)
        both = jnp.stack([attn_src, up_weight.reshape(rows, 4, D)], axis=0).astype(low_type)
        turned = lax.all_to_all(both.transpose(2, 0, 1, 3), "narrow", split_axis=0, concat_axis=0, tiled=True)
        turned = turned.transpose(1, 0, 2, 3).reshape(2, ROWS, D)
        source = jnp.concatenate([turned, down_weight.astype(low_type)[None]], axis=0)
        full = gather(source, wide_count // 2)
        attn_full = full[0].reshape(4, D, D)
        up_blocks = full[1].reshape(4, D, D)
        down_full = full[2].reshape(FF, D)
        qkv_blocks = attn_full[:3]
        out_full = attn_full[3]
        def times_qkv(v):
            return jnp.einsum("tk,bkn->tbn", v, qkv_blocks, preferred_element_type=wide_type).reshape(count, 3 * D)
        def times_qkv_back(v):
            return jnp.einsum("tbn,bkn->tk", v.reshape(count, 3, D), qkv_blocks, preferred_element_type=wide_type)
        def times_up(v):
            return jnp.einsum("tk,bkn->tbn", v, up_blocks, preferred_element_type=wide_type).reshape(count, FF)
        def times_up_back(v):
            return jnp.einsum("tbn,bkn->tk", v.reshape(count, 4, D), up_blocks, preferred_element_type=wide_type)
    else:
        qkv_full = lax.all_gather(qkv_weight.astype(low_type), AXES, axis=0, tiled=True)
        out_full = lax.all_gather(out_weight.astype(low_type), AXES, axis=0, tiled=True)
        up_full = lax.all_gather(up_weight.astype(low_type), AXES, axis=0, tiled=True)
        down_full = lax.all_gather(down_weight.astype(low_type), AXES, axis=0, tiled=True)
        def times_qkv(v):
            return jnp.dot(v, qkv_full, preferred_element_type=wide_type)
        def times_qkv_back(v):
            return jnp.dot(v, qkv_full.T, preferred_element_type=wide_type)
        def times_up(v):
            return jnp.dot(v, up_full, preferred_element_type=wide_type)
        def times_up_back(v):
            return jnp.dot(v, up_full.T, preferred_element_type=wide_type)
    arrived = lax.all_to_all(kept_tokens, AXES, split_axis=1, concat_axis=0, tiled=True)
    received = arrived.reshape(devices * slots, D)
    keep_flat = keep_mask.reshape(count)
    keep_float = keep_flat.astype(wide_type)
    ranks = running_rank(keep_flat)
    target = ranks % devices * slots + ranks // devices
    columns = jnp.arange(devices * slots, dtype=jnp.int32)
    selector = jnp.where((keep_flat[:, None] == 1) & (target[:, None] == columns[None, :]), 1.0, 0.0).astype(wide_type)
    stream_in = jnp.dot(selector.astype(low_type), received, preferred_element_type=wide_type)
    stream_in = stream_in + (1.0 - keep_float)[:, None] * token_full.astype(wide_type)[None, :]
    stream_in = stream_in.reshape(images, PATCHES, D)
    shift_one, scale_one, gate_one, shift_two, scale_two, gate_two = jnp.split(
        modulation[:, None, :], 6, axis=-1
    )
    normed_one = modulate(stream_in, shift_one, scale_one).astype(low_type).reshape(count, D)
    projected = times_qkv(normed_one).astype(low_type)
    projected = projected.reshape(images, PATCHES, 3, HEADS, HEAD_DIM)
    queries = projected[:, :, 0]
    key_rows = projected[:, :, 1]
    value_rows = projected[:, :, 2]
    relative = expand_bias(position_bias, GRID)
    scores = (
        jnp.einsum("iqhd,ikhd->ihqk", queries, key_rows, preferred_element_type=wide_type) * factor
        + relative[None]
    )
    att_weights = jax.nn.softmax(scores, axis=-1)
    att_low = att_weights.astype(low_type)
    mixed = (
        jnp.einsum("ihqk,ikhd->iqhd", att_low, value_rows, preferred_element_type=wide_type)
        .astype(low_type)
        .reshape(count, D)
    )
    branch = jnp.dot(mixed, out_full, preferred_element_type=wide_type).reshape(images, PATCHES, D)
    stream_mid = stream_in + gate_one * branch
    normed_two = modulate(stream_mid, shift_two, scale_two).astype(low_type).reshape(count, D)
    hidden = times_up(normed_two)
    activated = gelu_tanh(hidden).astype(low_type)
    down = jnp.dot(activated, down_full, preferred_element_type=wide_type).reshape(
        images, PATCHES, D
    )
    block_out = (stream_mid + gate_two * down).reshape(count, D).astype(low_type)
    incoming = cotangent.astype(wide_type).reshape(images, PATCHES, D)
    grad_gate_two = jnp.sum(incoming * down, axis=1)
    grad_down = (gate_two * incoming).astype(low_type).reshape(count, D)
    grad_activated = jnp.dot(grad_down, down_full.T, preferred_element_type=wide_type)
    _, gelu_pull = jax.vjp(gelu_tanh, hidden)
    grad_hidden = gelu_pull(grad_activated)[0].astype(low_type)
    grad_normed_two = times_up_back(grad_hidden).reshape(
        images, PATCHES, D
    )
    _, norm_pull_two = jax.vjp(modulate, stream_mid, shift_two, scale_two)
    grad_mid_norm, grad_shift_two, grad_scale_two = norm_pull_two(grad_normed_two)
    grad_mid = incoming + grad_mid_norm
    grad_gate_one = jnp.sum(grad_mid * branch, axis=1)
    grad_branch = (gate_one * grad_mid).astype(low_type).reshape(count, D)
    grad_mixed = jnp.dot(grad_branch, out_full.T, preferred_element_type=wide_type).astype(low_type)
    grad_mixed = grad_mixed.reshape(images, PATCHES, HEADS, HEAD_DIM)
    grad_att = jnp.einsum(
        "iqhd,ikhd->ihqk", grad_mixed, value_rows, preferred_element_type=wide_type
    )
    grad_values = jnp.einsum(
        "ihqk,iqhd->ikhd", att_low, grad_mixed, preferred_element_type=wide_type
    )
    grad_scores = (
        att_weights * (grad_att - jnp.sum(att_weights * grad_att, axis=-1, keepdims=True))
    ).astype(low_type)
    grad_queries = (
        jnp.einsum("ihqk,ikhd->iqhd", grad_scores, key_rows, preferred_element_type=wide_type)
        * factor
    )
    grad_keys = (
        jnp.einsum("ihqk,iqhd->ikhd", grad_scores, queries, preferred_element_type=wide_type)
        * factor
    )
    grad_table = bias_adjoint(jnp.sum(grad_scores.astype(wide_type), axis=0), GRID)
    grad_projected = (
        jnp.stack([grad_queries, grad_keys, grad_values], axis=2)
        .astype(low_type)
        .reshape(count, 3 * D)
    )
    grad_normed_one = times_qkv_back(grad_projected).reshape(
        images, PATCHES, D
    )
    _, norm_pull_one = jax.vjp(modulate, stream_in, shift_one, scale_one)
    grad_in_norm, grad_shift_one, grad_scale_one = norm_pull_one(grad_normed_one)
    grad_in = (grad_mid + grad_in_norm).reshape(count, D)
    grad_modulation = jnp.concatenate(
        [
            grad_shift_one[:, 0],
            grad_scale_one[:, 0],
            grad_gate_one,
            grad_shift_two[:, 0],
            grad_scale_two[:, 0],
            grad_gate_two,
        ],
        axis=-1,
    ).astype(low_type)
    grad_mod_all = lax.all_gather(grad_modulation, AXES, axis=0, tiled=True)
    grad_ada = lax.dot_general(silu_part, grad_mod_all, (((0,), (0,)), ((), ())), preferred_element_type=wide_type)
    bias_share = 6 * D // devices
    sum_bias = jnp.sum(lax.dynamic_slice_in_dim(grad_mod_all, me * bias_share, bias_share, axis=1).astype(wide_type), axis=0)
    silu_parts = lax.dot_general(grad_mod_all, ada_low, (((1,), (1,)), ((), ())), preferred_element_type=wide_type)
    silu_parts = lax.all_to_all(silu_parts.reshape(devices, images, rows), AXES, split_axis=0, concat_axis=0, tiled=True)
    grad_silu = silu_parts.transpose(1, 0, 2).reshape(images, D)
    _, silu_pull = jax.vjp(jax.nn.silu, conditioning)
    grad_cond = silu_pull(grad_silu)[0]
    grad_mask = jnp.sum((1.0 - keep_float)[:, None] * grad_in, axis=0)
    grad_received = jnp.dot(
        selector.T, grad_in, precision=lax.Precision.HIGHEST, preferred_element_type=wide_type
    ).astype(low_type)
    grad_kept = lax.all_to_all(
        grad_received.reshape(devices, 1, slots, D),
        ("wide", "narrow"),
        split_axis=0,
        concat_axis=1,
        tiled=True,
    )
    if fast:
        def own_blocks(which):
            gp = grad_projected.reshape(count, 3, D)
            pick = lambda one, other: jnp.where(which == 0, one, other)
            attn = (normed_one, pick(gp[:, 0], gp[:, 1]), pick(normed_one, mixed), pick(gp[:, 2], grad_branch))
            gh = grad_hidden.reshape(count, 4, D)
            up = (pick(gh[:, 0], gh[:, 1]), pick(gh[:, 2], gh[:, 3]))
            acts = activated.reshape(count, wide_count, 2, 2, ROWS)
            acts = pick(acts[:, :, :, 0], acts[:, :, :, 1]).transpose(0, 2, 1, 3).reshape(count, 2, D)
            return jnp.stack(attn + (normed_two,) + up + (grad_down, acts[:, 0], acts[:, 1]), axis=0)
        swap = [(n, n ^ 1) for n in range(4)]
        theirs = lax.ppermute(own_blocks(1 - core), "narrow", swap)
        factors = jnp.concatenate([own_blocks(core), theirs], axis=1)
        def grad_of(left, right):
            return lax.dot_general(factors[left], factors[right], (((0,), (0,)), ((), ())), preferred_element_type=wide_type).astype(low_type)
        partial = jnp.stack([grad_of(0, 1), grad_of(2, 3), grad_of(4, 5), grad_of(4, 6), grad_of(8, 7), grad_of(9, 7)])
        owned = reduce_units(partial.reshape(3, 2 * wide_count, ROWS, D), wide_count // 2)
        sum_down = owned[2]
        turned = owned[:2].reshape(2, 4, rows, D).transpose(1, 0, 2, 3)
        turned = lax.all_to_all(turned, "narrow", split_axis=0, concat_axis=0, tiled=True)
        sum_qkv = turned[:3, 0].transpose(1, 0, 2).reshape(rows, 3 * D)
        sum_out = turned[3, 0]
        sum_up = turned[:, 1].transpose(1, 0, 2).reshape(rows, FF)
    else:
        def scatter(left, right):
            partial = lax.dot_general(left, right, (((0,), (0,)), ((), ())), preferred_element_type=wide_type)
            return lax.psum_scatter(partial.reshape(-1), AXES, scatter_dimension=0, tiled=True).reshape(-1, right.shape[1])
        sum_qkv = scatter(normed_one, grad_projected)
        sum_out = scatter(mixed, grad_branch)
        sum_up = scatter(normed_two, grad_hidden)
        sum_down = scatter(activated, grad_down)
    grad_table_all, mask_whole = lax.psum((grad_table, grad_mask), AXES)
    mask_share = D // devices
    sum_mask = lax.dynamic_slice_in_dim(mask_whole, me * mask_share, mask_share)
    return (block_out, grad_kept, grad_cond, grad_ada, sum_bias, sum_qkv, sum_out, sum_up, sum_down, grad_table_all, sum_mask)


def solution(mesh):
    in_specs = (
        P(("wide", "narrow"), None, None, None),
        P(("wide", "narrow"), None),
        P(("wide", "narrow"), None),
        P(("wide", "narrow"), None),
        P(("wide", "narrow")),
        P(("wide", "narrow"), None),
        P(("wide", "narrow"), None),
        P(("wide", "narrow"), None),
        P(("wide", "narrow"), None),
        P(),
        P(("wide", "narrow")),
        P(("wide", "narrow"), None),
    )
    out_specs = (
        P(("wide", "narrow"), None),
        P(("wide", "narrow"), None, None, None),
        P(("wide", "narrow"), None),
        P(("wide", "narrow"), None),
        P(("wide", "narrow")),
        P(("wide", "narrow"), None),
        P(("wide", "narrow"), None),
        P(("wide", "narrow"), None),
        P(("wide", "narrow"), None),
        P(),
        P(("wide", "narrow")),
    )
    return jax.shard_map(
        per_device, mesh=mesh, in_specs=in_specs, out_specs=out_specs, check_vma=False
    )
```

```python
import functools
import math

import jax
import jax.numpy as jnp
from jax import lax
from jax.experimental import pallas as pl
from jax.experimental.pallas import tpu as pltpu
from jax.sharding import PartitionSpec as P

D = 1152
HEADS = 16
HEAD_DIM = 72
FF = 4608
GRID = 16
PATCHES = 256


EPSILON = 1e-06


def layer_norm(stream):
    center = stream - jnp.mean(stream, axis=-1, keepdims=True)
    variance = jnp.mean(center * center, axis=-1, keepdims=True)
    return center * lax.rsqrt(variance + EPSILON)


def modulate(stream, shift, scale):
    return layer_norm(stream) * (1.0 + scale) + shift


def offset_picker(grid):
    places = jnp.arange(grid, dtype=jnp.int32)
    spread = jnp.arange(2 * grid - 1, dtype=jnp.int32)
    return (
        places[:, None, None] - places[None, :, None] + grid - 1 == spread[None, None, :]
    ).astype(jnp.float32)


def expand_bias(table, grid):
    picker = offset_picker(grid)
    partial_rows = jnp.einsum("yka,had->hykd", picker, table, precision=lax.Precision.HIGHEST)
    expanded = jnp.einsum("hykd,xjd->hyxkj", partial_rows, picker, precision=lax.Precision.HIGHEST)
    return expanded.reshape(table.shape[0], grid * grid, grid * grid)


def bias_adjoint(grad_bias, grid):
    picker = offset_picker(grid)
    shaped = grad_bias.reshape(grad_bias.shape[0], grid, grid, grid, grid)
    partial_rows = jnp.einsum("hyxkj,xjd->hykd", shaped, picker, precision=lax.Precision.HIGHEST)
    return jnp.einsum("hykd,yka->had", partial_rows, picker, precision=lax.Precision.HIGHEST)


def gelu_tanh(value):
    return jax.nn.gelu(value, approximate=True)


MESH = pl.DeviceIdType.MESH
ROWS = 144
PARTS = ((0, 80, "zxy"), (80, 64, "zyx"))
AT = {"z": 0, "y": 1, "x": 2}
F32 = jnp.float32
BF16 = jnp.bfloat16
FACTOR = 1.0 / math.sqrt(HEAD_DIM)
NT = (((1,), (1,)), ((), ()))
TN = (((0,), (0,)), ((), ()))
SPAN = 2 * PATCHES


def rels(zc):
    return [(rz, ry, rx) for rz in range(zc) for ry in range(2) for rx in range(2)]


class Place:
    def __init__(self, zc):
        wide = lax.axis_index("wide")
        narrow = lax.axis_index("narrow")
        self.zc, self.wcount = zc, 2 * zc
        self.z, self.y, self.x, self.c = wide // 2, wide % 2, narrow // 2, narrow % 2
        self.hops = {"z": [(k, 0, 0) for k in range(1, zc)], "y": [(0, 1, 0)], "x": [(0, 0, 1)]}

    def shifted(self, rz, ry, rx):
        w = lax.rem(self.z + rz, self.zc) * 2 + (self.y + ry) % 2
        return w, (self.x + rx) % 2

    def device(self, rz, ry, rx, flip=0):
        w, x = self.shifted(rz, ry, rx)
        return w, x * 2 + (self.c + flip) % 2

    def greet(self):
        barrier = pltpu.get_barrier_semaphore()
        friends = [self.device(*h) for d in "zyx" for h in self.hops[d]] + [self.device(0, 0, 0, 1)]
        for f in friends:
            pl.semaphore_signal(barrier, inc=1, device_id=f, device_id_type=MESH)
        pl.semaphore_wait(barrier, len(friends))


def wait_rows(ref, total, sem):
    for blocks in range(1, ref.shape[0] + 1):
        if total % (blocks * 16) == 0 and total // blocks <= ref.shape[1]:
            some = ref.at[pl.ds(0, blocks), pl.ds(0, total // blocks)]
            pltpu.make_async_copy(some, some, sem).wait()
            return
    raise ValueError("rows")


def each_rows(total, step, body):
    def go(i, carry):
        body(pl.ds(pl.multiple_of(i * step, step), step))
        return carry
    lax.fori_loop(0, total // step, go, 0)


def each_columns(body):
    def go(i, carry):
        body(pl.ds(pl.multiple_of(i * 256, 256), 256))
        return carry
    lax.fori_loop(0, 4, go, 0)
    body(pl.ds(1024, 128))


def window(head):
    low = head * HEAD_DIM
    first, last = low // 128 * 128, -(-(low + HEAD_DIM) // 128) * 128
    lane = lax.broadcasted_iota(jnp.int32, (1, last - first), 1) + first
    mask = jnp.where((lane >= low) & (lane < low + HEAD_DIM), 1.0, 0.0).astype(F32)
    return slice(first, last), mask


class Gather:
    def __init__(self, me, src, out, sems):
        self.me, self.src, self.out = me, src, out
        self.send, self.recv, self.sib_send, self.sib_recv, self.own = sems
        self.all = rels(me.zc)
        self.index = {r: i for i, r in enumerate(self.all)}

    def block(self, g, rel, r0, rows):
        w, x = self.me.shifted(self.me.zc - rel[0], rel[1], rel[2])
        n = x * 2 + self.me.c
        b, row = (n, w * ROWS) if g < 2 else ((w * 4 + n) // self.me.wcount, lax.rem(w * 4 + n, self.me.wcount) * ROWS)
        return self.out.at[g, b, pl.ds(pl.multiple_of(row + r0, 16), rows)]

    def forward(self, g, p, rel):
        r0, rows, order = PARTS[p]
        at = max([i for i, d in enumerate(order) if rel[AT[d]]], default=-1)
        there = self.block(g, rel, r0, rows)
        here = there if any(rel) else self.src.at[g, pl.ds(r0, rows)]
        for d in order[at + 1:]:
            for h in self.me.hops[d]:
                seen = ((rel[0] + h[0]) % self.me.zc, (rel[1] + h[1]) % 2, (rel[2] + h[2]) % 2)
                pltpu.make_async_remote_copy(
                    src_ref=here, dst_ref=there, send_sem=self.send.at[g, p], recv_sem=self.recv.at[g, p, self.index[seen]],
                    device_id=self.me.device(*h), device_id_type=MESH).start()
        pltpu.make_async_remote_copy(
            src_ref=here, dst_ref=there, send_sem=self.sib_send.at[g, p], recv_sem=self.sib_recv.at[g, p],
            device_id=self.me.device(0, 0, 0, 1), device_id_type=MESH).start()

    def begin(self, g):
        for p in range(len(PARTS)):
            self.forward(g, p, (0, 0, 0))
        pltpu.make_async_copy(self.src.at[g], self.block(g, (0, 0, 0), 0, ROWS), self.own.at[g]).start()

    def ticks(self, g):
        todo = []
        for deep in (1, 2, 3):
            for rel in self.all:
                if sum(1 for v in rel if v) == deep:
                    todo.append(functools.partial(self.tick, g, rel))
        return todo

    def tick(self, g, rel):
        for p, (r0, rows, _) in enumerate(PARTS):
            wait_rows(self.out.at[g], rows, self.recv.at[g, p, self.index[rel]])
            self.forward(g, p, rel)

    def arrived(self, g):
        pltpu.make_async_copy(self.src.at[g], self.src.at[g], self.own.at[g]).wait()
        for p, (r0, rows, _) in enumerate(PARTS):
            wait_rows(self.out.at[g], 4 * self.me.zc * rows, self.sib_recv.at[g, p])

    def finish(self, g):
        for p, (r0, rows, _) in enumerate(PARTS):
            wait_rows(self.out.at[g], (4 * self.me.zc - 1) * rows, self.send.at[g, p])
            wait_rows(self.out.at[g], 4 * self.me.zc * rows, self.sib_send.at[g, p])


class Blocks:
    def __init__(self, full, buf, sems, order):
        self.full, self.buf, self.sems, self.order = full, buf, sems, order

    def fetch(self, i):
        if i < len(self.order):
            g, b = self.order[i]
            pltpu.make_async_copy(self.full.at[g, b], self.buf.at[i % 2], self.sems.at[i % 2]).start()

    def take(self, i):
        g, b = self.order[i]
        pltpu.make_async_copy(self.full.at[g, b], self.buf.at[i % 2], self.sems.at[i % 2]).wait()
        return self.buf.at[i % 2]


def standard(v):
    center = v - jnp.mean(v, axis=-1, keepdims=True)
    spread = lax.rsqrt(jnp.mean(center * center, axis=-1, keepdims=True) + EPSILON)
    return center * spread, spread


def gelu(v):
    return 0.5 * v * (1.0 + jnp.tanh(0.7978845608 * (v + 0.044715 * v * v * v)))


def gelu_slope(v):
    t = jnp.tanh(0.7978845608 * (v + 0.044715 * v * v * v))
    return 0.5 * (1.0 + t) + 0.5 * v * (1.0 - t * t) * 0.7978845608 * (1.0 + 3.0 * 0.044715 * v * v)


def turn(ref, out):
    def body(cols):
        out[cols, :] = ref[:, cols].astype(F32).T.astype(BF16)
    each_columns(body)


def forward_kernel(zc, src, stream_in, mod, spread_bias, cotangent, full, block_out, one_t, projected, att, mixed_t, branch,
                   stream_mid, two_t, hidden, act_t, gate_sum, wbuf, normed, wide_one, act, turned,
                   send, recv, sib_send, sib_recv, own, wsem):
    me = Place(zc)
    me.greet()
    net = Gather(me, src, full, (send, recv, sib_send, sib_recv, own))
    blocks = Blocks(full, wbuf, wsem, [(0, 0), (0, 1), (0, 2), (0, 3), (1, 0), (1, 1), (1, 2), (1, 3), (2, 0), (2, 1), (2, 2), (2, 3)])
    net.begin(0)

    def norm_one(rows):
        n, _ = standard(stream_in[rows, :])
        normed[rows, :] = (n * (1.0 + mod[1:2, :]) + mod[0:1, :]).astype(BF16)
    each_rows(PATCHES, 32, norm_one)
    turn(normed, one_t)
    ticks = net.ticks(0)
    for i, tick in enumerate(ticks):
        tick()
        if i == 11:
            net.begin(1)
    net.arrived(0)
    ticks = net.ticks(1)
    blocks.fetch(0)
    blocks.fetch(1)
    for b in range(3):
        w = blocks.take(b)
        def product(cols):
            projected[b, :, cols] = jnp.dot(normed[...], w[:, cols], preferred_element_type=F32).astype(BF16)
        each_columns(product)
        blocks.fetch(b + 2) if b + 2 < 4 else None
        ticks.pop(0)()
    wide_one[...] = jnp.zeros_like(wide_one)
    for head in range(HEADS):
        lanes, mask = window(head)
        q = projected[0, :, lanes] * mask.astype(BF16)
        scores = lax.dot_general(q, projected[1, :, lanes], NT, preferred_element_type=F32) * FACTOR
        u = spread_bias[head]
        bias = jnp.concatenate(
            [pltpu.roll(u, (SPAN - (GRID - 1 - r) * GRID) % SPAN, 1)[:, :PATCHES] for r in range(GRID)], axis=0)
        scores = scores + bias
        e = jnp.exp(scores - jnp.max(scores, axis=-1, keepdims=True))
        weights = e * (1.0 / jnp.sum(e, axis=-1, keepdims=True))
        att[head] = weights
        got = jnp.dot(weights.astype(BF16), projected[2, :, lanes], preferred_element_type=F32)
        wide_one[:, lanes] += got * mask
        if head % 2 and ticks:
            ticks.pop(0)()
        if head == 11:
            net.begin(2)
    normed[...] = wide_one[...].astype(BF16)
    turn(normed, mixed_t)
    w = blocks.take(3)
    def product(cols):
        branch[:, cols] = jnp.dot(normed[...], w[:, cols], preferred_element_type=F32)
    each_columns(product)
    def mid(rows):
        v = stream_in[rows, :] + mod[2:3, :] * branch[rows, :]
        stream_mid[rows, :] = v
        n, _ = standard(v)
        normed[rows, :] = (n * (1.0 + mod[4:5, :]) + mod[3:4, :]).astype(BF16)
    each_rows(PATCHES, 32, mid)
    turn(normed, two_t)
    for tick in ticks:
        tick()
    net.arrived(1)
    ticks = net.ticks(2)
    blocks.fetch(4)
    blocks.fetch(5)
    def turn_units(ref, b):
        turn(ref, turned)
        for i in range(8):
            unit = b * 8 + i
            w, n = unit // 4, unit % 4
            act_t[n % 2, n // 2, w * ROWS:(w + 1) * ROWS, :] = turned[i * ROWS:(i + 1) * ROWS, :]
    for b in range(4):
        w = blocks.take(4 + b)
        def product(cols):
            v = jnp.dot(normed[...], w[:, cols], preferred_element_type=F32)
            hidden[b, :, cols] = v
        each_columns(product)
        if b < 2:
            blocks.fetch(6 + b)
        def bend(rows):
            act[b, rows, :] = gelu(hidden[b, rows, :]).astype(BF16)
        each_rows(PATCHES, 32, bend)
        turn_units(act.at[b], b)
        for _ in range(2):
            ticks.pop(0)()
    for tick in ticks:
        tick()
    net.arrived(2)
    blocks.fetch(8)
    blocks.fetch(9)
    for b in range(4):
        w = blocks.take(8 + b)
        def product(cols):
            v = jnp.dot(act[b], w[:, cols], preferred_element_type=F32)
            wide_one[:, cols] = v if b == 0 else wide_one[:, cols] + v
        each_columns(product)
        if b < 2:
            blocks.fetch(10 + b)
    gate_sum[...] = jnp.zeros_like(gate_sum)
    def last(rows):
        v = wide_one[rows, :]
        block_out[rows, :] = (stream_mid[rows, :] + mod[5:6, :] * v).astype(BF16)
        gate_sum[...] += jnp.sum(cotangent[rows, :].astype(F32) * v, axis=0, keepdims=True)
    each_rows(PATCHES, 32, last)
    for g in range(3):
        net.finish(g)


def run_forward(src, stream_in, mod, spread_bias, cotangent, zc):
    vmem = pl.BlockSpec(memory_space=pltpu.VMEM)
    hbm = pl.BlockSpec(memory_space=pl.ANY)
    parts = len(PARTS)
    shape = jax.ShapeDtypeStruct
    return pl.pallas_call(
        functools.partial(forward_kernel, zc),
        out_shape=(
            shape((3, 4, D, D), BF16), shape((PATCHES, D), BF16), shape((D, PATCHES), BF16), shape((3, PATCHES, D), BF16),
            shape((HEADS, PATCHES, PATCHES), F32), shape((D, PATCHES), BF16), shape((PATCHES, D), F32), shape((PATCHES, D), F32),
            shape((D, PATCHES), BF16), shape((4, PATCHES, D), F32), shape((2, 2, D, PATCHES), BF16), shape((1, D), F32)),
        in_specs=[hbm, vmem, vmem, vmem, vmem],
        out_specs=(hbm,) + (vmem,) * 11,
        scratch_shapes=[
            pltpu.VMEM((2, D, D), BF16), pltpu.VMEM((PATCHES, D), BF16), pltpu.VMEM((PATCHES, D), F32), pltpu.VMEM((4, PATCHES, D), BF16), pltpu.VMEM((D, PATCHES), BF16),
            pltpu.SemaphoreType.DMA((3, parts)), pltpu.SemaphoreType.DMA((3, parts, 4 * zc)), pltpu.SemaphoreType.DMA((3, parts)),
            pltpu.SemaphoreType.DMA((3, parts)), pltpu.SemaphoreType.DMA((3,)), pltpu.SemaphoreType.DMA((2,))],
        compiler_params=pltpu.CompilerParams(collective_id=1, has_side_effects=True, vmem_limit_bytes=58 * 1024 * 1024),
        name="forward",
    )(src, stream_in, mod, spread_bias, cotangent)


def reduce_plan(zc, order):
    live, slots, phases = rels(zc), {}, []
    for j, d in enumerate(order[::-1]):
        sends = [r for r in live if r[AT[d]]]
        live = [r for r in live if not r[AT[d]]]
        hops = list(range(1, zc)) if d == "z" else [1]
        for r in live:
            for k in hops:
                slots[r, j, k] = len(slots)
        phases.append((d, sends, live, hops))
    return phases, slots


class Reduce:
    def __init__(self, me, sums, landed, owned, send, recv):
        self.me, self.sums, self.landed, self.owned, self.send_sem, self.recv = me, sums, landed, owned, send, recv
        self.plans = [reduce_plan(me.zc, part[2]) for part in PARTS]
        self.held = {}
        self.items = [(g, k) for g in (2, 1, 0) for k in list(range(1, me.zc)) + [0]]

    def partial(self, g, p, rel):
        r0, rows, _ = PARTS[p]
        if (g, p, rel) in self.held:
            return self.landed.at[g, self.held[g, p, rel], pl.ds(r0, rows)]
        w, x = self.me.shifted(*rel)
        return self.sums[g].at[x, pl.ds(pl.multiple_of(w * ROWS + r0, 16), rows)]

    def send(self, g, p, j, rel):
        r0, rows, _ = PARTS[p]
        d = self.plans[p][0][j][0]
        k = rel[AT[d]]
        hop = tuple(k if i == AT[d] else 0 for i in range(3))
        there = tuple(0 if i == AT[d] else rel[i] for i in range(3))
        slot = self.plans[p][1][there, j, k]
        pltpu.make_async_remote_copy(
            src_ref=self.partial(g, p, rel), dst_ref=self.landed.at[g, slot, pl.ds(r0, rows)],
            send_sem=self.send_sem.at[g, p, min(j, 1)], recv_sem=self.recv.at[g, p, slot],
            device_id=self.me.device(*hop), device_id_type=MESH).start()

    def receive(self, g, p, j, rel, final):
        r0, rows, _ = PARTS[p]
        slots = [self.plans[p][1][rel, j, k] for k in self.plans[p][0][j][3]]
        for s in slots:
            ref = self.landed.at[g, s, pl.ds(r0, rows)]
            pltpu.make_async_copy(ref, ref, self.recv.at[g, p, s]).wait()
        mine = self.partial(g, p, rel)
        def body(i, carry):
            at = pl.ds(pl.multiple_of(r0 + i * 16, 16), 16)
            total = mine[pl.ds(pl.multiple_of(i * 16, 16), 16), :].astype(F32)
            for s in slots:
                total += self.landed[g, s, at, :].astype(F32)
            if final:
                self.owned[g, at, :] = total
            else:
                self.landed[g, slots[0], at, :] = total.astype(BF16)
            return carry
        lax.fori_loop(0, rows // 16, body, 0)
        self.held[g, p, rel] = slots[0]

    def stage(self, j, g, k):
        for p in range(len(PARTS)):
            phases = self.plans[p][0]
            lowered = [r for r in phases[j - 1][2] if r[0] == k] if j else []
            sends = [r for r in phases[j][1] if r[0] == k] if j < 3 else []
            for rel in sorted(lowered, key=lambda r: r not in sends):
                self.receive(g, p, j - 1, rel, j == 3)
                if rel in sends:
                    self.send(g, p, j, rel)
            if j == 0:
                for rel in sends:
                    self.send(g, p, 0, rel)

    def step(self, t):
        for j in range(4):
            if 0 <= t - j < len(self.items):
                self.stage(j, *self.items[t - j])

    def steps(self):
        return len(self.items) + 3

    def sent(self, g, late):
        for p, (r0, rows, _) in enumerate(PARTS):
            phases = self.plans[p][0]
            count = sum(len(phases[j][1]) for j in ((1, 2) if late else (0,)))
            ref = self.landed.at[g, pl.ds(0, count), pl.ds(r0, rows)]
            pltpu.make_async_copy(ref, ref, self.send_sem.at[g, p, int(late)]).wait()


def backward_kernel(zc, full, mod, cotangent, stream_in, stream_mid, branch, projected, att, hidden, one_t, mixed_t, two_t, act_t,
                    owned, spread_grad, grad_in, small,
                    sum_a, sum_b, landed, wbuf, left, left_sib, acts, acts_sib, grad_down, right_sib, bent, rights, grad_mixed,
                    stream, hid, att_buf, grad_mid,
                    send, recv, sib_send, sib_recv, wsem, lsem, hsem, asem, ssem):
    me = Place(zc)
    me.greet()
    c = me.c
    net = Reduce(me, {2: sum_a, 1: sum_b, 0: sum_a}, landed, owned, send, recv)
    blocks = Blocks(full, wbuf, wsem, [(2, 0), (2, 1), (2, 2), (2, 3), (1, 0), (1, 1), (1, 2), (1, 3), (0, 3), (0, 0), (0, 1), (0, 2)])
    swaps = []

    def swap(src, dst):
        i = len(swaps)
        swaps.append(pltpu.make_async_remote_copy(
            src_ref=src, dst_ref=dst, send_sem=sib_send.at[i], recv_sem=sib_recv.at[i],
            device_id=me.device(0, 0, 0, 1), device_id_type=MESH))
        swaps[-1].start()
        return swaps[-1]

    def load(src, dst, sem):
        copy = pltpu.make_async_copy(src, dst, sem)
        copy.start()
        return copy

    act_swap = swap(act_t.at[1 - c], acts_sib)
    act_load = load(act_t.at[c], acts, lsem.at[0])
    blocks.fetch(0)
    blocks.fetch(1)
    hid_load = load(hidden.at[0], hid, hsem.at[0])

    def down(rows):
        grad_down[rows, :] = (mod[5:6, :] * cotangent[rows, :].astype(F32)).astype(BF16)
    each_rows(PATCHES, 32, down)
    down_swap = swap(grad_down, right_sib.at[0])
    left_loads = [load(ref, left.at[i], lsem.at[1 + i]) for i, ref in enumerate((one_t, mixed_t, two_t))]
    left_swaps = [swap(ref, left_sib.at[i]) for i, ref in enumerate((one_t, mixed_t, two_t))]
    mid_load = load(stream_mid, stream.at[0], ssem.at[0])
    branch_load = load(branch, stream.at[1], ssem.at[1])

    def weight_grad(total, mine, mine_right, theirs, their_right):
        def body(cols):
            v = jnp.dot(mine[...], mine_right[:, cols], preferred_element_type=F32)
            total[:, cols] = (v + jnp.dot(theirs[...], their_right[:, cols], preferred_element_type=F32)).astype(BF16)
        each_columns(body)

    act_load.wait()
    act_swap.wait_recv()
    down_swap.wait_recv()
    for j in range(2):
        weight_grad(sum_a.at[j], acts.at[j], grad_down, acts_sib.at[j], right_sib.at[0])
    net.step(0)
    for b in range(4):
        w = blocks.take(b)
        hid_load.wait()
        def bend(cols):
            v = lax.dot_general(grad_down[...], w[cols, :], NT, preferred_element_type=F32)
            bent[b, :, cols] = (v * gelu_slope(hid[:, cols])).astype(BF16)
        each_columns(bend)
        blocks.fetch(b + 2)
        if b < 3:
            hid_load = load(hidden.at[b + 1], hid, hsem.at[0])
        if b in (1, 3):
            net.step((b + 1) // 2)
    bent_swaps = [swap(bent.at[1 - c], right_sib.at[1]), swap(bent.at[3 - c], right_sib.at[2])]
    for copy in left_loads:
        copy.wait()
    for copy in left_swaps + bent_swaps:
        copy.wait_recv()
    for j in range(2):
        weight_grad(sum_b.at[j], left.at[2], bent.at[2 * j + c], left_sib.at[2], right_sib.at[1 + j])
    net.step(3)
    for b in range(4):
        w = blocks.take(4 + b)
        def back(cols):
            v = lax.dot_general(bent[b], w[cols, :], NT, preferred_element_type=F32)
            grad_in[:, cols] = v if b == 0 else grad_in[:, cols] + v
        each_columns(back)
        blocks.fetch(6 + b)
    mid_load.wait()
    branch_load.wait()
    small[...] = jnp.zeros_like(small)

    def norm_back(rows, stream_rows, scale, shift_at, scale_at):
        n, spread = standard(stream_rows)
        e = grad_in[rows, :]
        f = e * (1.0 + scale)
        small[shift_at:shift_at + 1, :] += jnp.sum(e, axis=0, keepdims=True)
        small[scale_at:scale_at + 1, :] += jnp.sum(e * n, axis=0, keepdims=True)
        return (f - jnp.mean(f, axis=-1, keepdims=True) - n * jnp.mean(f * n, axis=-1, keepdims=True)) * spread

    def back_two(rows):
        v = cotangent[rows, :].astype(F32) + norm_back(rows, stream[0, rows, :], mod[4:5, :], 3, 4)
        grad_mid[rows, :] = v
        small[2:3, :] += jnp.sum(v * stream[1, rows, :], axis=0, keepdims=True)
        rights[3, rows, :] = (mod[2:3, :] * v).astype(BF16)
    each_rows(PATCHES, 32, back_two)
    in_load = load(stream_in, stream.at[0], ssem.at[0])
    net.step(4)
    att_load = load(att.at[0], att_buf.at[0], asem.at[0])
    w = blocks.take(8)
    def mixed_back(cols):
        grad_mixed[:, cols] = lax.dot_general(rights[3], w[cols, :], NT, preferred_element_type=F32).astype(BF16)
    each_columns(mixed_back)
    blocks.fetch(10)
    for b in range(3):
        rights[b] = jnp.zeros((PATCHES, D), BF16)
    net.step(5)
    for head in range(HEADS):
        att_load.wait()
        if head + 1 < HEADS:
            att_load = load(att.at[head + 1], att_buf.at[(head + 1) % 2], asem.at[(head + 1) % 2])
        lanes, mask = window(head)
        weights = att_buf[head % 2]
        low = weights.astype(BF16)
        given = grad_mixed[:, lanes]
        grad_att = lax.dot_general(given * mask.astype(BF16), projected[2, :, lanes], NT, preferred_element_type=F32)
        v = lax.dot_general(low, given, TN, preferred_element_type=F32)
        rights[2, :, lanes] += (v * mask).astype(BF16)
        scores = weights * (grad_att - jnp.sum(weights * grad_att, axis=-1, keepdims=True))
        scores_low = scores.astype(BF16)
        v = jnp.dot(scores_low, projected[1, :, lanes], preferred_element_type=F32) * FACTOR
        rights[0, :, lanes] += (v * mask).astype(BF16)
        v = lax.dot_general(scores_low, projected[0, :, lanes], TN, preferred_element_type=F32) * FACTOR
        rights[1, :, lanes] += (v * mask).astype(BF16)
        rounded = scores_low.astype(F32)
        total = jnp.zeros((GRID, SPAN), F32)
        for r in range(GRID):
            rows = jnp.concatenate([rounded[r * GRID:(r + 1) * GRID], jnp.zeros((GRID, SPAN - PATCHES), F32)], axis=1)
            total += pltpu.roll(rows, (GRID - 1 - r) * GRID, 1)
        spread_grad[head] = total
        if head in (7, 15):
            net.step(6 + head // 8)
    end_swaps = [swap(rights.at[1 - c], right_sib.at[3]), swap(rights.at[3 - c], right_sib.at[4])]
    net.sent(2, False)
    for copy in end_swaps:
        copy.wait_recv()
    weight_grad(sum_a.at[0], left.at[0], rights.at[c], left_sib.at[0], right_sib.at[3])
    weight_grad(sum_a.at[1], left.at[c], rights.at[2 + c], left_sib.at[c], right_sib.at[4])
    net.step(8)
    net.step(9)
    for b in range(3):
        w = blocks.take(9 + b)
        def back(cols):
            v = lax.dot_general(rights[b], w[cols, :], NT, preferred_element_type=F32)
            grad_in[:, cols] = v if b == 0 else grad_in[:, cols] + v
        each_columns(back)
        blocks.fetch(11 + b)
    in_load.wait()
    def back_one(rows):
        v = norm_back(rows, stream[0, rows, :], mod[1:2, :], 0, 1)
        grad_in[rows, :] = grad_mid[rows, :] + v
    each_rows(PATCHES, 32, back_one)
    for t in range(10, net.steps()):
        net.step(t)
    net.sent(1, False)
    net.sent(0, False)
    for g in range(3):
        net.sent(g, True)
    for copy in swaps:
        copy.wait_send()


def run_backward(full, mod, cotangent, stream_in, stream_mid, branch, projected, att, hidden, one_t, mixed_t, two_t, act_t, zc):
    vmem = pl.BlockSpec(memory_space=pltpu.VMEM)
    hbm = pl.BlockSpec(memory_space=pl.ANY)
    parts = len(PARTS)
    shape = jax.ShapeDtypeStruct
    dma = pltpu.SemaphoreType.DMA
    return pl.pallas_call(
        functools.partial(backward_kernel, zc),
        out_shape=(shape((3, ROWS, D), F32), shape((HEADS, GRID, SPAN), F32), shape((PATCHES, D), F32), shape((8, D), F32)),
        in_specs=[hbm, vmem, vmem, hbm, hbm, hbm, vmem, hbm, hbm, hbm, hbm, hbm, hbm],
        out_specs=(vmem,) * 4,
        scratch_shapes=[
            pltpu.VMEM((2, D, D), BF16), pltpu.VMEM((2, D, D), BF16), pltpu.VMEM((3, 4 * zc - 1, ROWS, D), BF16),
            pltpu.VMEM((2, D, D), BF16), pltpu.VMEM((3, D, PATCHES), BF16), pltpu.VMEM((3, D, PATCHES), BF16),
            pltpu.VMEM((2, D, PATCHES), BF16), pltpu.VMEM((2, D, PATCHES), BF16), pltpu.VMEM((PATCHES, D), BF16),
            pltpu.VMEM((5, PATCHES, D), BF16), pltpu.VMEM((4, PATCHES, D), BF16), pltpu.VMEM((4, PATCHES, D), BF16),
            pltpu.VMEM((PATCHES, D), BF16), pltpu.VMEM((2, PATCHES, D), F32), pltpu.VMEM((PATCHES, D), F32),
            pltpu.VMEM((2, PATCHES, PATCHES), F32), pltpu.VMEM((PATCHES, D), F32),
            dma((3, parts, 2)), dma((3, parts, 4 * zc - 1)), dma((9,)), dma((9,)), dma((2,)), dma((4,)), dma((1,)), dma((2,)), dma((2,))],
        compiler_params=pltpu.CompilerParams(collective_id=2, has_side_effects=True, vmem_limit_bytes=61 * 1024 * 1024),
        name="backward",
    )(full, mod, cotangent, stream_in, stream_mid, branch, projected, att, hidden, one_t, mixed_t, two_t, act_t)


AXES = ("wide", "narrow")


def running_rank(keep_flat):
    count = keep_flat.shape[0]
    lower = (lax.broadcasted_iota(jnp.int32, (count, count), 0) >= lax.broadcasted_iota(jnp.int32, (count, count), 1))
    total = jnp.dot(lower.astype(jnp.bfloat16), keep_flat.astype(jnp.bfloat16)[:, None], preferred_element_type=jnp.float32)
    return total[:, 0].astype(jnp.int32) - 1


def per_device_plain(kept_tokens, keep_mask, conditioning, ada_weight, ada_bias, qkv_weight, out_weight, up_weight, down_weight, position_bias, mask_token, cotangent):
    wide_count = lax.axis_size("wide")
    narrow_count = lax.axis_size("narrow")
    devices = wide_count * narrow_count
    slots = kept_tokens.shape[2]
    images = conditioning.shape[0]
    count = images * PATCHES
    rows = qkv_weight.shape[0]
    me = lax.axis_index(AXES)
    factor = 1.0 / math.sqrt(HEAD_DIM)
    low_type = jnp.bfloat16
    wide_type = jnp.float32
    silu_cond = jax.nn.silu(conditioning).astype(low_type)
    small = jnp.concatenate([silu_cond.reshape(-1), ada_bias.astype(low_type), mask_token.astype(low_type)])
    smalls = lax.all_gather(small, AXES, axis=0, tiled=False)
    silu_all = smalls[:, : images * D].reshape(devices * images, D)
    bias_full = smalls[:, images * D : images * D + ada_bias.shape[0]].reshape(-1)
    token_full = smalls[:, images * D + ada_bias.shape[0] :].reshape(-1)
    ada_low = ada_weight.astype(low_type)
    silu_part = lax.dynamic_slice_in_dim(silu_all, me * rows, rows, axis=1)
    mod_part = jnp.dot(silu_part, ada_low, preferred_element_type=wide_type)
    mod_parts = lax.all_to_all(mod_part.reshape(devices, images, 6 * D), AXES, split_axis=0, concat_axis=0, tiled=True)
    modulation = jnp.sum(mod_parts, axis=0) + bias_full.astype(wide_type)[None, :]
    qkv_full = lax.all_gather(qkv_weight.astype(low_type), AXES, axis=0, tiled=True)
    out_full = lax.all_gather(out_weight.astype(low_type), AXES, axis=0, tiled=True)
    up_full = lax.all_gather(up_weight.astype(low_type), AXES, axis=0, tiled=True)
    down_full = lax.all_gather(down_weight.astype(low_type), AXES, axis=0, tiled=True)
    def times_qkv(v):
        return jnp.dot(v, qkv_full, preferred_element_type=wide_type)
    def times_qkv_back(v):
        return jnp.dot(v, qkv_full.T, preferred_element_type=wide_type)
    def times_up(v):
        return jnp.dot(v, up_full, preferred_element_type=wide_type)
    def times_up_back(v):
        return jnp.dot(v, up_full.T, preferred_element_type=wide_type)
    arrived = lax.all_to_all(kept_tokens, AXES, split_axis=1, concat_axis=0, tiled=True)
    received = arrived.reshape(devices * slots, D)
    keep_flat = keep_mask.reshape(count)
    keep_float = keep_flat.astype(wide_type)
    ranks = running_rank(keep_flat)
    target = ranks % devices * slots + ranks // devices
    columns = jnp.arange(devices * slots, dtype=jnp.int32)
    selector = jnp.where((keep_flat[:, None] == 1) & (target[:, None] == columns[None, :]), 1.0, 0.0).astype(wide_type)
    stream_in = jnp.dot(selector.astype(low_type), received, preferred_element_type=wide_type)
    stream_in = stream_in + (1.0 - keep_float)[:, None] * token_full.astype(wide_type)[None, :]
    stream_in = stream_in.reshape(images, PATCHES, D)
    shift_one, scale_one, gate_one, shift_two, scale_two, gate_two = jnp.split(
        modulation[:, None, :], 6, axis=-1
    )
    normed_one = modulate(stream_in, shift_one, scale_one).astype(low_type).reshape(count, D)
    projected = times_qkv(normed_one).astype(low_type)
    projected = projected.reshape(images, PATCHES, 3, HEADS, HEAD_DIM)
    queries = projected[:, :, 0]
    key_rows = projected[:, :, 1]
    value_rows = projected[:, :, 2]
    relative = expand_bias(position_bias, GRID)
    scores = (
        jnp.einsum("iqhd,ikhd->ihqk", queries, key_rows, preferred_element_type=wide_type) * factor
        + relative[None]
    )
    att_weights = jax.nn.softmax(scores, axis=-1)
    att_low = att_weights.astype(low_type)
    mixed = (
        jnp.einsum("ihqk,ikhd->iqhd", att_low, value_rows, preferred_element_type=wide_type)
        .astype(low_type)
        .reshape(count, D)
    )
    branch = jnp.dot(mixed, out_full, preferred_element_type=wide_type).reshape(images, PATCHES, D)
    stream_mid = stream_in + gate_one * branch
    normed_two = modulate(stream_mid, shift_two, scale_two).astype(low_type).reshape(count, D)
    hidden = times_up(normed_two)
    activated = gelu_tanh(hidden).astype(low_type)
    down = jnp.dot(activated, down_full, preferred_element_type=wide_type).reshape(
        images, PATCHES, D
    )
    block_out = (stream_mid + gate_two * down).reshape(count, D).astype(low_type)
    incoming = cotangent.astype(wide_type).reshape(images, PATCHES, D)
    grad_gate_two = jnp.sum(incoming * down, axis=1)
    grad_down = (gate_two * incoming).astype(low_type).reshape(count, D)
    grad_activated = jnp.dot(grad_down, down_full.T, preferred_element_type=wide_type)
    _, gelu_pull = jax.vjp(gelu_tanh, hidden)
    grad_hidden = gelu_pull(grad_activated)[0].astype(low_type)
    grad_normed_two = times_up_back(grad_hidden).reshape(
        images, PATCHES, D
    )
    _, norm_pull_two = jax.vjp(modulate, stream_mid, shift_two, scale_two)
    grad_mid_norm, grad_shift_two, grad_scale_two = norm_pull_two(grad_normed_two)
    grad_mid = incoming + grad_mid_norm
    grad_gate_one = jnp.sum(grad_mid * branch, axis=1)
    grad_branch = (gate_one * grad_mid).astype(low_type).reshape(count, D)
    grad_mixed = jnp.dot(grad_branch, out_full.T, preferred_element_type=wide_type).astype(low_type)
    grad_mixed = grad_mixed.reshape(images, PATCHES, HEADS, HEAD_DIM)
    grad_att = jnp.einsum(
        "iqhd,ikhd->ihqk", grad_mixed, value_rows, preferred_element_type=wide_type
    )
    grad_values = jnp.einsum(
        "ihqk,iqhd->ikhd", att_low, grad_mixed, preferred_element_type=wide_type
    )
    grad_scores = (
        att_weights * (grad_att - jnp.sum(att_weights * grad_att, axis=-1, keepdims=True))
    ).astype(low_type)
    grad_queries = (
        jnp.einsum("ihqk,ikhd->iqhd", grad_scores, key_rows, preferred_element_type=wide_type)
        * factor
    )
    grad_keys = (
        jnp.einsum("ihqk,iqhd->ikhd", grad_scores, queries, preferred_element_type=wide_type)
        * factor
    )
    grad_table = bias_adjoint(jnp.sum(grad_scores.astype(wide_type), axis=0), GRID)
    grad_projected = (
        jnp.stack([grad_queries, grad_keys, grad_values], axis=2)
        .astype(low_type)
        .reshape(count, 3 * D)
    )
    grad_normed_one = times_qkv_back(grad_projected).reshape(
        images, PATCHES, D
    )
    _, norm_pull_one = jax.vjp(modulate, stream_in, shift_one, scale_one)
    grad_in_norm, grad_shift_one, grad_scale_one = norm_pull_one(grad_normed_one)
    grad_in = (grad_mid + grad_in_norm).reshape(count, D)
    grad_modulation = jnp.concatenate(
        [
            grad_shift_one[:, 0],
            grad_scale_one[:, 0],
            grad_gate_one,
            grad_shift_two[:, 0],
            grad_scale_two[:, 0],
            grad_gate_two,
        ],
        axis=-1,
    ).astype(low_type)
    grad_mod_all = lax.all_gather(grad_modulation, AXES, axis=0, tiled=True)
    grad_ada = lax.dot_general(silu_part, grad_mod_all, (((0,), (0,)), ((), ())), preferred_element_type=wide_type)
    bias_share = 6 * D // devices
    sum_bias = jnp.sum(lax.dynamic_slice_in_dim(grad_mod_all, me * bias_share, bias_share, axis=1).astype(wide_type), axis=0)
    silu_parts = lax.dot_general(grad_mod_all, ada_low, (((1,), (1,)), ((), ())), preferred_element_type=wide_type)
    silu_parts = lax.all_to_all(silu_parts.reshape(devices, images, rows), AXES, split_axis=0, concat_axis=0, tiled=True)
    grad_silu = silu_parts.transpose(1, 0, 2).reshape(images, D)
    _, silu_pull = jax.vjp(jax.nn.silu, conditioning)
    grad_cond = silu_pull(grad_silu)[0]
    grad_mask = jnp.sum((1.0 - keep_float)[:, None] * grad_in, axis=0)
    grad_received = jnp.dot(
        selector.T, grad_in, precision=lax.Precision.HIGHEST, preferred_element_type=wide_type
    ).astype(low_type)
    grad_kept = lax.all_to_all(
        grad_received.reshape(devices, 1, slots, D),
        ("wide", "narrow"),
        split_axis=0,
        concat_axis=1,
        tiled=True,
    )
    def scatter(left, right):
        partial = lax.dot_general(left, right, (((0,), (0,)), ((), ())), preferred_element_type=wide_type)
        return lax.psum_scatter(partial.reshape(-1), AXES, scatter_dimension=0, tiled=True).reshape(-1, right.shape[1])
    sum_qkv = scatter(normed_one, grad_projected)
    sum_out = scatter(mixed, grad_branch)
    sum_up = scatter(normed_two, grad_hidden)
    sum_down = scatter(activated, grad_down)
    grad_table_all, mask_whole = lax.psum((grad_table, grad_mask), AXES)
    mask_share = D // devices
    sum_mask = lax.dynamic_slice_in_dim(mask_whole, me * mask_share, mask_share)
    return (block_out, grad_kept, grad_cond, grad_ada, sum_bias, sum_qkv, sum_out, sum_up, sum_down, grad_table_all, sum_mask)


def to_all(row, devices):
    spread = jnp.broadcast_to(row[None], (devices,) + row.shape)
    return lax.all_to_all(spread, AXES, split_axis=0, concat_axis=0, tiled=True)


def lay_bias(table):
    turned = table[:, ::-1, ::-1]
    rows = [turned[:, :, GRID - 1 - x : 2 * GRID - 1 - x].reshape(HEADS, 1, -1) for x in range(GRID)]
    return jnp.pad(jnp.concatenate(rows, axis=1), ((0, 0), (0, 0), (0, GRID)))


def unlay_bias(spread):
    rows = spread[:, :, : (2 * GRID - 1) * GRID].reshape(HEADS, GRID, 2 * GRID - 1, GRID)
    total = sum(jnp.pad(rows[:, x], ((0, 0), (0, 0), (GRID - 1 - x, x))) for x in range(GRID))
    return total[:, ::-1, ::-1]


def per_device(kept_tokens, keep_mask, conditioning, ada_weight, ada_bias, qkv_weight, out_weight, up_weight, down_weight, position_bias, mask_token, cotangent):
    wide_count = lax.axis_size("wide")
    devices = wide_count * lax.axis_size("narrow")
    slots = kept_tokens.shape[2]
    rows = qkv_weight.shape[0]
    share = ada_bias.shape[0]
    me = lax.axis_index(AXES)
    zc = wide_count // 2
    attn_src = jnp.concatenate([qkv_weight.reshape(rows, 3, D), out_weight.reshape(rows, 1, D)], axis=1)
    both = jnp.stack([attn_src, up_weight.reshape(rows, 4, D)], axis=0).astype(BF16)
    turned = lax.all_to_all(both.transpose(2, 0, 1, 3), "narrow", split_axis=0, concat_axis=0, tiled=True)
    turned = turned.transpose(1, 0, 2, 3).reshape(2, ROWS, D)
    source = jnp.concatenate([turned, down_weight.astype(BF16)[None]], axis=0)

    silu_cond = jax.nn.silu(conditioning).astype(BF16)
    smalls = to_all(jnp.concatenate([silu_cond.reshape(-1), ada_bias.astype(BF16), mask_token.astype(BF16)]), devices)
    silu_part = lax.dynamic_slice_in_dim(smalls[:, :D], me * rows, rows, axis=1)
    bias_full = smalls[:, D : D + share].reshape(1, -1).astype(F32)
    token_full = smalls[:, D + share :].reshape(1, D).astype(F32)
    ada_low = ada_weight.astype(BF16)
    mod_part = jnp.dot(silu_part, ada_low, preferred_element_type=F32)
    mod_parts = lax.all_to_all(mod_part, AXES, split_axis=0, concat_axis=0, tiled=True)
    mod = (jnp.sum(mod_parts, axis=0, keepdims=True) + bias_full).reshape(6, D)

    received = lax.all_to_all(kept_tokens, AXES, split_axis=1, concat_axis=0, tiled=True).reshape(devices * slots, D)
    keep = keep_mask.reshape(PATCHES)
    keep_float = keep.astype(F32)[:, None]
    ranks = running_rank(keep)
    target = ranks % devices * slots + ranks // devices
    columns = jnp.arange(devices * slots, dtype=jnp.int32)
    selector = ((keep[:, None] == 1) & (target[:, None] == columns[None, :])).astype(BF16)
    stream_in = jnp.dot(selector, received, preferred_element_type=F32) + (1.0 - keep_float) * token_full

    (full, block_out, one_t, projected, att, mixed_t, branch, stream_mid, two_t, hidden, act_t, gate_sum) = run_forward(
        source, stream_in, mod, lay_bias(position_bias), cotangent, zc)
    owned, spread_grad, grad_in, small = run_backward(
        full, mod, cotangent, stream_in, stream_mid, branch, projected, att, hidden, one_t, mixed_t, two_t, act_t, zc)

    grad_modulation = jnp.concatenate([small[:5].reshape(-1), gate_sum.reshape(-1)]).astype(BF16)
    grad_mod_all = to_all(grad_modulation, devices)
    grad_ada = lax.dot_general(silu_part, grad_mod_all, TN, preferred_element_type=F32)
    sum_bias = jnp.sum(lax.dynamic_slice_in_dim(grad_mod_all, me * share, share, axis=1).astype(F32), axis=0)
    silu_parts = lax.dot_general(grad_mod_all, ada_low, NT, preferred_element_type=F32)
    grad_silu = lax.all_to_all(silu_parts, AXES, split_axis=0, concat_axis=0, tiled=True).reshape(1, D)
    _, silu_pull = jax.vjp(jax.nn.silu, conditioning)
    grad_cond = silu_pull(grad_silu)[0]

    grad_mask = jnp.sum((1.0 - keep_float) * grad_in, axis=0)
    grad_received = lax.dot_general(selector, grad_in.astype(BF16), TN, preferred_element_type=F32).astype(BF16)
    grad_kept = lax.all_to_all(grad_received.reshape(devices, 1, slots, D), AXES, split_axis=0, concat_axis=1, tiled=True)

    table_size = position_bias.size
    line = -(-table_size // devices)
    table = jnp.pad(unlay_bias(spread_grad).reshape(-1), (0, line * devices - table_size)).reshape(devices, line)
    parts = lax.all_to_all(jnp.concatenate([table, grad_mask.reshape(devices, rows)], axis=1), AXES, split_axis=0, concat_axis=0, tiled=True)
    summed = jnp.sum(parts, axis=0)
    sum_mask = summed[line:]
    grad_table = to_all(summed[:line], devices).reshape(-1)[:table_size].reshape(position_bias.shape)

    sum_down = owned[2]
    turned = owned[:2].reshape(2, 4, rows, D).transpose(1, 0, 2, 3)
    turned = lax.all_to_all(turned, "narrow", split_axis=0, concat_axis=0, tiled=True)
    sum_qkv = turned[:3, 0].transpose(1, 0, 2).reshape(rows, 3 * D)
    sum_out = turned[3, 0]
    sum_up = turned[:, 1].transpose(1, 0, 2).reshape(rows, FF)
    return (block_out, grad_kept, grad_cond, grad_ada, sum_bias, sum_qkv, sum_out, sum_up, sum_down, grad_table, sum_mask)


def solution(mesh):
    in_specs = (
        P(("wide", "narrow"), None, None, None),
        P(("wide", "narrow"), None),
        P(("wide", "narrow"), None),
        P(("wide", "narrow"), None),
        P(("wide", "narrow")),
        P(("wide", "narrow"), None),
        P(("wide", "narrow"), None),
        P(("wide", "narrow"), None),
        P(("wide", "narrow"), None),
        P(),
        P(("wide", "narrow")),
        P(("wide", "narrow"), None),
    )
    out_specs = (
        P(("wide", "narrow"), None),
        P(("wide", "narrow"), None, None, None),
        P(("wide", "narrow"), None),
        P(("wide", "narrow"), None),
        P(("wide", "narrow")),
        P(("wide", "narrow"), None),
        P(("wide", "narrow"), None),
        P(("wide", "narrow"), None),
        P(("wide", "narrow"), None),
        P(),
        P(("wide", "narrow")),
    )
    shape = dict(mesh.shape)
    rows = D // (shape["wide"] * shape["narrow"])
    fast = shape["narrow"] == 4 and shape["wide"] % 2 == 0 and rows * 4 == ROWS
    return jax.shard_map(
        per_device if fast else per_device_plain, mesh=mesh, in_specs=in_specs, out_specs=out_specs, check_vma=False
    )
```

```python
import functools
import math

import jax
import jax.numpy as jnp
from jax import lax
from jax.experimental import pallas as pl
from jax.experimental.pallas import tpu as pltpu
from jax.sharding import PartitionSpec as P

D = 1152
HEADS = 16
HEAD_DIM = 72
FF = 4608
GRID = 16
PATCHES = 256


EPSILON = 1e-06


def layer_norm(stream):
    center = stream - jnp.mean(stream, axis=-1, keepdims=True)
    variance = jnp.mean(center * center, axis=-1, keepdims=True)
    return center * lax.rsqrt(variance + EPSILON)


def modulate(stream, shift, scale):
    return layer_norm(stream) * (1.0 + scale) + shift


def offset_picker(grid):
    places = jnp.arange(grid, dtype=jnp.int32)
    spread = jnp.arange(2 * grid - 1, dtype=jnp.int32)
    return (
        places[:, None, None] - places[None, :, None] + grid - 1 == spread[None, None, :]
    ).astype(jnp.float32)


def expand_bias(table, grid):
    picker = offset_picker(grid)
    partial_rows = jnp.einsum("yka,had->hykd", picker, table, precision=lax.Precision.HIGHEST)
    expanded = jnp.einsum("hykd,xjd->hyxkj", partial_rows, picker, precision=lax.Precision.HIGHEST)
    return expanded.reshape(table.shape[0], grid * grid, grid * grid)


def bias_adjoint(grad_bias, grid):
    picker = offset_picker(grid)
    shaped = grad_bias.reshape(grad_bias.shape[0], grid, grid, grid, grid)
    partial_rows = jnp.einsum("hyxkj,xjd->hykd", shaped, picker, precision=lax.Precision.HIGHEST)
    return jnp.einsum("hykd,yka->had", partial_rows, picker, precision=lax.Precision.HIGHEST)


def gelu_tanh(value):
    return jax.nn.gelu(value, approximate=True)


MESH = pl.DeviceIdType.MESH
ROWS = 144
PARTS = ((0, 80, "zxy"), (80, 64, "zyx"))
AT = {"z": 0, "y": 1, "x": 2}
F32 = jnp.float32
BF16 = jnp.bfloat16
FACTOR = 1.0 / math.sqrt(HEAD_DIM)
NT = (((1,), (1,)), ((), ()))
TN = (((0,), (0,)), ((), ()))
SPAN = 2 * PATCHES


def rels(zc):
    return [(rz, ry, rx) for rz in range(zc) for ry in range(2) for rx in range(2)]


class Place:
    def __init__(self, zc):
        wide = lax.axis_index("wide")
        narrow = lax.axis_index("narrow")
        self.zc, self.wcount = zc, 2 * zc
        self.line, self.count = wide * 4 + narrow, 8 * zc
        self.z, self.y, self.x, self.c = wide // 2, wide % 2, narrow // 2, narrow % 2
        self.hops = {"z": [(k, 0, 0) for k in range(1, zc)], "y": [(0, 1, 0)], "x": [(0, 0, 1)]}

    def shifted(self, rz, ry, rx):
        w = lax.rem(self.z + rz, self.zc) * 2 + (self.y + ry) % 2
        return w, (self.x + rx) % 2

    def device(self, rz, ry, rx, flip=0):
        w, x = self.shifted(rz, ry, rx)
        return w, x * 2 + (self.c + flip) % 2

    def greet(self):
        barrier = pltpu.get_barrier_semaphore()
        def hello(k, carry):
            t = lax.rem(self.line + k, self.count)
            pl.semaphore_signal(barrier, inc=1, device_id=(t // 4, t % 4), device_id_type=MESH)
            return carry
        lax.fori_loop(1, self.count, hello, 0)
        pl.semaphore_wait(barrier, self.count - 1)

    def turned(self, t):
        return t % 2 * (self.count // 2) + t // 2

    def exchange(self, piece, there, send, recv):
        def go(k, carry):
            t = lax.rem(self.line + k, self.count)
            pltpu.make_async_remote_copy(
                src_ref=piece(t), dst_ref=there, send_sem=send, recv_sem=recv,
                device_id=(t // 4, t % 4), device_id_type=MESH).start()
            return carry
        lax.fori_loop(1, self.count, go, 0)

    def exchange_chips(self, piece, there, send, recv):
        def go(k, carry):
            t = lax.rem(self.line + 2 * k, self.count)
            pltpu.make_async_remote_copy(
                src_ref=piece(t // 2), dst_ref=there, send_sem=send, recv_sem=recv,
                device_id=(t // 4, t % 4), device_id_type=MESH).start()
            return carry
        lax.fori_loop(1, self.count // 2, go, 0)

    def exchanged(self, got, sem):
        others = got.at[pl.ds(0, got.shape[0] - 1)]
        pltpu.make_async_copy(others, others, sem).wait()


def wait_rows(ref, total, sem):
    for blocks in range(1, ref.shape[0] + 1):
        if total % (blocks * 16) == 0 and total // blocks <= ref.shape[1]:
            some = ref.at[pl.ds(0, blocks), pl.ds(0, total // blocks)]
            pltpu.make_async_copy(some, some, sem).wait()
            return
    raise ValueError("rows")


def each_rows(total, step, body):
    def go(i, carry):
        body(pl.ds(pl.multiple_of(i * step, step), step))
        return carry
    lax.fori_loop(0, total // step, go, 0)


def each_columns(body):
    def go(i, carry):
        body(pl.ds(pl.multiple_of(i * 256, 256), 256))
        return carry
    lax.fori_loop(0, 4, go, 0)
    body(pl.ds(1024, 128))


def window(head):
    low = head * HEAD_DIM
    first, last = low // 128 * 128, -(-(low + HEAD_DIM) // 128) * 128
    lane = lax.broadcasted_iota(jnp.int32, (1, last - first), 1) + first
    mask = jnp.where((lane >= low) & (lane < low + HEAD_DIM), 1.0, 0.0).astype(F32)
    return slice(first, last), mask


class Gather:
    def __init__(self, me, src, out, sems):
        self.me, self.src, self.out = me, src, out
        self.send, self.recv, self.sib_send, self.sib_recv, self.own = sems
        self.all = rels(me.zc)
        self.index = {r: i for i, r in enumerate(self.all)}

    def block(self, g, rel, r0, rows):
        w, x = self.me.shifted(self.me.zc - rel[0], rel[1], rel[2])
        n = x * 2 + self.me.c
        b, row = (n, w * ROWS) if g < 2 else ((w * 4 + n) // self.me.wcount, lax.rem(w * 4 + n, self.me.wcount) * ROWS)
        return self.out.at[g, b, pl.ds(pl.multiple_of(row + r0, 16), rows)]

    def forward(self, g, p, rel):
        r0, rows, order = PARTS[p]
        at = max([i for i, d in enumerate(order) if rel[AT[d]]], default=-1)
        there = self.block(g, rel, r0, rows)
        here = there if any(rel) else self.src.at[g, pl.ds(r0, rows)]
        for d in order[at + 1:]:
            for h in self.me.hops[d]:
                seen = ((rel[0] + h[0]) % self.me.zc, (rel[1] + h[1]) % 2, (rel[2] + h[2]) % 2)
                pltpu.make_async_remote_copy(
                    src_ref=here, dst_ref=there, send_sem=self.send.at[g, p], recv_sem=self.recv.at[g, p, self.index[seen]],
                    device_id=self.me.device(*h), device_id_type=MESH).start()
        pltpu.make_async_remote_copy(
            src_ref=here, dst_ref=there, send_sem=self.sib_send.at[g, p], recv_sem=self.sib_recv.at[g, p],
            device_id=self.me.device(0, 0, 0, 1), device_id_type=MESH).start()

    def begin(self, g):
        for p in range(len(PARTS)):
            self.forward(g, p, (0, 0, 0))
        pltpu.make_async_copy(self.src.at[g], self.block(g, (0, 0, 0), 0, ROWS), self.own.at[g]).start()

    def ticks(self, g):
        todo = []
        for deep in (1, 2, 3):
            for rel in self.all:
                if sum(1 for v in rel if v) == deep:
                    todo.append(functools.partial(self.tick, g, rel))
        return todo

    def tick(self, g, rel):
        for p, (r0, rows, _) in enumerate(PARTS):
            wait_rows(self.out.at[g], rows, self.recv.at[g, p, self.index[rel]])
            self.forward(g, p, rel)

    def arrived(self, g):
        pltpu.make_async_copy(self.src.at[g], self.src.at[g], self.own.at[g]).wait()
        for p, (r0, rows, _) in enumerate(PARTS):
            wait_rows(self.out.at[g], 4 * self.me.zc * rows, self.sib_recv.at[g, p])

    def finish(self, g):
        for p, (r0, rows, _) in enumerate(PARTS):
            wait_rows(self.out.at[g], (4 * self.me.zc - 1) * rows, self.send.at[g, p])
            wait_rows(self.out.at[g], 4 * self.me.zc * rows, self.sib_send.at[g, p])


class Blocks:
    def __init__(self, full, buf, sems, order):
        self.full, self.buf, self.sems, self.order = full, buf, sems, order

    def fetch(self, i):
        if i < len(self.order):
            g, b = self.order[i]
            pltpu.make_async_copy(self.full.at[g, b], self.buf.at[i % 2], self.sems.at[i % 2]).start()

    def take(self, i):
        g, b = self.order[i]
        pltpu.make_async_copy(self.full.at[g, b], self.buf.at[i % 2], self.sems.at[i % 2]).wait()
        return self.buf.at[i % 2]


def standard(v):
    center = v - jnp.mean(v, axis=-1, keepdims=True)
    spread = lax.rsqrt(jnp.mean(center * center, axis=-1, keepdims=True) + EPSILON)
    return center * spread, spread


def gelu(v):
    return 0.5 * v * (1.0 + jnp.tanh(0.7978845608 * (v + 0.044715 * v * v * v)))


def gelu_slope(v):
    t = jnp.tanh(0.7978845608 * (v + 0.044715 * v * v * v))
    return 0.5 * (1.0 + t) + 0.5 * v * (1.0 - t * t) * 0.7978845608 * (1.0 + 3.0 * 0.044715 * v * v)


def turn(ref, out):
    def body(cols):
        out[cols, :] = ref[:, cols].astype(F32).T.astype(BF16)
    each_columns(body)


def table_picker(x, entries, line):
    entry = lax.broadcasted_iota(jnp.int32, (entries, line), 0) % 128
    lane = lax.broadcasted_iota(jnp.int32, (entries, line), 1)
    return jnp.where(entry == x - lane % GRID + GRID - 1, 1.0, 0.0).astype(BF16)


def row_picker(line):
    row = lax.broadcasted_iota(jnp.int32, (2 * GRID, line), 0)
    lane = lax.broadcasted_iota(jnp.int32, (2 * GRID, line), 1)
    return jnp.where(row == 2 * GRID - 2 - lane // GRID, 1.0, 0.0).astype(F32)


def forward_kernel(zc, src, silu_out, ada, bias_row, token_row, kept, keep, table, cotangent,
                   full, block_out, one_t, projected, att, mixed_t, branch,
                   stream_mid, two_t, hidden, act_t, stream_in, mod, silu_part, selector, gate_sum,
                   wbuf, normed, wide_one, act, turned, silu_got, mod_rows, mod_sib, mod_got, kept_got, spread_bias,
                   send, recv, sib_send, sib_recv, own, wsem, small_send, small_recv):
    me = Place(zc)
    me.greet()
    net = Gather(me, src, full, (send, recv, sib_send, sib_recv, own))
    blocks = Blocks(full, wbuf, wsem, [(0, 0), (0, 1), (0, 2), (0, 3), (1, 0), (1, 1), (1, 2), (1, 3), (2, 0), (2, 1), (2, 2), (2, 3)])
    core_line = me.turned(me.line)
    me.exchange(lambda t: silu_out.at[t], silu_got.at[core_line], small_send.at[0], small_recv.at[0])
    net.begin(0)
    me.exchange(lambda t: kept.at[t], kept_got.at[me.line], small_send.at[1], small_recv.at[1])
    silu_got[core_line] = silu_out[me.line]
    kept_got[me.line] = kept[me.line]
    ticks = net.ticks(0)

    me.exchanged(silu_got, small_recv.at[0])
    silu_part[...] = silu_got[:, 0, :]
    mine = silu_part[:, : ada.shape[0]].astype(BF16)
    def mod_column(j, carry):
        lanes = pl.ds(pl.multiple_of(j * 128, 128), 128)
        v = jnp.dot(mine, ada[:, lanes].astype(BF16), preferred_element_type=F32) + bias_row[:, lanes]
        mod_rows[:, pl.ds(j, 1), :] = v[:, None, :]
        return carry
    lax.fori_loop(0, 54, mod_column, 0)
    def token_column(j, carry):
        v = jnp.broadcast_to(token_row[:, pl.ds(pl.multiple_of(j * 128, 128), 128)], (me.count, 128))
        mod_rows[:, pl.ds(54 + j, 1), :] = v[:, None, :]
        return carry
    lax.fori_loop(0, 9, token_column, 0)
    mod_rows[:, 63:64, :] = jnp.zeros((me.count, 1, 128), F32)
    half = me.count // 2
    chip = me.line // 2
    mod_swap = pltpu.make_async_remote_copy(
        src_ref=mod_rows.at[pl.ds((1 - me.c) * half, half)], dst_ref=mod_sib, send_sem=small_send.at[3], recv_sem=small_recv.at[3],
        device_id=me.device(0, 0, 0, 1), device_id_type=MESH)
    mod_swap.start()
    for _ in range(3):
        ticks.pop(0)()
    mod_swap.wait()
    def both(i, carry):
        mod_sib[i] += mod_rows[me.c * half + i]
        return carry
    lax.fori_loop(0, half, both, 0)
    me.exchange_chips(lambda t: mod_sib.at[t], mod_got.at[chip], small_send.at[2], small_recv.at[2])
    mod_got[chip] = mod_sib[chip]
    for _ in range(2):
        ticks.pop(0)()

    v = table[...]
    high = v.astype(BF16)
    rest = v - high.astype(F32)
    middle = rest.astype(BF16)
    halves = jnp.concatenate([high, middle, (rest - middle.astype(F32)).astype(BF16)], axis=1)
    picked_rows = row_picker(SPAN)
    def spread(x, carry):
        got = jnp.dot(halves, table_picker(x, 384, SPAN), preferred_element_type=F32)
        spread_bias[x] = jnp.sum(got.reshape(HEADS, 2 * GRID, SPAN) * picked_rows[None], axis=1)
        return carry
    lax.fori_loop(0, GRID // 2, spread, 0)
    for _ in range(4):
        ticks.pop(0)()
    lax.fori_loop(GRID // 2, GRID, spread, 0)

    row = lax.broadcasted_iota(jnp.int32, (PATCHES, PATCHES), 0)
    column = lax.broadcasted_iota(jnp.int32, (PATCHES, PATCHES), 1)
    kept_here = keep[...].astype(F32)
    before = jnp.where(row >= column, 1.0, 0.0).astype(BF16)
    ranks = jnp.dot(before, jnp.broadcast_to(kept_here, (PATCHES, 128)).astype(BF16), preferred_element_type=F32)
    ranks = ranks[:, :1].astype(jnp.int32) - 1
    slot = (ranks % me.count) * 8 + ranks // me.count
    selector[...] = jnp.where((keep[...] == 1) & (slot == column), 1.0, 0.0).astype(BF16)
    me.exchanged(mod_got, small_recv.at[2])
    total = mod_got[0]
    for i in range(1, half):
        total += mod_got[i]
    for i in range(63):
        mod[i // 9:i // 9 + 1, i % 9 * 128:(i % 9 + 1) * 128] = total[i:i + 1, :]
    me.exchanged(kept_got, small_recv.at[1])
    def put(cols):
        v = jnp.dot(selector[...], kept_got[:, :, cols].reshape(me.count * 8, -1), preferred_element_type=F32)
        stream_in[:, cols] = v + (1.0 - kept_here) * mod[6:7, cols]
    each_columns(put)

    def norm_one(rows):
        n, _ = standard(stream_in[rows, :])
        normed[rows, :] = (n * (1.0 + mod[1:2, :]) + mod[0:1, :]).astype(BF16)
    each_rows(PATCHES, 32, norm_one)
    turn(normed, one_t)
    net.begin(1)
    for tick in ticks:
        tick()
    net.arrived(0)
    ticks = net.ticks(1)
    blocks.fetch(0)
    blocks.fetch(1)
    for b in range(3):
        w = blocks.take(b)
        def product(cols):
            projected[b, :, cols] = jnp.dot(normed[...], w[:, cols], preferred_element_type=F32).astype(BF16)
        each_columns(product)
        blocks.fetch(b + 2) if b + 2 < 4 else None
        ticks.pop(0)()
    wide_one[...] = jnp.zeros_like(wide_one)
    for head in range(HEADS):
        lanes, mask = window(head)
        q = projected[0, :, lanes] * mask.astype(BF16)
        scores = lax.dot_general(q, projected[1, :, lanes], NT, preferred_element_type=F32) * FACTOR
        u = spread_bias[:, head, :]
        bias = jnp.concatenate(
            [pltpu.roll(u, (SPAN - (GRID - 1 - r) * GRID) % SPAN, 1)[:, :PATCHES] for r in range(GRID)], axis=0)
        scores = scores + bias
        e = jnp.exp(scores - jnp.max(scores, axis=-1, keepdims=True))
        weights = e * (1.0 / jnp.sum(e, axis=-1, keepdims=True))
        att[head] = weights
        got = jnp.dot(weights.astype(BF16), projected[2, :, lanes], preferred_element_type=F32)
        wide_one[:, lanes] += got * mask
        if head % 2 and ticks:
            ticks.pop(0)()
        if head == 11:
            net.begin(2)
    normed[...] = wide_one[...].astype(BF16)
    turn(normed, mixed_t)
    w = blocks.take(3)
    def product(cols):
        branch[:, cols] = jnp.dot(normed[...], w[:, cols], preferred_element_type=F32)
    each_columns(product)
    def mid(rows):
        v = stream_in[rows, :] + mod[2:3, :] * branch[rows, :]
        stream_mid[rows, :] = v
        n, _ = standard(v)
        normed[rows, :] = (n * (1.0 + mod[4:5, :]) + mod[3:4, :]).astype(BF16)
    each_rows(PATCHES, 32, mid)
    turn(normed, two_t)
    for tick in ticks:
        tick()
    net.arrived(1)
    ticks = net.ticks(2)
    blocks.fetch(4)
    blocks.fetch(5)
    def turn_units(ref, b):
        turn(ref, turned)
        for i in range(8):
            unit = b * 8 + i
            w, n = unit // 4, unit % 4
            act_t[n % 2, n // 2, w * ROWS:(w + 1) * ROWS, :] = turned[i * ROWS:(i + 1) * ROWS, :]
    for b in range(4):
        w = blocks.take(4 + b)
        def product(cols):
            v = jnp.dot(normed[...], w[:, cols], preferred_element_type=F32)
            hidden[b, :, cols] = v
        each_columns(product)
        if b < 2:
            blocks.fetch(6 + b)
        def bend(rows):
            act[b, rows, :] = gelu(hidden[b, rows, :]).astype(BF16)
        each_rows(PATCHES, 32, bend)
        turn_units(act.at[b], b)
        for _ in range(2):
            ticks.pop(0)()
    for tick in ticks:
        tick()
    net.arrived(2)
    blocks.fetch(8)
    blocks.fetch(9)
    for b in range(4):
        w = blocks.take(8 + b)
        def product(cols):
            v = jnp.dot(act[b], w[:, cols], preferred_element_type=F32)
            wide_one[:, cols] = v if b == 0 else wide_one[:, cols] + v
        each_columns(product)
        if b < 2:
            blocks.fetch(10 + b)
    gate_sum[...] = jnp.zeros_like(gate_sum)
    def last(rows):
        v = wide_one[rows, :]
        block_out[rows, :] = (stream_mid[rows, :] + mod[5:6, :] * v).astype(BF16)
        gate_sum[...] += jnp.sum(cotangent[rows, :].astype(F32) * v, axis=0, keepdims=True)
    each_rows(PATCHES, 32, last)
    for g in range(3):
        net.finish(g)
    for i, got in enumerate((silu_got, kept_got, mod_got)):
        me.exchanged(got, small_send.at[i])


def run_forward(src, silu_out, ada, bias_row, token_row, kept, keep, table, cotangent, zc):
    vmem = pl.BlockSpec(memory_space=pltpu.VMEM)
    hbm = pl.BlockSpec(memory_space=pl.ANY)
    parts, count = len(PARTS), 8 * zc
    shape = jax.ShapeDtypeStruct
    dma = pltpu.SemaphoreType.DMA
    return pl.pallas_call(
        functools.partial(forward_kernel, zc),
        out_shape=(
            shape((3, 4, D, D), BF16), shape((PATCHES, D), BF16), shape((D, PATCHES), BF16), shape((3, PATCHES, D), BF16),
            shape((HEADS, PATCHES, PATCHES), F32), shape((D, PATCHES), BF16), shape((PATCHES, D), F32), shape((PATCHES, D), F32),
            shape((D, PATCHES), BF16), shape((4, PATCHES, D), F32), shape((2, 2, D, PATCHES), BF16), shape((PATCHES, D), F32),
            shape((8, D), F32), shape((count, 128), F32), shape((PATCHES, PATCHES), BF16), shape((1, D), F32)),
        in_specs=[hbm] + [vmem] * 8,
        out_specs=(hbm,) + (vmem,) * 15,
        scratch_shapes=[
            pltpu.VMEM((2, D, D), BF16), pltpu.VMEM((PATCHES, D), BF16), pltpu.VMEM((PATCHES, D), F32), pltpu.VMEM((4, PATCHES, D), BF16), pltpu.VMEM((D, PATCHES), BF16),
            pltpu.VMEM((count, 8, 128), F32), pltpu.VMEM((count, 64, 128), F32), pltpu.VMEM((count // 2, 64, 128), F32), pltpu.VMEM((count // 2, 64, 128), F32),
            pltpu.VMEM((count, 8, D), BF16), pltpu.VMEM((GRID, HEADS, SPAN), F32),
            dma((3, parts)), dma((3, parts, 4 * zc)), dma((3, parts)), dma((3, parts)), dma((3,)), dma((2,)), dma((4,)), dma((4,))],
        compiler_params=pltpu.CompilerParams(collective_id=1, has_side_effects=True, vmem_limit_bytes=58 * 1024 * 1024),
        name="forward",
    )(src, silu_out, ada, bias_row, token_row, kept, keep, table, cotangent)


def reduce_plan(zc, order):
    live, slots, phases = rels(zc), {}, []
    for j, d in enumerate(order[::-1]):
        sends = [r for r in live if r[AT[d]]]
        live = [r for r in live if not r[AT[d]]]
        hops = list(range(1, zc)) if d == "z" else [1]
        for r in live:
            for k in hops:
                slots[r, j, k] = len(slots)
        phases.append((d, sends, live, hops))
    return phases, slots


class Reduce:
    def __init__(self, me, sums, landed, owned, send, recv):
        self.me, self.sums, self.landed, self.owned, self.send_sem, self.recv = me, sums, landed, owned, send, recv
        self.plans = [reduce_plan(me.zc, part[2]) for part in PARTS]
        self.held = {}
        self.items = [(g, k) for g in (2, 1, 0) for k in list(range(1, me.zc)) + [0]]

    def partial(self, g, p, rel):
        r0, rows, _ = PARTS[p]
        if (g, p, rel) in self.held:
            return self.landed.at[g, self.held[g, p, rel], pl.ds(r0, rows)]
        w, x = self.me.shifted(*rel)
        return self.sums[g].at[x, pl.ds(pl.multiple_of(w * ROWS + r0, 16), rows)]

    def send(self, g, p, j, rel):
        r0, rows, _ = PARTS[p]
        d = self.plans[p][0][j][0]
        k = rel[AT[d]]
        hop = tuple(k if i == AT[d] else 0 for i in range(3))
        there = tuple(0 if i == AT[d] else rel[i] for i in range(3))
        slot = self.plans[p][1][there, j, k]
        pltpu.make_async_remote_copy(
            src_ref=self.partial(g, p, rel), dst_ref=self.landed.at[g, slot, pl.ds(r0, rows)],
            send_sem=self.send_sem.at[g, p, min(j, 1)], recv_sem=self.recv.at[g, p, slot],
            device_id=self.me.device(*hop), device_id_type=MESH).start()

    def receive(self, g, p, j, rel, final):
        r0, rows, _ = PARTS[p]
        slots = [self.plans[p][1][rel, j, k] for k in self.plans[p][0][j][3]]
        for s in slots:
            ref = self.landed.at[g, s, pl.ds(r0, rows)]
            pltpu.make_async_copy(ref, ref, self.recv.at[g, p, s]).wait()
        mine = self.partial(g, p, rel)
        def body(i, carry):
            at = pl.ds(pl.multiple_of(r0 + i * 16, 16), 16)
            total = mine[pl.ds(pl.multiple_of(i * 16, 16), 16), :].astype(F32)
            for s in slots:
                total += self.landed[g, s, at, :].astype(F32)
            if final:
                self.owned[g][at, :] = total.astype(self.owned[g].dtype)
            else:
                self.landed[g, slots[0], at, :] = total.astype(BF16)
            return carry
        lax.fori_loop(0, rows // 16, body, 0)
        self.held[g, p, rel] = slots[0]

    def stage(self, j, g, k):
        for p in range(len(PARTS)):
            phases = self.plans[p][0]
            lowered = [r for r in phases[j - 1][2] if r[0] == k] if j else []
            sends = [r for r in phases[j][1] if r[0] == k] if j < 3 else []
            for rel in sorted(lowered, key=lambda r: r not in sends):
                self.receive(g, p, j - 1, rel, j == 3)
                if rel in sends:
                    self.send(g, p, j, rel)
            if j == 0:
                for rel in sends:
                    self.send(g, p, 0, rel)

    def step(self, t):
        for j in range(4):
            if 0 <= t - j < len(self.items):
                self.stage(j, *self.items[t - j])

    def steps(self):
        return len(self.items) + 3

    def sent(self, g, late):
        for p, (r0, rows, _) in enumerate(PARTS):
            phases = self.plans[p][0]
            count = sum(len(phases[j][1]) for j in ((1, 2) if late else (0,)))
            ref = self.landed.at[g, pl.ds(0, count), pl.ds(r0, rows)]
            pltpu.make_async_copy(ref, ref, self.send_sem.at[g, p, int(late)]).wait()


def backward_kernel(zc, full, mod, cotangent, stream_in, stream_mid, branch, projected, att, hidden, one_t, mixed_t, two_t, act_t,
                    ada, silu_part, selector, keep, gate_sum,
                    owned_down, owned_turned, grad_ada, mod_total, silu_back, kept_grad, table_grad, token_grad,
                    sum_a, sum_b, landed, wbuf, left, left_sib, acts, acts_sib, grad_down, right_sib, bent, rights, grad_mixed,
                    stream, hid, att_buf, spread_grad, grad_in, small,
                    owned_out, lines, line_low, mod_got, mod_flat, ada_wide, ada_low, silu_out, kept_out, table_sum, table_got, token_got, table_mine, rights_out,
                    send, recv, sib_send, sib_recv, wsem, lsem, hsem, asem, ssem, small_send, small_recv, turn_send, turn_recv):
    me = Place(zc)
    me.greet()
    c = me.c
    net = Reduce(me, {2: sum_a, 1: sum_b, 0: sum_a}, landed, {2: owned_down, 1: owned_out.at[1], 0: owned_out.at[0]}, send, recv)
    blocks = Blocks(full, wbuf, wsem, [(2, 0), (2, 1), (2, 2), (2, 3), (1, 0), (1, 1), (1, 2), (1, 3), (0, 3), (0, 0), (0, 1), (0, 2)])
    swaps = []

    def swap(src, dst):
        i = len(swaps)
        swaps.append(pltpu.make_async_remote_copy(
            src_ref=src, dst_ref=dst, send_sem=sib_send.at[i], recv_sem=sib_recv.at[i],
            device_id=me.device(0, 0, 0, 1), device_id_type=MESH))
        swaps[-1].start()
        return swaps[-1]

    def load(src, dst, sem):
        copy = pltpu.make_async_copy(src, dst, sem)
        copy.start()
        return copy

    act_swap = swap(act_t.at[1 - c], acts_sib)
    act_load = load(act_t.at[c], acts, lsem.at[0])
    blocks.fetch(0)
    blocks.fetch(1)
    hid_load = load(hidden.at[0], hid, hsem.at[0])

    def down(rows):
        grad_down[rows, :] = (mod[5:6, :] * cotangent[rows, :].astype(F32)).astype(BF16)
    each_rows(PATCHES, 32, down)
    down_swap = swap(grad_down, right_sib.at[0])
    ada_load = load(ada, ada_wide, lsem.at[4])
    left_loads = [load(ref, left.at[i], lsem.at[1 + i]) for i, ref in enumerate((one_t, mixed_t, two_t))]
    left_swaps = [swap(ref, left_sib.at[i]) for i, ref in enumerate((one_t, mixed_t, two_t))]
    mid_load = load(stream_mid, stream.at[0], ssem.at[0])

    def weight_grad(total, mine, mine_right, theirs, their_right):
        def body(cols):
            v = jnp.dot(mine[...], mine_right[:, cols], preferred_element_type=F32)
            total[:, cols] = (v + jnp.dot(theirs[...], their_right[:, cols], preferred_element_type=F32)).astype(BF16)
        each_columns(body)

    act_load.wait()
    act_swap.wait_recv()
    down_swap.wait_recv()
    for j in range(2):
        weight_grad(sum_a.at[j], acts.at[j], grad_down, acts_sib.at[j], right_sib.at[0])
    net.step(0)
    for b in range(4):
        w = blocks.take(b)
        hid_load.wait()
        def bend(cols):
            v = lax.dot_general(grad_down[...], w[cols, :], NT, preferred_element_type=F32)
            bent[b, :, cols] = (v * gelu_slope(hid[:, cols])).astype(BF16)
        each_columns(bend)
        blocks.fetch(b + 2)
        if b < 3:
            hid_load = load(hidden.at[b + 1], hid, hsem.at[0])
        if b in (1, 3):
            net.step((b + 1) // 2)
    branch_load = load(branch, hid, ssem.at[1])
    bent_swaps = [swap(bent.at[1 - c], right_sib.at[1]), swap(bent.at[3 - c], right_sib.at[2])]
    for copy in left_loads:
        copy.wait()
    for copy in left_swaps + bent_swaps:
        copy.wait_recv()
    for j in range(2):
        weight_grad(sum_b.at[j], left.at[2], bent.at[2 * j + c], left_sib.at[2], right_sib.at[1 + j])
    net.step(3)
    for b in range(4):
        w = blocks.take(4 + b)
        def back(cols):
            v = lax.dot_general(bent[b], w[cols, :], NT, preferred_element_type=F32)
            grad_in[:, cols] = v if b == 0 else grad_in[:, cols] + v
        each_columns(back)
        blocks.fetch(6 + b)
    mid_load.wait()
    branch_load.wait()
    small[...] = jnp.zeros_like(small)

    def norm_back(rows, stream_rows, scale, shift_at, scale_at):
        n, spread = standard(stream_rows)
        e = grad_in[rows, :]
        f = e * (1.0 + scale)
        small[shift_at:shift_at + 1, :] += jnp.sum(e, axis=0, keepdims=True)
        small[scale_at:scale_at + 1, :] += jnp.sum(e * n, axis=0, keepdims=True)
        return (f - jnp.mean(f, axis=-1, keepdims=True) - n * jnp.mean(f * n, axis=-1, keepdims=True)) * spread

    def back_two(rows):
        v = cotangent[rows, :].astype(F32) + norm_back(rows, stream[0, rows, :], mod[4:5, :], 3, 4)
        small[2:3, :] += jnp.sum(v * hid[rows, :], axis=0, keepdims=True)
        hid[rows, :] = v
        rights[3, rows, :] = (mod[2:3, :] * v).astype(BF16)
    each_rows(PATCHES, 32, back_two)
    in_load = load(stream_in, stream.at[0], ssem.at[0])
    net.step(4)
    att_load = load(att.at[0], att_buf.at[0], asem.at[0])
    w = blocks.take(8)
    def mixed_back(cols):
        grad_mixed[:, cols] = lax.dot_general(rights[3], w[cols, :], NT, preferred_element_type=F32).astype(BF16)
    each_columns(mixed_back)
    blocks.fetch(10)
    for b in range(3):
        rights[b] = jnp.zeros((PATCHES, D), BF16)
    net.step(5)
    for head in range(HEADS):
        att_load.wait()
        if head + 1 < HEADS:
            att_load = load(att.at[head + 1], att_buf.at[(head + 1) % 2], asem.at[(head + 1) % 2])
        lanes, mask = window(head)
        weights = att_buf[head % 2]
        low = weights.astype(BF16)
        given = grad_mixed[:, lanes]
        grad_att = lax.dot_general(given * mask.astype(BF16), projected[2, :, lanes], NT, preferred_element_type=F32)
        v = lax.dot_general(low, given, TN, preferred_element_type=F32)
        rights[2, :, lanes] += (v * mask).astype(BF16)
        scores = weights * (grad_att - jnp.sum(weights * grad_att, axis=-1, keepdims=True))
        scores_low = scores.astype(BF16)
        v = jnp.dot(scores_low, projected[1, :, lanes], preferred_element_type=F32) * FACTOR
        rights[0, :, lanes] += (v * mask).astype(BF16)
        v = lax.dot_general(scores_low, projected[0, :, lanes], TN, preferred_element_type=F32) * FACTOR
        rights[1, :, lanes] += (v * mask).astype(BF16)
        rounded = scores_low.astype(F32)
        total = jnp.zeros((GRID, SPAN), F32)
        for r in range(GRID):
            rows = jnp.concatenate([rounded[r * GRID:(r + 1) * GRID], jnp.zeros((GRID, SPAN - PATCHES), F32)], axis=1)
            total += pltpu.roll(rows, (GRID - 1 - r) * GRID, 1)
        spread_grad[:, head, :] = total
        if head in (7, 15):
            net.step(6 + head // 8)
    end_swaps = [swap(rights.at[1 - c], right_sib.at[3]), swap(rights.at[3 - c], right_sib.at[4])]
    net.sent(2, False)
    for copy in end_swaps:
        copy.wait_recv()
    weight_grad(sum_a.at[0], left.at[0], rights.at[c], left_sib.at[0], right_sib.at[3])
    weight_grad(sum_a.at[1], left.at[c], rights.at[2 + c], left_sib.at[c], right_sib.at[4])
    net.step(8)
    net.step(9)
    for b in range(3):
        w = blocks.take(9 + b)
        def back(cols):
            v = lax.dot_general(rights[b], w[cols, :], NT, preferred_element_type=F32)
            grad_in[:, cols] = v if b == 0 else grad_in[:, cols] + v
        each_columns(back)
        blocks.fetch(11 + b)
    in_load.wait()
    def back_one(rows):
        v = norm_back(rows, stream[0, rows, :], mod[1:2, :], 0, 1)
        grad_in[rows, :] = hid[rows, :] + v
    each_rows(PATCHES, 32, back_one)
    for v in range(6):
        for i in range(9):
            piece = small[v:v + 1, i * 128:(i + 1) * 128] if v < 5 else gate_sum[:, i * 128:(i + 1) * 128]
            lines[v * 9 + i:v * 9 + i + 1, :] = piece
    lines[54:64, :] = jnp.zeros((10, 128), F32)
    line_low[...] = lines[...].astype(BF16)
    core_line = me.turned(me.line)
    me.exchange(lambda t: line_low, mod_got.at[core_line], small_send.at[0], small_recv.at[0])
    mod_got[core_line] = line_low[...]
    masked = 1.0 - keep[...].astype(F32)
    token = jnp.sum(masked * grad_in[...], axis=0, keepdims=True)
    for i in range(9):
        lines[i:i + 1, :] = token[:, i * 128:(i + 1) * 128]
    lines[9:16, :] = jnp.zeros((7, 128), F32)
    table_mine[1] = lines[0:16, :]
    me.exchange(lambda t: table_mine.at[1], token_got.at[me.line], small_send.at[3], small_recv.at[3])
    token_got[me.line] = table_mine[1]
    grad_mixed[...] = grad_in[...].astype(BF16)
    def put_back(cols):
        v = lax.dot_general(selector[...], grad_mixed[:, cols], TN, preferred_element_type=F32).astype(BF16)
        kept_out[:, :, cols] = v.reshape(me.count, 8, -1)
    each_columns(put_back)
    me.exchange(lambda t: kept_out.at[t], kept_grad.at[me.line], small_send.at[1], small_recv.at[1])
    kept_own = load(kept_out.at[me.line], kept_grad.at[me.line], ssem.at[1])
    net.step(10)

    picked_rows = row_picker(SPAN)
    table_sum[...] = jnp.zeros_like(table_sum)
    def gather_table(x, carry):
        picker = table_picker(x, 128, SPAN)
        v = (spread_grad[x][:, None, :] * picked_rows[None]).reshape(HEADS * 2 * GRID, SPAN)
        high = v.astype(BF16)
        rest = v - high.astype(F32)
        middle = rest.astype(BF16)
        low = (rest - middle.astype(F32)).astype(BF16)
        for part in (high, middle, low):
            table_sum[...] += lax.dot_general(part, picker, NT, preferred_element_type=F32)
        return carry
    lax.fori_loop(0, GRID, gather_table, 0)
    share = HEADS * 2 * GRID // me.count
    me.exchange(lambda t: table_sum.at[pl.ds(pl.multiple_of(t * share, share), share)], table_got.at[me.line], small_send.at[2], small_recv.at[2])
    table_got[me.line] = table_sum[pl.ds(pl.multiple_of(me.line * share, share), share), :]
    net.step(11)

    me.exchanged(mod_got, small_recv.at[0])
    total = jnp.zeros((64, 128), F32)
    for i in range(me.count):
        total += mod_got[i].astype(F32)
    mod_total[...] = total
    ada_load.wait()
    def flat(j, carry):
        lanes = pl.ds(pl.multiple_of(j * 128, 128), 128)
        ada_low[:, lanes] = ada_wide[:, lanes].astype(BF16)
        return carry
    lax.fori_loop(0, 54, flat, 0)
    for j in range(54):
        mod_flat[:, j * 128:(j + 1) * 128] = mod_got[:, j, :]
    width = ada.shape[0]
    mine = silu_part[:, :width].astype(BF16)
    def outer(j, carry):
        lanes = pl.ds(pl.multiple_of(j * 256, 256), 256)
        grad_ada[:, lanes] = lax.dot_general(mine, mod_flat[:, lanes], TN, preferred_element_type=F32)
        return carry
    lax.fori_loop(0, 27, outer, 0)
    back_silu = lax.dot_general(mod_flat[...], ada_low[...], NT, preferred_element_type=F32)
    silu_out[...] = jnp.zeros_like(silu_out)
    silu_out[:, 0:1, 0:width] = back_silu[:, None, :]
    me.exchange(lambda t: silu_out.at[me.turned(t)], silu_back.at[me.line], small_send.at[4], small_recv.at[4])
    silu_back[me.line] = silu_out[core_line]
    me.exchanged(table_got, small_recv.at[2])
    total = table_got[0]
    for i in range(1, me.count):
        total += table_got[i]
    table_mine[0] = total
    me.exchange(lambda t: table_mine.at[0], table_grad.at[me.line], small_send.at[5], small_recv.at[5])
    table_grad[me.line] = total
    net.step(12)
    turns = []

    def turn_rows(g):
        for n in range(4):
            rights_out[n, g] = owned_out[g, n * width:(n + 1) * width, :].astype(BF16)
        for k in range(1, 4):
            n = (me.x * 2 + me.c + k) % 4
            copy = pltpu.make_async_remote_copy(
                src_ref=rights_out.at[n, g], dst_ref=owned_turned.at[me.x * 2 + me.c, g], send_sem=turn_send.at[g, k - 1], recv_sem=turn_recv.at[g, k - 1],
                device_id=(me.line // 4, n), device_id_type=MESH)
            copy.start()
            turns.append(copy)
        owned_turned[me.x * 2 + me.c, g] = rights_out[me.x * 2 + me.c, g]

    turn_rows(1)
    net.step(13)
    me.exchanged(token_got, small_recv.at[3])
    total = token_got[0]
    for i in range(1, me.count):
        total += token_got[i]
    token_grad[...] = total
    net.step(14)
    turn_rows(0)
    net.sent(1, False)
    net.sent(0, False)
    for g in range(3):
        net.sent(g, True)
    for copy in swaps:
        copy.wait_send()
    kept_own.wait()
    me.exchanged(kept_grad, small_recv.at[1])
    me.exchanged(silu_back, small_recv.at[4])
    me.exchanged(table_grad, small_recv.at[5])
    for i, got in enumerate((mod_got, kept_grad, table_got, token_got, silu_back, table_grad)):
        me.exchanged(got, small_send.at[i])
    for copy in turns:
        copy.wait()


def run_backward(full, mod, cotangent, stream_in, stream_mid, branch, projected, att, hidden, one_t, mixed_t, two_t, act_t,
                 ada, silu_part, selector, keep, gate_sum, zc):
    vmem = pl.BlockSpec(memory_space=pltpu.VMEM)
    hbm = pl.BlockSpec(memory_space=pl.ANY)
    parts, count, width = len(PARTS), 8 * zc, ada.shape[0]
    share = HEADS * 2 * GRID // count
    shape = jax.ShapeDtypeStruct
    dma = pltpu.SemaphoreType.DMA
    return pl.pallas_call(
        functools.partial(backward_kernel, zc),
        out_shape=(shape((ROWS, D), F32), shape((4, 2, width, D), BF16), shape((width, 6 * D), F32), shape((64, 128), F32),
                   shape((count, 8, 128), F32), shape((count, 8, D), BF16), shape((count, share, 128), F32), shape((16, 128), F32)),
        in_specs=[hbm, vmem, vmem, hbm, hbm, hbm, vmem, hbm, hbm, hbm, hbm, hbm, hbm, hbm, vmem, vmem, vmem, vmem],
        out_specs=(vmem, vmem, vmem, vmem, vmem, hbm, vmem, vmem),
        scratch_shapes=[
            pltpu.VMEM((2, D, D), BF16), pltpu.VMEM((2, D, D), BF16), pltpu.VMEM((3, 4 * zc - 1, ROWS, D), BF16),
            pltpu.VMEM((2, D, D), BF16), pltpu.VMEM((3, D, PATCHES), BF16), pltpu.VMEM((3, D, PATCHES), BF16),
            pltpu.VMEM((2, D, PATCHES), BF16), pltpu.VMEM((2, D, PATCHES), BF16), pltpu.VMEM((PATCHES, D), BF16),
            pltpu.VMEM((5, PATCHES, D), BF16), pltpu.VMEM((4, PATCHES, D), BF16), pltpu.VMEM((4, PATCHES, D), BF16),
            pltpu.VMEM((PATCHES, D), BF16), pltpu.VMEM((1, PATCHES, D), F32), pltpu.VMEM((PATCHES, D), F32),
            pltpu.VMEM((2, PATCHES, PATCHES), F32),
            pltpu.VMEM((GRID, HEADS, SPAN), F32), pltpu.VMEM((PATCHES, D), F32), pltpu.VMEM((8, D), F32),
            pltpu.VMEM((2, ROWS, D), F32), pltpu.VMEM((64, 128), F32), pltpu.VMEM((64, 128), BF16), pltpu.VMEM((count, 64, 128), BF16),
            pltpu.VMEM((count, 6 * D), BF16), pltpu.VMEM((width, 6 * D), F32), pltpu.VMEM((width, 6 * D), BF16), pltpu.VMEM((count, 8, 128), F32),
            pltpu.VMEM((count, 8, D), BF16), pltpu.VMEM((HEADS * 2 * GRID, 128), F32), pltpu.VMEM((count, share, 128), F32),
            pltpu.VMEM((count, 16, 128), F32), pltpu.VMEM((2, 16, 128), F32), pltpu.VMEM((4, 2, width, D), BF16),
            dma((3, parts, 2)), dma((3, parts, 4 * zc - 1)), dma((9,)), dma((9,)), dma((2,)), dma((5,)), dma((1,)), dma((2,)), dma((2,)),
            dma((6,)), dma((6,)), dma((2, 3)), dma((2, 3))],
        compiler_params=pltpu.CompilerParams(collective_id=2, has_side_effects=True, vmem_limit_bytes=63 * 1024 * 1024),
        name="backward",
    )(full, mod, cotangent, stream_in, stream_mid, branch, projected, att, hidden, one_t, mixed_t, two_t, act_t,
      ada, silu_part, selector, keep, gate_sum)


AXES = ("wide", "narrow")


def running_rank(keep_flat):
    count = keep_flat.shape[0]
    lower = (lax.broadcasted_iota(jnp.int32, (count, count), 0) >= lax.broadcasted_iota(jnp.int32, (count, count), 1))
    total = jnp.dot(lower.astype(jnp.bfloat16), keep_flat.astype(jnp.bfloat16)[:, None], preferred_element_type=jnp.float32)
    return total[:, 0].astype(jnp.int32) - 1


def per_device_plain(kept_tokens, keep_mask, conditioning, ada_weight, ada_bias, qkv_weight, out_weight, up_weight, down_weight, position_bias, mask_token, cotangent):
    wide_count = lax.axis_size("wide")
    narrow_count = lax.axis_size("narrow")
    devices = wide_count * narrow_count
    slots = kept_tokens.shape[2]
    images = conditioning.shape[0]
    count = images * PATCHES
    rows = qkv_weight.shape[0]
    me = lax.axis_index(AXES)
    factor = 1.0 / math.sqrt(HEAD_DIM)
    low_type = jnp.bfloat16
    wide_type = jnp.float32
    silu_cond = jax.nn.silu(conditioning).astype(low_type)
    small = jnp.concatenate([silu_cond.reshape(-1), ada_bias.astype(low_type), mask_token.astype(low_type)])
    smalls = lax.all_gather(small, AXES, axis=0, tiled=False)
    silu_all = smalls[:, : images * D].reshape(devices * images, D)
    bias_full = smalls[:, images * D : images * D + ada_bias.shape[0]].reshape(-1)
    token_full = smalls[:, images * D + ada_bias.shape[0] :].reshape(-1)
    ada_low = ada_weight.astype(low_type)
    silu_part = lax.dynamic_slice_in_dim(silu_all, me * rows, rows, axis=1)
    mod_part = jnp.dot(silu_part, ada_low, preferred_element_type=wide_type)
    mod_parts = lax.all_to_all(mod_part.reshape(devices, images, 6 * D), AXES, split_axis=0, concat_axis=0, tiled=True)
    modulation = jnp.sum(mod_parts, axis=0) + bias_full.astype(wide_type)[None, :]
    qkv_full = lax.all_gather(qkv_weight.astype(low_type), AXES, axis=0, tiled=True)
    out_full = lax.all_gather(out_weight.astype(low_type), AXES, axis=0, tiled=True)
    up_full = lax.all_gather(up_weight.astype(low_type), AXES, axis=0, tiled=True)
    down_full = lax.all_gather(down_weight.astype(low_type), AXES, axis=0, tiled=True)
    def times_qkv(v):
        return jnp.dot(v, qkv_full, preferred_element_type=wide_type)
    def times_qkv_back(v):
        return jnp.dot(v, qkv_full.T, preferred_element_type=wide_type)
    def times_up(v):
        return jnp.dot(v, up_full, preferred_element_type=wide_type)
    def times_up_back(v):
        return jnp.dot(v, up_full.T, preferred_element_type=wide_type)
    arrived = lax.all_to_all(kept_tokens, AXES, split_axis=1, concat_axis=0, tiled=True)
    received = arrived.reshape(devices * slots, D)
    keep_flat = keep_mask.reshape(count)
    keep_float = keep_flat.astype(wide_type)
    ranks = running_rank(keep_flat)
    target = ranks % devices * slots + ranks // devices
    columns = jnp.arange(devices * slots, dtype=jnp.int32)
    selector = jnp.where((keep_flat[:, None] == 1) & (target[:, None] == columns[None, :]), 1.0, 0.0).astype(wide_type)
    stream_in = jnp.dot(selector.astype(low_type), received, preferred_element_type=wide_type)
    stream_in = stream_in + (1.0 - keep_float)[:, None] * token_full.astype(wide_type)[None, :]
    stream_in = stream_in.reshape(images, PATCHES, D)
    shift_one, scale_one, gate_one, shift_two, scale_two, gate_two = jnp.split(
        modulation[:, None, :], 6, axis=-1
    )
    normed_one = modulate(stream_in, shift_one, scale_one).astype(low_type).reshape(count, D)
    projected = times_qkv(normed_one).astype(low_type)
    projected = projected.reshape(images, PATCHES, 3, HEADS, HEAD_DIM)
    queries = projected[:, :, 0]
    key_rows = projected[:, :, 1]
    value_rows = projected[:, :, 2]
    relative = expand_bias(position_bias, GRID)
    scores = (
        jnp.einsum("iqhd,ikhd->ihqk", queries, key_rows, preferred_element_type=wide_type) * factor
        + relative[None]
    )
    att_weights = jax.nn.softmax(scores, axis=-1)
    att_low = att_weights.astype(low_type)
    mixed = (
        jnp.einsum("ihqk,ikhd->iqhd", att_low, value_rows, preferred_element_type=wide_type)
        .astype(low_type)
        .reshape(count, D)
    )
    branch = jnp.dot(mixed, out_full, preferred_element_type=wide_type).reshape(images, PATCHES, D)
    stream_mid = stream_in + gate_one * branch
    normed_two = modulate(stream_mid, shift_two, scale_two).astype(low_type).reshape(count, D)
    hidden = times_up(normed_two)
    activated = gelu_tanh(hidden).astype(low_type)
    down = jnp.dot(activated, down_full, preferred_element_type=wide_type).reshape(
        images, PATCHES, D
    )
    block_out = (stream_mid + gate_two * down).reshape(count, D).astype(low_type)
    incoming = cotangent.astype(wide_type).reshape(images, PATCHES, D)
    grad_gate_two = jnp.sum(incoming * down, axis=1)
    grad_down = (gate_two * incoming).astype(low_type).reshape(count, D)
    grad_activated = jnp.dot(grad_down, down_full.T, preferred_element_type=wide_type)
    _, gelu_pull = jax.vjp(gelu_tanh, hidden)
    grad_hidden = gelu_pull(grad_activated)[0].astype(low_type)
    grad_normed_two = times_up_back(grad_hidden).reshape(
        images, PATCHES, D
    )
    _, norm_pull_two = jax.vjp(modulate, stream_mid, shift_two, scale_two)
    grad_mid_norm, grad_shift_two, grad_scale_two = norm_pull_two(grad_normed_two)
    grad_mid = incoming + grad_mid_norm
    grad_gate_one = jnp.sum(grad_mid * branch, axis=1)
    grad_branch = (gate_one * grad_mid).astype(low_type).reshape(count, D)
    grad_mixed = jnp.dot(grad_branch, out_full.T, preferred_element_type=wide_type).astype(low_type)
    grad_mixed = grad_mixed.reshape(images, PATCHES, HEADS, HEAD_DIM)
    grad_att = jnp.einsum(
        "iqhd,ikhd->ihqk", grad_mixed, value_rows, preferred_element_type=wide_type
    )
    grad_values = jnp.einsum(
        "ihqk,iqhd->ikhd", att_low, grad_mixed, preferred_element_type=wide_type
    )
    grad_scores = (
        att_weights * (grad_att - jnp.sum(att_weights * grad_att, axis=-1, keepdims=True))
    ).astype(low_type)
    grad_queries = (
        jnp.einsum("ihqk,ikhd->iqhd", grad_scores, key_rows, preferred_element_type=wide_type)
        * factor
    )
    grad_keys = (
        jnp.einsum("ihqk,iqhd->ikhd", grad_scores, queries, preferred_element_type=wide_type)
        * factor
    )
    grad_table = bias_adjoint(jnp.sum(grad_scores.astype(wide_type), axis=0), GRID)
    grad_projected = (
        jnp.stack([grad_queries, grad_keys, grad_values], axis=2)
        .astype(low_type)
        .reshape(count, 3 * D)
    )
    grad_normed_one = times_qkv_back(grad_projected).reshape(
        images, PATCHES, D
    )
    _, norm_pull_one = jax.vjp(modulate, stream_in, shift_one, scale_one)
    grad_in_norm, grad_shift_one, grad_scale_one = norm_pull_one(grad_normed_one)
    grad_in = (grad_mid + grad_in_norm).reshape(count, D)
    grad_modulation = jnp.concatenate(
        [
            grad_shift_one[:, 0],
            grad_scale_one[:, 0],
            grad_gate_one,
            grad_shift_two[:, 0],
            grad_scale_two[:, 0],
            grad_gate_two,
        ],
        axis=-1,
    ).astype(low_type)
    grad_mod_all = lax.all_gather(grad_modulation, AXES, axis=0, tiled=True)
    grad_ada = lax.dot_general(silu_part, grad_mod_all, (((0,), (0,)), ((), ())), preferred_element_type=wide_type)
    bias_share = 6 * D // devices
    sum_bias = jnp.sum(lax.dynamic_slice_in_dim(grad_mod_all, me * bias_share, bias_share, axis=1).astype(wide_type), axis=0)
    silu_parts = lax.dot_general(grad_mod_all, ada_low, (((1,), (1,)), ((), ())), preferred_element_type=wide_type)
    silu_parts = lax.all_to_all(silu_parts.reshape(devices, images, rows), AXES, split_axis=0, concat_axis=0, tiled=True)
    grad_silu = silu_parts.transpose(1, 0, 2).reshape(images, D)
    _, silu_pull = jax.vjp(jax.nn.silu, conditioning)
    grad_cond = silu_pull(grad_silu)[0]
    grad_mask = jnp.sum((1.0 - keep_float)[:, None] * grad_in, axis=0)
    grad_received = jnp.dot(
        selector.T, grad_in, precision=lax.Precision.HIGHEST, preferred_element_type=wide_type
    ).astype(low_type)
    grad_kept = lax.all_to_all(
        grad_received.reshape(devices, 1, slots, D),
        ("wide", "narrow"),
        split_axis=0,
        concat_axis=1,
        tiled=True,
    )
    def scatter(left, right):
        partial = lax.dot_general(left, right, (((0,), (0,)), ((), ())), preferred_element_type=wide_type)
        return lax.psum_scatter(partial.reshape(-1), AXES, scatter_dimension=0, tiled=True).reshape(-1, right.shape[1])
    sum_qkv = scatter(normed_one, grad_projected)
    sum_out = scatter(mixed, grad_branch)
    sum_up = scatter(normed_two, grad_hidden)
    sum_down = scatter(activated, grad_down)
    grad_table_all, mask_whole = lax.psum((grad_table, grad_mask), AXES)
    mask_share = D // devices
    sum_mask = lax.dynamic_slice_in_dim(mask_whole, me * mask_share, mask_share)
    return (block_out, grad_kept, grad_cond, grad_ada, sum_bias, sum_qkv, sum_out, sum_up, sum_down, grad_table_all, sum_mask)


def rounded(v):
    return lax.reduce_precision(v, 8, 7)


def per_device(kept_tokens, keep_mask, conditioning, ada_weight, ada_bias, qkv_weight, out_weight, up_weight, down_weight, position_bias, mask_token, cotangent):
    if kept_tokens.shape[2] > 8 or conditioning.shape[0] != 1:
        return per_device_plain(kept_tokens, keep_mask, conditioning, ada_weight, ada_bias, qkv_weight, out_weight, up_weight, down_weight, position_bias, mask_token, cotangent)
    wide_count = lax.axis_size("wide")
    devices = wide_count * lax.axis_size("narrow")
    slots = kept_tokens.shape[2]
    rows = qkv_weight.shape[0]
    share = ada_bias.shape[0]
    me = lax.axis_index(AXES)
    zc = wide_count // 2
    attn_src = jnp.concatenate([qkv_weight.reshape(rows, 3, D), out_weight.reshape(rows, 1, D)], axis=1)
    both = jnp.stack([attn_src, up_weight.reshape(rows, 4, D)], axis=0).astype(BF16)
    turned = lax.all_to_all(both.transpose(2, 0, 1, 3), "narrow", split_axis=0, concat_axis=0, tiled=True)
    turned = turned.transpose(1, 0, 2, 3).reshape(2, ROWS, D)
    source = jnp.concatenate([turned, down_weight.astype(BF16)[None]], axis=0)

    silu_out = jnp.pad(rounded(jax.nn.silu(conditioning)).reshape(devices, 1, rows), ((0, 0), (0, 7), (0, 128 - rows)))
    bias_row = lax.dynamic_update_slice(jnp.zeros((1, 6 * D), F32), rounded(ada_bias)[None], (0, me * share))
    token_row = lax.dynamic_update_slice(jnp.zeros((1, D), F32), rounded(mask_token)[None], (0, me * rows))
    kept = jnp.pad(kept_tokens.reshape(devices, slots, D), ((0, 0), (0, 8 - slots), (0, 0)))
    table = jnp.pad(position_bias, ((0, 0), (0, 1), (0, 128 - position_bias.shape[2]))).reshape(HEADS * 2 * GRID, 128)
    keep = keep_mask.reshape(PATCHES, 1)
    keep_float = keep.astype(F32)

    (full, block_out, one_t, projected, att, mixed_t, branch, stream_mid, two_t, hidden, act_t, stream_in, mod, silu_part, selector, gate_sum) = run_forward(
        source, silu_out, ada_weight, bias_row, token_row, kept, keep, table, cotangent, zc)
    sum_down, turned, grad_ada, mod_total, silu_back, kept_grad, table_grad, token_grad = run_backward(
        full, mod, cotangent, stream_in, stream_mid, branch, projected, att, hidden, one_t, mixed_t, two_t, act_t,
        ada_weight, silu_part, selector, keep, gate_sum, zc)

    sum_bias = lax.dynamic_slice(mod_total[:54].reshape(-1), (me * share,), (share,))
    sum_mask = lax.dynamic_slice(token_grad[:9].reshape(-1), (me * rows,), (rows,))
    _, silu_pull = jax.vjp(jax.nn.silu, conditioning)
    grad_cond = silu_pull(silu_back[:, 0, :rows].reshape(1, D))[0]
    grad_kept = kept_grad[None, :, :slots]
    offsets = position_bias.shape[2]
    grad_table = table_grad.reshape(HEADS, 2 * GRID, 128)[:, :offsets, :offsets]
    sum_qkv = turned[:3, 0].transpose(1, 0, 2).reshape(rows, 3 * D).astype(F32)
    sum_out = turned[3, 0].astype(F32)
    sum_up = turned[:, 1].transpose(1, 0, 2).reshape(rows, FF).astype(F32)
    return (block_out, grad_kept, grad_cond, grad_ada, sum_bias, sum_qkv, sum_out, sum_up, sum_down, grad_table, sum_mask)


def solution(mesh):
    in_specs = (
        P(("wide", "narrow"), None, None, None),
        P(("wide", "narrow"), None),
        P(("wide", "narrow"), None),
        P(("wide", "narrow"), None),
        P(("wide", "narrow")),
        P(("wide", "narrow"), None),
        P(("wide", "narrow"), None),
        P(("wide", "narrow"), None),
        P(("wide", "narrow"), None),
        P(),
        P(("wide", "narrow")),
        P(("wide", "narrow"), None),
    )
    out_specs = (
        P(("wide", "narrow"), None),
        P(("wide", "narrow"), None, None, None),
        P(("wide", "narrow"), None),
        P(("wide", "narrow"), None),
        P(("wide", "narrow")),
        P(("wide", "narrow"), None),
        P(("wide", "narrow"), None),
        P(("wide", "narrow"), None),
        P(("wide", "narrow"), None),
        P(),
        P(("wide", "narrow")),
    )
    shape = dict(mesh.shape)
    rows = D // (shape["wide"] * shape["narrow"])
    fast = shape["narrow"] == 4 and shape["wide"] % 2 == 0 and rows * 4 == ROWS
    return jax.shard_map(
        per_device if fast else per_device_plain, mesh=mesh, in_specs=in_specs, out_specs=out_specs, check_vma=False
    )
```

```python
import functools
import math

import jax
import jax.numpy as jnp
from jax import lax
from jax.experimental import pallas as pl
from jax.experimental.pallas import tpu as pltpu
from jax.sharding import PartitionSpec as P

D = 1152
HEADS = 16
HEAD_DIM = 72
FF = 4608
GRID = 16
PATCHES = 256


EPSILON = 1e-06


def layer_norm(stream):
    center = stream - jnp.mean(stream, axis=-1, keepdims=True)
    variance = jnp.mean(center * center, axis=-1, keepdims=True)
    return center * lax.rsqrt(variance + EPSILON)


def modulate(stream, shift, scale):
    return layer_norm(stream) * (1.0 + scale) + shift


def offset_picker(grid):
    places = jnp.arange(grid, dtype=jnp.int32)
    spread = jnp.arange(2 * grid - 1, dtype=jnp.int32)
    return (
        places[:, None, None] - places[None, :, None] + grid - 1 == spread[None, None, :]
    ).astype(jnp.float32)


def expand_bias(table, grid):
    picker = offset_picker(grid)
    partial_rows = jnp.einsum("yka,had->hykd", picker, table, precision=lax.Precision.HIGHEST)
    expanded = jnp.einsum("hykd,xjd->hyxkj", partial_rows, picker, precision=lax.Precision.HIGHEST)
    return expanded.reshape(table.shape[0], grid * grid, grid * grid)


def bias_adjoint(grad_bias, grid):
    picker = offset_picker(grid)
    shaped = grad_bias.reshape(grad_bias.shape[0], grid, grid, grid, grid)
    partial_rows = jnp.einsum("hyxkj,xjd->hykd", shaped, picker, precision=lax.Precision.HIGHEST)
    return jnp.einsum("hykd,yka->had", partial_rows, picker, precision=lax.Precision.HIGHEST)


def gelu_tanh(value):
    return jax.nn.gelu(value, approximate=True)


MESH = pl.DeviceIdType.MESH
ROWS = 144
PARTS = (
    ((0, 80, "zxy"), (80, 64, "zyx")),
    ((0, 64, "zxy"), (64, 48, "zyx"), (112, 32, "xyz")),
    ((0, 64, "zxy"), (64, 64, "zyx"), (128, 16, "xyz")),
)
AT = {"z": 0, "y": 1, "x": 2}
F32 = jnp.float32
BF16 = jnp.bfloat16
FACTOR = 1.0 / math.sqrt(HEAD_DIM)
NT = (((1,), (1,)), ((), ()))
TN = (((0,), (0,)), ((), ()))
SPAN = 2 * PATCHES


def rels(zc):
    return [(rz, ry, rx) for rz in range(zc) for ry in range(2) for rx in range(2)]


class Place:
    def __init__(self, zc):
        wide = lax.axis_index("wide")
        narrow = lax.axis_index("narrow")
        self.zc, self.wcount = zc, 2 * zc
        self.line, self.count = wide * 4 + narrow, 8 * zc
        self.z, self.y, self.x, self.c = wide // 2, wide % 2, narrow // 2, narrow % 2
        self.hops = {"z": [(k, 0, 0) for k in range(1, zc)], "y": [(0, 1, 0)], "x": [(0, 0, 1)]}

    def shifted(self, rz, ry, rx):
        w = lax.rem(self.z + rz, self.zc) * 2 + (self.y + ry) % 2
        return w, (self.x + rx) % 2

    def device(self, rz, ry, rx, flip=0):
        w, x = self.shifted(rz, ry, rx)
        return w, x * 2 + (self.c + flip) % 2

    def greet(self):
        barrier = pltpu.get_barrier_semaphore()
        def hello(k, carry):
            t = lax.rem(self.line + k, self.count)
            pl.semaphore_signal(barrier, inc=1, device_id=(t // 4, t % 4), device_id_type=MESH)
            return carry
        lax.fori_loop(1, self.count, hello, 0)
        pl.semaphore_wait(barrier, self.count - 1)

    def turned(self, t):
        return t % 2 * (self.count // 2) + t // 2

    def exchange(self, piece, there, send, recv):
        def go(k, carry):
            t = lax.rem(self.line + k, self.count)
            pltpu.make_async_remote_copy(
                src_ref=piece(t), dst_ref=there, send_sem=send, recv_sem=recv,
                device_id=(t // 4, t % 4), device_id_type=MESH).start()
            return carry
        lax.fori_loop(1, self.count, go, 0)

    def exchange_chips(self, piece, there, send, recv):
        def go(k, carry):
            t = lax.rem(self.line + 2 * k, self.count)
            pltpu.make_async_remote_copy(
                src_ref=piece(t // 2), dst_ref=there, send_sem=send, recv_sem=recv,
                device_id=(t // 4, t % 4), device_id_type=MESH).start()
            return carry
        lax.fori_loop(1, self.count // 2, go, 0)

    def exchanged(self, got, sem):
        others = got.at[pl.ds(0, got.shape[0] - 1)]
        pltpu.make_async_copy(others, others, sem).wait()


def wait_rows(ref, total, sem):
    for blocks in range(1, ref.shape[0] + 1):
        if total % (blocks * 16) == 0 and total // blocks <= ref.shape[1]:
            some = ref.at[pl.ds(0, blocks), pl.ds(0, total // blocks)]
            pltpu.make_async_copy(some, some, sem).wait()
            return
    raise ValueError("rows")


def each_rows(total, step, body):
    def go(i, carry):
        body(pl.ds(pl.multiple_of(i * step, step), step))
        return carry
    lax.fori_loop(0, total // step, go, 0)


def each_columns(body):
    def go(i, carry):
        body(pl.ds(pl.multiple_of(i * 256, 256), 256))
        return carry
    lax.fori_loop(0, 4, go, 0)
    body(pl.ds(1024, 128))


def window(head):
    low = head * HEAD_DIM
    first, last = low // 128 * 128, -(-(low + HEAD_DIM) // 128) * 128
    lane = lax.broadcasted_iota(jnp.int32, (1, last - first), 1) + first
    mask = jnp.where((lane >= low) & (lane < low + HEAD_DIM), 1.0, 0.0).astype(F32)
    return slice(first, last), mask


class Gather:
    def __init__(self, me, src, out, sems):
        self.me, self.src, self.out = me, src, out
        self.send, self.recv, self.sib_send, self.sib_recv, self.own = sems
        self.all = rels(me.zc)
        self.index = {r: i for i, r in enumerate(self.all)}

    def block(self, g, rel, r0, rows):
        w, x = self.me.shifted(self.me.zc - rel[0], rel[1], rel[2])
        n = x * 2 + self.me.c
        b, row = (n, w * ROWS) if g < 2 else ((w * 4 + n) // self.me.wcount, lax.rem(w * 4 + n, self.me.wcount) * ROWS)
        return self.out.at[g, b, pl.ds(pl.multiple_of(row + r0, 16), rows)]

    def forward(self, g, p, rel):
        r0, rows, order = PARTS[g][p]
        at = max([i for i, d in enumerate(order) if rel[AT[d]]], default=-1)
        there = self.block(g, rel, r0, rows)
        here = there if any(rel) else self.src.at[g, pl.ds(r0, rows)]
        for d in order[at + 1:]:
            for h in self.me.hops[d]:
                seen = ((rel[0] + h[0]) % self.me.zc, (rel[1] + h[1]) % 2, (rel[2] + h[2]) % 2)
                pltpu.make_async_remote_copy(
                    src_ref=here, dst_ref=there, send_sem=self.send.at[g, p], recv_sem=self.recv.at[g, p, self.index[seen]],
                    device_id=self.me.device(*h), device_id_type=MESH).start()
        pltpu.make_async_remote_copy(
            src_ref=here, dst_ref=there, send_sem=self.sib_send.at[g, p], recv_sem=self.sib_recv.at[g, p, rel[0]],
            device_id=self.me.device(0, 0, 0, 1), device_id_type=MESH).start()

    def begin(self, g):
        for p in range(len(PARTS[g])):
            self.forward(g, p, (0, 0, 0))
        pltpu.make_async_copy(self.src.at[g], self.block(g, (0, 0, 0), 0, ROWS), self.own.at[g]).start()

    def ticks(self, g):
        soon, late = [], []
        for deep in (1, 2, 3):
            for rel in self.all:
                if sum(1 for v in rel if v) == deep:
                    now = [p for p, part in enumerate(PARTS[g]) if part[2][-1] != "z" or not rel[0]]
                    if now:
                        soon.append(functools.partial(self.tick, g, rel, now))
                    if len(now) < len(PARTS[g]):
                        late.append(functools.partial(self.tick, g, rel, [p for p in range(len(PARTS[g])) if p not in now]))
        return soon, late

    def tick(self, g, rel, parts):
        for p in parts:
            wait_rows(self.out.at[g], PARTS[g][p][1], self.recv.at[g, p, self.index[rel]])
            self.forward(g, p, rel)

    def arrived(self, g, levels):
        if 0 in levels:
            pltpu.make_async_copy(self.src.at[g], self.src.at[g], self.own.at[g]).wait()
        for p, (r0, rows, _) in enumerate(PARTS[g]):
            for rz in levels:
                wait_rows(self.out.at[g], 4 * rows, self.sib_recv.at[g, p, rz])

    def finish(self, g):
        for p, (r0, rows, _) in enumerate(PARTS[g]):
            wait_rows(self.out.at[g], (4 * self.me.zc - 1) * rows, self.send.at[g, p])
            wait_rows(self.out.at[g], 4 * self.me.zc * rows, self.sib_send.at[g, p])


class Blocks:
    def __init__(self, full, buf, sems, order):
        self.full, self.buf, self.sems, self.order = full, buf, sems, order

    def fetch(self, i):
        if i < len(self.order):
            g, b = self.order[i]
            pltpu.make_async_copy(self.full.at[g, b], self.buf.at[i % 2], self.sems.at[i % 2]).start()

    def take(self, i):
        g, b = self.order[i]
        pltpu.make_async_copy(self.full.at[g, b], self.buf.at[i % 2], self.sems.at[i % 2]).wait()
        return self.buf.at[i % 2]


def standard(v):
    center = v - jnp.mean(v, axis=-1, keepdims=True)
    spread = lax.rsqrt(jnp.mean(center * center, axis=-1, keepdims=True) + EPSILON)
    return center * spread, spread


def gelu(v):
    return 0.5 * v * (1.0 + jnp.tanh(0.7978845608 * (v + 0.044715 * v * v * v)))


def gelu_slope(v):
    t = jnp.tanh(0.7978845608 * (v + 0.044715 * v * v * v))
    return 0.5 * (1.0 + t) + 0.5 * v * (1.0 - t * t) * 0.7978845608 * (1.0 + 3.0 * 0.044715 * v * v)


def turn(ref, out):
    def body(cols):
        out[cols, :] = ref[:, cols].astype(F32).T.astype(BF16)
    each_columns(body)


def table_picker(x, entries, line):
    entry = lax.broadcasted_iota(jnp.int32, (entries, line), 0) % 128
    lane = lax.broadcasted_iota(jnp.int32, (entries, line), 1)
    return jnp.where(entry == x - lane % GRID + GRID - 1, 1.0, 0.0).astype(BF16)


def row_picker(line):
    row = lax.broadcasted_iota(jnp.int32, (2 * GRID, line), 0)
    lane = lax.broadcasted_iota(jnp.int32, (2 * GRID, line), 1)
    return jnp.where(row == 2 * GRID - 2 - lane // GRID, 1.0, 0.0).astype(F32)


def forward_kernel(zc, src, silu_out, ada, bias_row, token_row, kept, keep, table, cotangent,
                   full, one_t_out, projected_out, att_out, mixed_t_out, branch_out, stream_mid_out, two_t_out, hidden_out, act_t_out, stream_in_out,
                   block_out, mod, silu_part, selector, gate_sum,
                   one_t, projected, att, mixed_t, branch, stream_mid, two_t, hidden, act_t, stream_in, save_sem,
                   wbuf, normed, wide_one, act, turned, silu_got, mod_rows, mod_sib, mod_got, kept_got, spread_bias,
                   send, recv, sib_send, sib_recv, own, wsem, small_send, small_recv):
    me = Place(zc)
    me.greet()
    net = Gather(me, src, full, (send, recv, sib_send, sib_recv, own))
    blocks = Blocks(full, wbuf, wsem, [(0, 0), (0, 1), (0, 2), (0, 3), (1, 0), (1, 1), (1, 2), (1, 3)])
    saves = []

    def save(here, there):
        copy = pltpu.make_async_copy(here, there, save_sem.at[len(saves)])
        copy.start()
        saves.append(copy)

    core_line = me.turned(me.line)
    me.exchange(lambda t: silu_out.at[t], silu_got.at[core_line], small_send.at[0], small_recv.at[0])
    net.begin(0)
    me.exchange(lambda t: kept.at[t], kept_got.at[me.line], small_send.at[1], small_recv.at[1])
    silu_got[core_line] = silu_out[me.line]
    kept_got[me.line] = kept[me.line]
    ticks, _ = net.ticks(0)

    me.exchanged(silu_got, small_recv.at[0])
    silu_part[...] = silu_got[:, 0, :]
    mine = silu_part[:, : ada.shape[0]].astype(BF16)
    def mod_column(j, carry):
        lanes = pl.ds(pl.multiple_of(j * 128, 128), 128)
        v = jnp.dot(mine, ada[:, lanes].astype(BF16), preferred_element_type=F32) + bias_row[:, lanes]
        mod_rows[:, pl.ds(j, 1), :] = v[:, None, :]
        return carry
    lax.fori_loop(0, 54, mod_column, 0)
    def token_column(j, carry):
        v = jnp.broadcast_to(token_row[:, pl.ds(pl.multiple_of(j * 128, 128), 128)], (me.count, 128))
        mod_rows[:, pl.ds(54 + j, 1), :] = v[:, None, :]
        return carry
    lax.fori_loop(0, 9, token_column, 0)
    mod_rows[:, 63:64, :] = jnp.zeros((me.count, 1, 128), F32)
    half = me.count // 2
    chip = me.line // 2
    mod_swap = pltpu.make_async_remote_copy(
        src_ref=mod_rows.at[pl.ds((1 - me.c) * half, half)], dst_ref=mod_sib, send_sem=small_send.at[3], recv_sem=small_recv.at[3],
        device_id=me.device(0, 0, 0, 1), device_id_type=MESH)
    mod_swap.start()
    for _ in range(3):
        ticks.pop(0)()
    mod_swap.wait()
    def both(i, carry):
        mod_sib[i] += mod_rows[me.c * half + i]
        return carry
    lax.fori_loop(0, half, both, 0)
    me.exchange_chips(lambda t: mod_sib.at[t], mod_got.at[chip], small_send.at[2], small_recv.at[2])
    mod_got[chip] = mod_sib[chip]
    for _ in range(2):
        ticks.pop(0)()

    v = table[...]
    high = v.astype(BF16)
    rest = v - high.astype(F32)
    middle = rest.astype(BF16)
    halves = jnp.concatenate([high, middle, (rest - middle.astype(F32)).astype(BF16)], axis=1)
    picked_rows = row_picker(SPAN)
    def spread(x, carry):
        got = jnp.dot(halves, table_picker(x, 384, SPAN), preferred_element_type=F32)
        spread_bias[x] = jnp.sum(got.reshape(HEADS, 2 * GRID, SPAN) * picked_rows[None], axis=1)
        return carry
    lax.fori_loop(0, GRID // 2, spread, 0)
    for _ in range(4):
        ticks.pop(0)()
    lax.fori_loop(GRID // 2, GRID, spread, 0)

    row = lax.broadcasted_iota(jnp.int32, (PATCHES, PATCHES), 0)
    column = lax.broadcasted_iota(jnp.int32, (PATCHES, PATCHES), 1)
    kept_here = keep[...].astype(F32)
    before = jnp.where(row >= column, 1.0, 0.0).astype(BF16)
    ranks = jnp.dot(before, jnp.broadcast_to(kept_here, (PATCHES, 128)).astype(BF16), preferred_element_type=F32)
    ranks = ranks[:, :1].astype(jnp.int32) - 1
    slot = (ranks % me.count) * 8 + ranks // me.count
    selector[...] = jnp.where((keep[...] == 1) & (slot == column), 1.0, 0.0).astype(BF16)
    me.exchanged(mod_got, small_recv.at[2])
    total = mod_got[0]
    for i in range(1, half):
        total += mod_got[i]
    for i in range(63):
        mod[i // 9:i // 9 + 1, i % 9 * 128:(i % 9 + 1) * 128] = total[i:i + 1, :]
    me.exchanged(kept_got, small_recv.at[1])
    def put(cols):
        v = jnp.dot(selector[...], kept_got[:, :, cols].reshape(me.count * 8, -1), preferred_element_type=F32)
        stream_in[:, cols] = v + (1.0 - kept_here) * mod[6:7, cols]
    each_columns(put)

    def norm_one(rows):
        n, _ = standard(stream_in[rows, :])
        normed[rows, :] = (n * (1.0 + mod[1:2, :]) + mod[0:1, :]).astype(BF16)
    each_rows(PATCHES, 32, norm_one)
    turn(normed, one_t)
    save(stream_in, stream_in_out)
    save(one_t, one_t_out)
    net.begin(1)
    for tick in ticks:
        tick()
    net.arrived(0, range(zc))
    ticks, late = net.ticks(1)
    blocks.fetch(0)
    blocks.fetch(1)
    for b in range(3):
        w = blocks.take(b)
        def product(cols):
            projected[b, :, cols] = jnp.dot(normed[...], w[:, cols], preferred_element_type=F32).astype(BF16)
        each_columns(product)
        blocks.fetch(b + 2) if b + 2 < 4 else None
        ticks.pop(0)()
    save(projected, projected_out)
    wide_one[...] = jnp.zeros_like(wide_one)
    for head in range(HEADS):
        lanes, mask = window(head)
        q = projected[0, :, lanes] * mask.astype(BF16)
        scores = lax.dot_general(q, projected[1, :, lanes], NT, preferred_element_type=F32) * FACTOR
        u = spread_bias[:, head, :]
        bias = jnp.concatenate(
            [pltpu.roll(u, (SPAN - (GRID - 1 - r) * GRID) % SPAN, 1)[:, :PATCHES] for r in range(GRID)], axis=0)
        scores = scores + bias
        e = jnp.exp(scores - jnp.max(scores, axis=-1, keepdims=True))
        weights = e * (1.0 / jnp.sum(e, axis=-1, keepdims=True))
        att[head] = weights
        got = jnp.dot(weights.astype(BF16), projected[2, :, lanes], preferred_element_type=F32)
        wide_one[:, lanes] += got * mask
        if head % 2 and ticks:
            ticks.pop(0)()
        if head == 11:
            net.begin(2)
    normed[...] = wide_one[...].astype(BF16)
    turn(normed, mixed_t)
    save(att, att_out)
    save(mixed_t, mixed_t_out)
    w = blocks.take(3)
    def product(cols):
        branch[:, cols] = jnp.dot(normed[...], w[:, cols], preferred_element_type=F32)
    each_columns(product)
    def mid(rows):
        v = stream_in[rows, :] + mod[2:3, :] * branch[rows, :]
        stream_mid[rows, :] = v
        n, _ = standard(v)
        normed[rows, :] = (n * (1.0 + mod[4:5, :]) + mod[3:4, :]).astype(BF16)
    each_rows(PATCHES, 32, mid)
    turn(normed, two_t)
    save(branch, branch_out)
    save(stream_mid, stream_mid_out)
    save(two_t, two_t_out)
    for tick in ticks + late:
        tick()
    net.arrived(1, range(zc))
    ticks, late = net.ticks(2)
    def down_block(i):
        w = blocks.take(i)
        part = act.at[blocks.order[i][1]]
        def product(cols):
            v = jnp.dot(part[...], w[:, cols], preferred_element_type=F32)
            wide_one[:, cols] = v if i == 8 else wide_one[:, cols] + v
        each_columns(product)
    blocks.fetch(4)
    blocks.fetch(5)
    def turn_units(ref, b):
        turn(ref, turned)
        for i in range(8):
            unit = b * 8 + i
            w, n = unit // 4, unit % 4
            act_t[n % 2, n // 2, w * ROWS:(w + 1) * ROWS, :] = turned[i * ROWS:(i + 1) * ROWS, :]
    for b in range(4):
        w = blocks.take(4 + b)
        def product(cols):
            v = jnp.dot(normed[...], w[:, cols], preferred_element_type=F32)
            hidden[b, :, cols] = v
        each_columns(product)
        if b < 2:
            blocks.fetch(6 + b)
        def bend(rows):
            act[b, rows, :] = gelu(hidden[b, rows, :]).astype(BF16)
        each_rows(PATCHES, 32, bend)
        turn_units(act.at[b], b)
        save(hidden.at[b], hidden_out.at[b])
        for _ in range(2):
            ticks.pop(0)()
    save(act_t, act_t_out)
    for i in range(zc):
        blocks.order.append((2, lax.rem(me.z + zc - i, zc)))
    last_ticks = [[t for t in ticks + late if t.args[1][0] == i] for i in range(zc)]
    middle = [t for t in ticks if t.args[1][0] and sum(map(bool, t.args[1])) < 3]
    for i in range(zc):
        for t in last_ticks[i]:
            if t not in middle:
                t()
        if i == 0:
            for t in middle:
                t()
        net.arrived(2, [i])
        blocks.fetch(8 + i)
        if i:
            down_block(7 + i)
    down_block(7 + zc)
    gate_sum[...] = jnp.zeros_like(gate_sum)
    def last(rows):
        v = wide_one[rows, :]
        block_out[rows, :] = (stream_mid[rows, :] + mod[5:6, :] * v).astype(BF16)
        gate_sum[...] += jnp.sum(cotangent[rows, :].astype(F32) * v, axis=0, keepdims=True)
    each_rows(PATCHES, 32, last)
    for copy in saves:
        copy.wait()
    for g in range(3):
        net.finish(g)
    for i, got in enumerate((silu_got, kept_got, mod_got)):
        me.exchanged(got, small_send.at[i])


def run_forward(src, silu_out, ada, bias_row, token_row, kept, keep, table, cotangent, zc):
    vmem = pl.BlockSpec(memory_space=pltpu.VMEM)
    hbm = pl.BlockSpec(memory_space=pl.ANY)
    parts, count = max(map(len, PARTS)), 8 * zc
    shape = jax.ShapeDtypeStruct
    dma = pltpu.SemaphoreType.DMA
    kept_on = [((D, PATCHES), BF16), ((3, PATCHES, D), BF16), ((HEADS, PATCHES, PATCHES), F32), ((D, PATCHES), BF16), ((PATCHES, D), F32),
               ((PATCHES, D), F32), ((D, PATCHES), BF16), ((4, PATCHES, D), F32), ((2, 2, D, PATCHES), BF16), ((PATCHES, D), F32)]
    return pl.pallas_call(
        functools.partial(forward_kernel, zc),
        out_shape=[shape((3, 4, D, D), BF16)] + [shape(*k) for k in kept_on] + [
            shape((PATCHES, D), BF16), shape((8, D), F32), shape((count, 128), F32), shape((PATCHES, PATCHES), BF16), shape((1, D), F32)],
        in_specs=[hbm] + [vmem] * 8,
        out_specs=[hbm] * 11 + [vmem] * 5,
        scratch_shapes=[pltpu.VMEM(*k) for k in kept_on] + [
            dma((13,)),
            pltpu.VMEM((2, D, D), BF16), pltpu.VMEM((PATCHES, D), BF16), pltpu.VMEM((PATCHES, D), F32), pltpu.VMEM((4, PATCHES, D), BF16), pltpu.VMEM((D, PATCHES), BF16),
            pltpu.VMEM((count, 8, 128), F32), pltpu.VMEM((count, 64, 128), F32), pltpu.VMEM((count // 2, 64, 128), F32), pltpu.VMEM((count // 2, 64, 128), F32),
            pltpu.VMEM((count, 8, D), BF16), pltpu.VMEM((GRID, HEADS, SPAN), F32),
            dma((3, parts)), dma((3, parts, 4 * zc)), dma((3, parts)), dma((3, parts, zc)), dma((3,)), dma((2,)), dma((4,)), dma((4,))],
        compiler_params=pltpu.CompilerParams(collective_id=1, has_side_effects=True, vmem_limit_bytes=58 * 1024 * 1024),
        name="forward",
    )(src, silu_out, ada, bias_row, token_row, kept, keep, table, cotangent)


RPARTS = (((0, 80, "zxy"), (80, 64, "zyx")),) * 3


def reduce_plan(zc, order):
    live, slots, phases = rels(zc), {}, []
    for j, d in enumerate(order[::-1]):
        sends = [r for r in live if r[AT[d]]]
        live = [r for r in live if not r[AT[d]]]
        hops = list(range(1, zc)) if d == "z" else [1]
        for r in live:
            for k in hops:
                slots[r, j, k] = len(slots)
        phases.append((d, sends, live, hops))
    return phases, slots


class Reduce:
    def __init__(self, me, sums, landed, owned, send, recv):
        self.me, self.sums, self.landed, self.owned, self.send_sem, self.recv = me, sums, landed, owned, send, recv
        self.plans = [[reduce_plan(me.zc, part[2]) for part in parts] for parts in RPARTS]
        self.held = {}
        self.items = [(g, k) for g in (2, 1, 0) for k in list(range(1, me.zc)) + [0]]

    def partial(self, g, p, rel):
        r0, rows, _ = RPARTS[g][p]
        if (g, p, rel) in self.held:
            return self.landed.at[g, self.held[g, p, rel], pl.ds(r0, rows)]
        w, x = self.me.shifted(*rel)
        return self.sums[g].at[x, pl.ds(pl.multiple_of(w * ROWS + r0, 16), rows)]

    def send(self, g, p, j, rel):
        r0, rows, _ = RPARTS[g][p]
        d = self.plans[g][p][0][j][0]
        k = rel[AT[d]]
        hop = tuple(k if i == AT[d] else 0 for i in range(3))
        there = tuple(0 if i == AT[d] else rel[i] for i in range(3))
        slot = self.plans[g][p][1][there, j, k]
        pltpu.make_async_remote_copy(
            src_ref=self.partial(g, p, rel), dst_ref=self.landed.at[g, slot, pl.ds(r0, rows)],
            send_sem=self.send_sem.at[g, p, min(j, 1)], recv_sem=self.recv.at[g, p, slot],
            device_id=self.me.device(*hop), device_id_type=MESH).start()

    def receive(self, g, p, j, rel, final):
        r0, rows, _ = RPARTS[g][p]
        slots = [self.plans[g][p][1][rel, j, k] for k in self.plans[g][p][0][j][3]]
        for s in slots:
            ref = self.landed.at[g, s, pl.ds(r0, rows)]
            pltpu.make_async_copy(ref, ref, self.recv.at[g, p, s]).wait()
        mine = self.partial(g, p, rel)
        def body(i, carry):
            at = pl.ds(pl.multiple_of(r0 + i * 16, 16), 16)
            total = mine[pl.ds(pl.multiple_of(i * 16, 16), 16), :].astype(F32)
            for s in slots:
                total += self.landed[g, s, at, :].astype(F32)
            if final:
                self.owned[g][at, :] = total.astype(self.owned[g].dtype)
            else:
                self.landed[g, slots[0], at, :] = total.astype(BF16)
            return carry
        lax.fori_loop(0, rows // 16, body, 0)
        self.held[g, p, rel] = slots[0]

    def stage(self, j, g, k):
        for p in range(len(RPARTS[g])):
            phases = self.plans[g][p][0]
            lowered = [r for r in phases[j - 1][2] if r[0] == k] if j else []
            sends = [r for r in phases[j][1] if r[0] == k] if j < 3 else []
            for rel in sorted(lowered, key=lambda r: r not in sends):
                self.receive(g, p, j - 1, rel, j == 3)
                if rel in sends:
                    self.send(g, p, j, rel)
            if j == 0:
                for rel in sends:
                    self.send(g, p, 0, rel)

    def step(self, t):
        for j in range(4):
            if 0 <= t - j < len(self.items):
                self.stage(j, *self.items[t - j])

    def steps(self):
        return len(self.items) + 3

    def sent(self, g, late):
        for p, (r0, rows, _) in enumerate(RPARTS[g]):
            phases = self.plans[g][p][0]
            count = sum(len(phases[j][1]) for j in ((1, 2) if late else (0,)))
            ref = self.landed.at[g, pl.ds(0, count), pl.ds(r0, rows)]
            pltpu.make_async_copy(ref, ref, self.send_sem.at[g, p, int(late)]).wait()


class Fold:
    def __init__(self, me, table, token, lands, tokens, whole, send, recv):
        self.me, self.table, self.token, self.lands, self.whole = me, table, token, lands, whole
        self.token_land, self.token_out = tokens
        self.send, self.recv, self.started = send, recv, []
        self.steps, lo, size = [], 0, table.shape[0]
        for bit, many, peers in ((me.c, 2, [(0, 0, 0, 1)]), (me.x, 2, [(0, 0, 1)]), (me.y, 2, [(0, 1, 0)]),
                                 (me.z, me.zc, [(k, 0, 0) for k in range(1, me.zc)])):
            part = size // many
            self.steps.append((lo, size, part, bit, many, peers))
            lo, size = lo + bit * part, part
        self.lo = lo

    def rows(self, ref, at, count):
        return ref.at[pl.ds(pl.multiple_of(at, 8), count)]

    def remote(self, src, dst, which, peer):
        copy = pltpu.make_async_remote_copy(
            src_ref=src, dst_ref=dst, send_sem=self.send.at[which], recv_sem=self.recv.at[which],
            device_id=self.me.device(*peer), device_id_type=MESH)
        copy.start()
        self.started.append(copy)

    def give(self, i):
        lo, size, part, bit, many, peers = self.steps[i]
        self.token_out[i] = self.token[...]
        for k, peer in enumerate(peers):
            other = lax.rem(bit + k + 1, many)
            land = self.lands[i].at[k] if many > 2 or i == 3 else self.lands[i]
            self.remote(self.rows(self.table, lo + other * part, part), land, (i, 0, k), peer)
            self.remote(self.token_out.at[i], self.token_land.at[i, k], (i, 1, k), peer)

    def take(self, i):
        lo, size, part, bit, many, peers = self.steps[i]
        mine = pl.ds(pl.multiple_of(lo + bit * part, 8), part)
        for k in range(len(peers)):
            land = self.lands[i].at[k] if many > 2 or i == 3 else self.lands[i]
            pltpu.make_async_copy(land, land, self.recv.at[i, 0, k]).wait()
            pltpu.make_async_copy(self.token_land.at[i, k], self.token_land.at[i, k], self.recv.at[i, 1, k]).wait()
            self.table[mine, :] += land[...]
            self.token[...] += self.token_land[i, k]
        if i == 3:
            self.whole[mine, :] = self.table[mine, :]

    def hand(self, i):
        lo, size, part, bit, many, peers = self.steps[i]
        mine = self.rows(self.whole, lo + bit * part, part)
        for k, peer in enumerate(peers):
            self.remote(mine, mine, (4 + i, 0, k), peer)

    def handed(self, i):
        lo, size, part, bit, many, peers = self.steps[i]
        some = self.rows(self.whole, 0, part)
        for k in range(len(peers)):
            pltpu.make_async_copy(some, some, self.recv.at[4 + i, 0, k]).wait()

    def finish(self):
        for copy in self.started:
            copy.wait_send()


def backward_kernel(zc, full, mod, cotangent, stream_in, stream_mid, branch, projected, att, hidden, one_t, mixed_t, two_t, act_t,
                    ada, silu_part, selector, keep, gate_sum,
                    owned_down, owned_turned, grad_ada, mod_total, silu_back, kept_grad, table_grad, token_grad,
                    sum_a, sum_b, landed, wbuf, left, left_sib, acts, acts_sib, grad_down, right_sib, bent, rights, grad_mixed,
                    stream, hid, att_buf, spread_grad, grad_in, small,
                    owned_out, lines, line_low, mod_got, mod_flat, ada_wide, ada_low, silu_out, kept_out, table_sum, token_sum,
                    land_core, land_x, land_y, land_z, land_token, token_out, rights_out,
                    send, recv, sib_send, sib_recv, wsem, lsem, hsem, asem, ssem, small_send, small_recv, turn_send, turn_recv, fold_send, fold_recv):
    me = Place(zc)
    me.greet()
    c = me.c
    net = Reduce(me, {2: sum_a, 1: sum_b, 0: sum_a}, landed, {2: owned_down, 1: owned_out.at[1], 0: owned_out.at[0]}, send, recv)
    blocks = Blocks(full, wbuf, wsem, [(2, 0), (2, 1), (2, 2), (2, 3), (1, 0), (1, 1), (1, 2), (1, 3), (0, 3), (0, 0), (0, 1), (0, 2)])
    swaps = []

    def swap(src, dst):
        i = len(swaps)
        swaps.append(pltpu.make_async_remote_copy(
            src_ref=src, dst_ref=dst, send_sem=sib_send.at[i], recv_sem=sib_recv.at[i],
            device_id=me.device(0, 0, 0, 1), device_id_type=MESH))
        swaps[-1].start()
        return swaps[-1]

    def load(src, dst, sem):
        copy = pltpu.make_async_copy(src, dst, sem)
        copy.start()
        return copy

    act_swap = swap(act_t.at[1 - c], acts_sib)
    act_load = load(act_t.at[c], acts, lsem.at[0])
    blocks.fetch(0)
    blocks.fetch(1)
    hid_load = load(hidden.at[0], hid, hsem.at[0])

    def down(rows):
        grad_down[rows, :] = (mod[5:6, :] * cotangent[rows, :].astype(F32)).astype(BF16)
    each_rows(PATCHES, 32, down)
    down_swap = swap(grad_down, right_sib.at[0])
    ada_load = load(ada, ada_wide, lsem.at[4])
    left_loads = [load(ref, left.at[i], lsem.at[1 + i]) for i, ref in enumerate((one_t, mixed_t, two_t))]
    left_swaps = [swap(ref, left_sib.at[i]) for i, ref in enumerate((one_t, mixed_t, two_t))]
    mid_load = load(stream_mid, stream.at[0], ssem.at[0])

    def weight_grad(total, mine, mine_right, theirs, their_right):
        def body(cols):
            v = jnp.dot(mine[...], mine_right[:, cols], preferred_element_type=F32)
            total[:, cols] = (v + jnp.dot(theirs[...], their_right[:, cols], preferred_element_type=F32)).astype(BF16)
        each_columns(body)

    act_load.wait()
    act_swap.wait_recv()
    down_swap.wait_recv()
    for j in range(2):
        weight_grad(sum_a.at[j], acts.at[j], grad_down, acts_sib.at[j], right_sib.at[0])
    net.step(0)
    for b in range(4):
        w = blocks.take(b)
        hid_load.wait()
        def bend(cols):
            v = lax.dot_general(grad_down[...], w[cols, :], NT, preferred_element_type=F32)
            bent[b, :, cols] = (v * gelu_slope(hid[:, cols])).astype(BF16)
        each_columns(bend)
        blocks.fetch(b + 2)
        if b < 3:
            hid_load = load(hidden.at[b + 1], hid, hsem.at[0])
        if b in (1, 3):
            net.step((b + 1) // 2)
    branch_load = load(branch, hid, ssem.at[1])
    bent_swaps = [swap(bent.at[1 - c], right_sib.at[1]), swap(bent.at[3 - c], right_sib.at[2])]
    for copy in left_loads:
        copy.wait()
    for copy in left_swaps + bent_swaps:
        copy.wait_recv()
    for j in range(2):
        weight_grad(sum_b.at[j], left.at[2], bent.at[2 * j + c], left_sib.at[2], right_sib.at[1 + j])
    net.step(3)
    for b in range(4):
        w = blocks.take(4 + b)
        def back(cols):
            v = lax.dot_general(bent[b], w[cols, :], NT, preferred_element_type=F32)
            grad_in[:, cols] = v if b == 0 else grad_in[:, cols] + v
        each_columns(back)
        blocks.fetch(6 + b)
    mid_load.wait()
    branch_load.wait()
    small[...] = jnp.zeros_like(small)

    def norm_back(rows, stream_rows, scale, shift_at, scale_at):
        n, spread = standard(stream_rows)
        e = grad_in[rows, :]
        f = e * (1.0 + scale)
        small[shift_at:shift_at + 1, :] += jnp.sum(e, axis=0, keepdims=True)
        small[scale_at:scale_at + 1, :] += jnp.sum(e * n, axis=0, keepdims=True)
        return (f - jnp.mean(f, axis=-1, keepdims=True) - n * jnp.mean(f * n, axis=-1, keepdims=True)) * spread

    def back_two(rows):
        v = cotangent[rows, :].astype(F32) + norm_back(rows, stream[0, rows, :], mod[4:5, :], 3, 4)
        small[2:3, :] += jnp.sum(v * hid[rows, :], axis=0, keepdims=True)
        hid[rows, :] = v
        rights[3, rows, :] = (mod[2:3, :] * v).astype(BF16)
    each_rows(PATCHES, 32, back_two)
    in_load = load(stream_in, stream.at[0], ssem.at[0])
    net.step(4)
    att_load = load(att.at[0], att_buf.at[0], asem.at[0])
    w = blocks.take(8)
    def mixed_back(cols):
        grad_mixed[:, cols] = lax.dot_general(rights[3], w[cols, :], NT, preferred_element_type=F32).astype(BF16)
    each_columns(mixed_back)
    blocks.fetch(10)
    for b in range(3):
        rights[b] = jnp.zeros((PATCHES, D), BF16)
    net.step(5)
    for head in range(HEADS):
        att_load.wait()
        if head + 1 < HEADS:
            att_load = load(att.at[head + 1], att_buf.at[(head + 1) % 2], asem.at[(head + 1) % 2])
        lanes, mask = window(head)
        weights = att_buf[head % 2]
        low = weights.astype(BF16)
        given = grad_mixed[:, lanes]
        grad_att = lax.dot_general(given * mask.astype(BF16), projected[2, :, lanes], NT, preferred_element_type=F32)
        v = lax.dot_general(low, given, TN, preferred_element_type=F32)
        rights[2, :, lanes] += (v * mask).astype(BF16)
        scores = weights * (grad_att - jnp.sum(weights * grad_att, axis=-1, keepdims=True))
        scores_low = scores.astype(BF16)
        v = jnp.dot(scores_low, projected[1, :, lanes], preferred_element_type=F32) * FACTOR
        rights[0, :, lanes] += (v * mask).astype(BF16)
        v = lax.dot_general(scores_low, projected[0, :, lanes], TN, preferred_element_type=F32) * FACTOR
        rights[1, :, lanes] += (v * mask).astype(BF16)
        rounded = scores_low.astype(F32)
        total = jnp.zeros((GRID, SPAN), F32)
        for r in range(GRID):
            rows = jnp.concatenate([rounded[r * GRID:(r + 1) * GRID], jnp.zeros((GRID, SPAN - PATCHES), F32)], axis=1)
            total += pltpu.roll(rows, (GRID - 1 - r) * GRID, 1)
        spread_grad[:, head, :] = total
        if head in (7, 15):
            net.step(6 + head // 8)
    end_swaps = [swap(rights.at[1 - c], right_sib.at[3]), swap(rights.at[3 - c], right_sib.at[4])]
    for b in range(3):
        w = blocks.take(9 + b)
        def back(cols):
            v = lax.dot_general(rights[b], w[cols, :], NT, preferred_element_type=F32)
            grad_in[:, cols] = v if b == 0 else grad_in[:, cols] + v
        each_columns(back)
        blocks.fetch(11 + b)
    in_load.wait()
    def back_one(rows):
        v = norm_back(rows, stream[0, rows, :], mod[1:2, :], 0, 1)
        grad_in[rows, :] = hid[rows, :] + v
    each_rows(PATCHES, 32, back_one)
    for v in range(6):
        for i in range(9):
            piece = small[v:v + 1, i * 128:(i + 1) * 128] if v < 5 else gate_sum[:, i * 128:(i + 1) * 128]
            lines[v * 9 + i:v * 9 + i + 1, :] = piece
    lines[54:64, :] = jnp.zeros((10, 128), F32)
    line_low[...] = lines[...].astype(BF16)
    half, chip = me.count // 2, me.line // 2
    mine_at = c * half
    me.exchange_chips(lambda t: line_low, mod_got.at[mine_at + chip], small_send.at[0], small_recv.at[0])
    mod_got[mine_at + chip] = line_low[...]
    grad_mixed[...] = grad_in[...].astype(BF16)
    def put_back(cols):
        v = lax.dot_general(selector[...], grad_mixed[:, cols], TN, preferred_element_type=F32).astype(BF16)
        kept_out[:, :, cols] = v.reshape(me.count, 8, -1)
    each_columns(put_back)
    me.exchange(lambda t: kept_out.at[t], kept_grad.at[me.line], small_send.at[1], small_recv.at[1])
    kept_own = load(kept_out.at[me.line], kept_grad.at[me.line], ssem.at[1])
    net.sent(2, False)
    for copy in end_swaps:
        copy.wait_recv()
    weight_grad(sum_a.at[0], left.at[0], rights.at[c], left_sib.at[0], right_sib.at[3])
    weight_grad(sum_a.at[1], left.at[c], rights.at[2 + c], left_sib.at[c], right_sib.at[4])
    net.step(8)

    masked = 1.0 - keep[...].astype(F32)
    token = jnp.sum(masked * grad_in[...], axis=0, keepdims=True)
    for i in range(9):
        token_sum[i:i + 1, :] = token[:, i * 128:(i + 1) * 128]
    token_sum[9:16, :] = jnp.zeros((7, 128), F32)
    picked_rows = row_picker(SPAN)
    table_sum[...] = jnp.zeros_like(table_sum)
    def gather_table(x, carry):
        picker = table_picker(x, 128, SPAN)
        v = (spread_grad[x][:, None, :] * picked_rows[None]).reshape(HEADS * 2 * GRID, SPAN)
        high = v.astype(BF16)
        rest = v - high.astype(F32)
        middle = rest.astype(BF16)
        low = (rest - middle.astype(F32)).astype(BF16)
        for part in (high, middle, low):
            table_sum[...] += lax.dot_general(part, picker, NT, preferred_element_type=F32)
        return carry
    lax.fori_loop(0, GRID, gather_table, 0)
    fold = Fold(me, table_sum, token_sum, (land_core, land_x, land_y, land_z), (land_token, token_out), table_grad, fold_send, fold_recv)
    fold.give(0)
    net.step(9)
    fold.take(0)
    fold.give(1)

    plane = mod_got.at[pl.ds(mine_at, half)]
    me.exchanged(plane, small_recv.at[0])
    mod_swap = pltpu.make_async_remote_copy(
        src_ref=plane, dst_ref=plane, send_sem=small_send.at[2], recv_sem=small_recv.at[2],
        device_id=me.device(0, 0, 0, 1), device_id_type=MESH)
    mod_swap.start()
    ada_load.wait()
    def flat(j, carry):
        lanes = pl.ds(pl.multiple_of(j * 128, 128), 128)
        ada_low[:, lanes] = ada_wide[:, lanes].astype(BF16)
        return carry
    lax.fori_loop(0, 54, flat, 0)
    mod_swap.wait_recv()
    for j in range(54):
        mod_flat[:, j * 128:(j + 1) * 128] = mod_got[:, j, :]
    width = ada.shape[0]
    back_silu = lax.dot_general(mod_flat[...], ada_low[...], NT, preferred_element_type=F32)
    silu_out[...] = jnp.zeros_like(silu_out)
    silu_out[:, 0:1, 0:width] = back_silu[:, None, :]
    me.exchange(lambda t: silu_out.at[me.turned(t)], silu_back.at[me.line], small_send.at[3], small_recv.at[3])
    silu_back[me.line] = silu_out[me.turned(me.line)]
    net.step(10)
    fold.take(1)
    fold.give(2)
    mine = silu_part[:, :width].astype(BF16)
    def outer(j, carry):
        lanes = pl.ds(pl.multiple_of(j * 256, 256), 256)
        grad_ada[:, lanes] = lax.dot_general(mine, mod_flat[:, lanes], TN, preferred_element_type=F32)
        return carry
    lax.fori_loop(0, 27, outer, 0)
    total = jnp.zeros((64, 128), F32)
    for i in range(me.count):
        total += mod_got[i].astype(F32)
    mod_total[...] = total
    net.step(11)
    fold.take(2)
    fold.give(3)
    turns = []

    def turn_rows(g):
        for n in range(4):
            rights_out[n, g] = owned_out[g, n * width:(n + 1) * width, :].astype(BF16)
        for k in range(1, 4):
            n = (me.x * 2 + me.c + k) % 4
            copy = pltpu.make_async_remote_copy(
                src_ref=rights_out.at[n, g], dst_ref=owned_turned.at[me.x * 2 + me.c, g], send_sem=turn_send.at[g, k - 1], recv_sem=turn_recv.at[g, k - 1],
                device_id=(me.line // 4, n), device_id_type=MESH)
            copy.start()
            turns.append(copy)
        owned_turned[me.x * 2 + me.c, g] = rights_out[me.x * 2 + me.c, g]

    turn_rows(1)
    fold.take(3)
    token_grad[...] = token_sum[...]
    fold.hand(3)
    net.step(12)
    fold.handed(3)
    fold.hand(2)
    net.step(13)
    fold.handed(2)
    fold.hand(1)
    net.step(14)
    turn_rows(0)
    fold.handed(1)
    fold.hand(0)
    net.sent(1, False)
    net.sent(0, False)
    for g in range(3):
        net.sent(g, True)
    for copy in swaps:
        copy.wait_send()
    kept_own.wait()
    me.exchanged(kept_grad, small_recv.at[1])
    me.exchanged(silu_back, small_recv.at[3])
    me.exchanged(plane, small_send.at[0])
    me.exchanged(kept_grad, small_send.at[1])
    mod_swap.wait_send()
    me.exchanged(silu_back, small_send.at[3])
    fold.handed(0)
    fold.finish()
    for copy in turns:
        copy.wait()


def run_backward(full, mod, cotangent, stream_in, stream_mid, branch, projected, att, hidden, one_t, mixed_t, two_t, act_t,
                 ada, silu_part, selector, keep, gate_sum, zc):
    vmem = pl.BlockSpec(memory_space=pltpu.VMEM)
    hbm = pl.BlockSpec(memory_space=pl.ANY)
    parts, count, width = max(map(len, RPARTS)), 8 * zc, ada.shape[0]
    table = HEADS * 2 * GRID
    shape = jax.ShapeDtypeStruct
    dma = pltpu.SemaphoreType.DMA
    return pl.pallas_call(
        functools.partial(backward_kernel, zc),
        out_shape=(shape((ROWS, D), F32), shape((4, 2, width, D), BF16), shape((width, 6 * D), F32), shape((64, 128), F32),
                   shape((count, 8, 128), F32), shape((count, 8, D), BF16), shape((HEADS * 2 * GRID, 128), F32), shape((16, 128), F32)),
        in_specs=[hbm, vmem, vmem, hbm, hbm, hbm, vmem, hbm, hbm, hbm, hbm, hbm, hbm, hbm, vmem, vmem, vmem, vmem],
        out_specs=(vmem, vmem, vmem, vmem, vmem, hbm, vmem, vmem),
        scratch_shapes=[
            pltpu.VMEM((2, D, D), BF16), pltpu.VMEM((2, D, D), BF16), pltpu.VMEM((3, 4 * zc - 1, ROWS, D), BF16),
            pltpu.VMEM((2, D, D), BF16), pltpu.VMEM((3, D, PATCHES), BF16), pltpu.VMEM((3, D, PATCHES), BF16),
            pltpu.VMEM((2, D, PATCHES), BF16), pltpu.VMEM((2, D, PATCHES), BF16), pltpu.VMEM((PATCHES, D), BF16),
            pltpu.VMEM((5, PATCHES, D), BF16), pltpu.VMEM((4, PATCHES, D), BF16), pltpu.VMEM((4, PATCHES, D), BF16),
            pltpu.VMEM((PATCHES, D), BF16), pltpu.VMEM((1, PATCHES, D), F32), pltpu.VMEM((PATCHES, D), F32),
            pltpu.VMEM((2, PATCHES, PATCHES), F32),
            pltpu.VMEM((GRID, HEADS, SPAN), F32), pltpu.VMEM((PATCHES, D), F32), pltpu.VMEM((8, D), F32),
            pltpu.VMEM((2, ROWS, D), F32), pltpu.VMEM((64, 128), F32), pltpu.VMEM((64, 128), BF16), pltpu.VMEM((count, 64, 128), BF16),
            pltpu.VMEM((count, 6 * D), BF16), pltpu.VMEM((width, 6 * D), F32), pltpu.VMEM((width, 6 * D), BF16), pltpu.VMEM((count, 8, 128), F32),
            pltpu.VMEM((count, 8, D), BF16), pltpu.VMEM((table, 128), F32), pltpu.VMEM((16, 128), F32),
            pltpu.VMEM((table // 2, 128), F32), pltpu.VMEM((table // 4, 128), F32), pltpu.VMEM((table // 8, 128), F32),
            pltpu.VMEM((zc - 1, table // 8 // zc, 128), F32), pltpu.VMEM((4, zc - 1, 16, 128), F32), pltpu.VMEM((4, 16, 128), F32), pltpu.VMEM((4, 2, width, D), BF16),
            dma((3, parts, 2)), dma((3, parts, 4 * zc - 1)), dma((9,)), dma((9,)), dma((2,)), dma((5,)), dma((1,)), dma((2,)), dma((2,)),
            dma((4,)), dma((4,)), dma((2, 3)), dma((2, 3)), dma((8, 2, zc - 1)), dma((8, 2, zc - 1))],
        compiler_params=pltpu.CompilerParams(collective_id=2, has_side_effects=True, vmem_limit_bytes=63 * 1024 * 1024),
        name="backward",
    )(full, mod, cotangent, stream_in, stream_mid, branch, projected, att, hidden, one_t, mixed_t, two_t, act_t,
      ada, silu_part, selector, keep, gate_sum)


AXES = ("wide", "narrow")


def running_rank(keep_flat):
    count = keep_flat.shape[0]
    lower = (lax.broadcasted_iota(jnp.int32, (count, count), 0) >= lax.broadcasted_iota(jnp.int32, (count, count), 1))
    total = jnp.dot(lower.astype(jnp.bfloat16), keep_flat.astype(jnp.bfloat16)[:, None], preferred_element_type=jnp.float32)
    return total[:, 0].astype(jnp.int32) - 1


def per_device_plain(kept_tokens, keep_mask, conditioning, ada_weight, ada_bias, qkv_weight, out_weight, up_weight, down_weight, position_bias, mask_token, cotangent):
    wide_count = lax.axis_size("wide")
    narrow_count = lax.axis_size("narrow")
    devices = wide_count * narrow_count
    slots = kept_tokens.shape[2]
    images = conditioning.shape[0]
    count = images * PATCHES
    rows = qkv_weight.shape[0]
    me = lax.axis_index(AXES)
    factor = 1.0 / math.sqrt(HEAD_DIM)
    low_type = jnp.bfloat16
    wide_type = jnp.float32
    silu_cond = jax.nn.silu(conditioning).astype(low_type)
    small = jnp.concatenate([silu_cond.reshape(-1), ada_bias.astype(low_type), mask_token.astype(low_type)])
    smalls = lax.all_gather(small, AXES, axis=0, tiled=False)
    silu_all = smalls[:, : images * D].reshape(devices * images, D)
    bias_full = smalls[:, images * D : images * D + ada_bias.shape[0]].reshape(-1)
    token_full = smalls[:, images * D + ada_bias.shape[0] :].reshape(-1)
    ada_low = ada_weight.astype(low_type)
    silu_part = lax.dynamic_slice_in_dim(silu_all, me * rows, rows, axis=1)
    mod_part = jnp.dot(silu_part, ada_low, preferred_element_type=wide_type)
    mod_parts = lax.all_to_all(mod_part.reshape(devices, images, 6 * D), AXES, split_axis=0, concat_axis=0, tiled=True)
    modulation = jnp.sum(mod_parts, axis=0) + bias_full.astype(wide_type)[None, :]
    qkv_full = lax.all_gather(qkv_weight.astype(low_type), AXES, axis=0, tiled=True)
    out_full = lax.all_gather(out_weight.astype(low_type), AXES, axis=0, tiled=True)
    up_full = lax.all_gather(up_weight.astype(low_type), AXES, axis=0, tiled=True)
    down_full = lax.all_gather(down_weight.astype(low_type), AXES, axis=0, tiled=True)
    def times_qkv(v):
        return jnp.dot(v, qkv_full, preferred_element_type=wide_type)
    def times_qkv_back(v):
        return jnp.dot(v, qkv_full.T, preferred_element_type=wide_type)
    def times_up(v):
        return jnp.dot(v, up_full, preferred_element_type=wide_type)
    def times_up_back(v):
        return jnp.dot(v, up_full.T, preferred_element_type=wide_type)
    arrived = lax.all_to_all(kept_tokens, AXES, split_axis=1, concat_axis=0, tiled=True)
    received = arrived.reshape(devices * slots, D)
    keep_flat = keep_mask.reshape(count)
    keep_float = keep_flat.astype(wide_type)
    ranks = running_rank(keep_flat)
    target = ranks % devices * slots + ranks // devices
    columns = jnp.arange(devices * slots, dtype=jnp.int32)
    selector = jnp.where((keep_flat[:, None] == 1) & (target[:, None] == columns[None, :]), 1.0, 0.0).astype(wide_type)
    stream_in = jnp.dot(selector.astype(low_type), received, preferred_element_type=wide_type)
    stream_in = stream_in + (1.0 - keep_float)[:, None] * token_full.astype(wide_type)[None, :]
    stream_in = stream_in.reshape(images, PATCHES, D)
    shift_one, scale_one, gate_one, shift_two, scale_two, gate_two = jnp.split(
        modulation[:, None, :], 6, axis=-1
    )
    normed_one = modulate(stream_in, shift_one, scale_one).astype(low_type).reshape(count, D)
    projected = times_qkv(normed_one).astype(low_type)
    projected = projected.reshape(images, PATCHES, 3, HEADS, HEAD_DIM)
    queries = projected[:, :, 0]
    key_rows = projected[:, :, 1]
    value_rows = projected[:, :, 2]
    relative = expand_bias(position_bias, GRID)
    scores = (
        jnp.einsum("iqhd,ikhd->ihqk", queries, key_rows, preferred_element_type=wide_type) * factor
        + relative[None]
    )
    att_weights = jax.nn.softmax(scores, axis=-1)
    att_low = att_weights.astype(low_type)
    mixed = (
        jnp.einsum("ihqk,ikhd->iqhd", att_low, value_rows, preferred_element_type=wide_type)
        .astype(low_type)
        .reshape(count, D)
    )
    branch = jnp.dot(mixed, out_full, preferred_element_type=wide_type).reshape(images, PATCHES, D)
    stream_mid = stream_in + gate_one * branch
    normed_two = modulate(stream_mid, shift_two, scale_two).astype(low_type).reshape(count, D)
    hidden = times_up(normed_two)
    activated = gelu_tanh(hidden).astype(low_type)
    down = jnp.dot(activated, down_full, preferred_element_type=wide_type).reshape(
        images, PATCHES, D
    )
    block_out = (stream_mid + gate_two * down).reshape(count, D).astype(low_type)
    incoming = cotangent.astype(wide_type).reshape(images, PATCHES, D)
    grad_gate_two = jnp.sum(incoming * down, axis=1)
    grad_down = (gate_two * incoming).astype(low_type).reshape(count, D)
    grad_activated = jnp.dot(grad_down, down_full.T, preferred_element_type=wide_type)
    _, gelu_pull = jax.vjp(gelu_tanh, hidden)
    grad_hidden = gelu_pull(grad_activated)[0].astype(low_type)
    grad_normed_two = times_up_back(grad_hidden).reshape(
        images, PATCHES, D
    )
    _, norm_pull_two = jax.vjp(modulate, stream_mid, shift_two, scale_two)
    grad_mid_norm, grad_shift_two, grad_scale_two = norm_pull_two(grad_normed_two)
    grad_mid = incoming + grad_mid_norm
    grad_gate_one = jnp.sum(grad_mid * branch, axis=1)
    grad_branch = (gate_one * grad_mid).astype(low_type).reshape(count, D)
    grad_mixed = jnp.dot(grad_branch, out_full.T, preferred_element_type=wide_type).astype(low_type)
    grad_mixed = grad_mixed.reshape(images, PATCHES, HEADS, HEAD_DIM)
    grad_att = jnp.einsum(
        "iqhd,ikhd->ihqk", grad_mixed, value_rows, preferred_element_type=wide_type
    )
    grad_values = jnp.einsum(
        "ihqk,iqhd->ikhd", att_low, grad_mixed, preferred_element_type=wide_type
    )
    grad_scores = (
        att_weights * (grad_att - jnp.sum(att_weights * grad_att, axis=-1, keepdims=True))
    ).astype(low_type)
    grad_queries = (
        jnp.einsum("ihqk,ikhd->iqhd", grad_scores, key_rows, preferred_element_type=wide_type)
        * factor
    )
    grad_keys = (
        jnp.einsum("ihqk,iqhd->ikhd", grad_scores, queries, preferred_element_type=wide_type)
        * factor
    )
    grad_table = bias_adjoint(jnp.sum(grad_scores.astype(wide_type), axis=0), GRID)
    grad_projected = (
        jnp.stack([grad_queries, grad_keys, grad_values], axis=2)
        .astype(low_type)
        .reshape(count, 3 * D)
    )
    grad_normed_one = times_qkv_back(grad_projected).reshape(
        images, PATCHES, D
    )
    _, norm_pull_one = jax.vjp(modulate, stream_in, shift_one, scale_one)
    grad_in_norm, grad_shift_one, grad_scale_one = norm_pull_one(grad_normed_one)
    grad_in = (grad_mid + grad_in_norm).reshape(count, D)
    grad_modulation = jnp.concatenate(
        [
            grad_shift_one[:, 0],
            grad_scale_one[:, 0],
            grad_gate_one,
            grad_shift_two[:, 0],
            grad_scale_two[:, 0],
            grad_gate_two,
        ],
        axis=-1,
    ).astype(low_type)
    grad_mod_all = lax.all_gather(grad_modulation, AXES, axis=0, tiled=True)
    grad_ada = lax.dot_general(silu_part, grad_mod_all, (((0,), (0,)), ((), ())), preferred_element_type=wide_type)
    bias_share = 6 * D // devices
    sum_bias = jnp.sum(lax.dynamic_slice_in_dim(grad_mod_all, me * bias_share, bias_share, axis=1).astype(wide_type), axis=0)
    silu_parts = lax.dot_general(grad_mod_all, ada_low, (((1,), (1,)), ((), ())), preferred_element_type=wide_type)
    silu_parts = lax.all_to_all(silu_parts.reshape(devices, images, rows), AXES, split_axis=0, concat_axis=0, tiled=True)
    grad_silu = silu_parts.transpose(1, 0, 2).reshape(images, D)
    _, silu_pull = jax.vjp(jax.nn.silu, conditioning)
    grad_cond = silu_pull(grad_silu)[0]
    grad_mask = jnp.sum((1.0 - keep_float)[:, None] * grad_in, axis=0)
    grad_received = jnp.dot(
        selector.T, grad_in, precision=lax.Precision.HIGHEST, preferred_element_type=wide_type
    ).astype(low_type)
    grad_kept = lax.all_to_all(
        grad_received.reshape(devices, 1, slots, D),
        ("wide", "narrow"),
        split_axis=0,
        concat_axis=1,
        tiled=True,
    )
    def scatter(left, right):
        partial = lax.dot_general(left, right, (((0,), (0,)), ((), ())), preferred_element_type=wide_type)
        return lax.psum_scatter(partial.reshape(-1), AXES, scatter_dimension=0, tiled=True).reshape(-1, right.shape[1])
    sum_qkv = scatter(normed_one, grad_projected)
    sum_out = scatter(mixed, grad_branch)
    sum_up = scatter(normed_two, grad_hidden)
    sum_down = scatter(activated, grad_down)
    grad_table_all, mask_whole = lax.psum((grad_table, grad_mask), AXES)
    mask_share = D // devices
    sum_mask = lax.dynamic_slice_in_dim(mask_whole, me * mask_share, mask_share)
    return (block_out, grad_kept, grad_cond, grad_ada, sum_bias, sum_qkv, sum_out, sum_up, sum_down, grad_table_all, sum_mask)


def rounded(v):
    return lax.reduce_precision(v, 8, 7)


def per_device(kept_tokens, keep_mask, conditioning, ada_weight, ada_bias, qkv_weight, out_weight, up_weight, down_weight, position_bias, mask_token, cotangent):
    if kept_tokens.shape[2] > 8 or conditioning.shape[0] != 1:
        return per_device_plain(kept_tokens, keep_mask, conditioning, ada_weight, ada_bias, qkv_weight, out_weight, up_weight, down_weight, position_bias, mask_token, cotangent)
    wide_count = lax.axis_size("wide")
    devices = wide_count * lax.axis_size("narrow")
    slots = kept_tokens.shape[2]
    rows = qkv_weight.shape[0]
    share = ada_bias.shape[0]
    me = lax.axis_index(AXES)
    zc = wide_count // 2
    attn_src = jnp.concatenate([qkv_weight.reshape(rows, 3, D), out_weight.reshape(rows, 1, D)], axis=1)
    both = jnp.stack([attn_src, up_weight.reshape(rows, 4, D)], axis=0).astype(BF16)
    turned = lax.all_to_all(both.transpose(2, 0, 1, 3), "narrow", split_axis=0, concat_axis=0, tiled=True)
    turned = turned.transpose(1, 0, 2, 3).reshape(2, ROWS, D)
    source = jnp.concatenate([turned, down_weight.astype(BF16)[None]], axis=0)

    silu_out = jnp.pad(rounded(jax.nn.silu(conditioning)).reshape(devices, 1, rows), ((0, 0), (0, 7), (0, 128 - rows)))
    bias_row = lax.dynamic_update_slice(jnp.zeros((1, 6 * D), F32), rounded(ada_bias)[None], (0, me * share))
    token_row = lax.dynamic_update_slice(jnp.zeros((1, D), F32), rounded(mask_token)[None], (0, me * rows))
    kept = jnp.pad(kept_tokens.reshape(devices, slots, D), ((0, 0), (0, 8 - slots), (0, 0)))
    table = jnp.pad(position_bias, ((0, 0), (0, 1), (0, 128 - position_bias.shape[2]))).reshape(HEADS * 2 * GRID, 128)
    keep = keep_mask.reshape(PATCHES, 1)
    keep_float = keep.astype(F32)

    (full, one_t, projected, att, mixed_t, branch, stream_mid, two_t, hidden, act_t, stream_in, block_out, mod, silu_part, selector, gate_sum) = run_forward(
        source, silu_out, ada_weight, bias_row, token_row, kept, keep, table, cotangent, zc)
    sum_down, turned, grad_ada, mod_total, silu_back, kept_grad, table_grad, token_grad = run_backward(
        full, mod, cotangent, stream_in, stream_mid, branch, projected, att, hidden, one_t, mixed_t, two_t, act_t,
        ada_weight, silu_part, selector, keep, gate_sum, zc)

    sum_bias = lax.dynamic_slice(mod_total[:54].reshape(-1), (me * share,), (share,))
    sum_mask = lax.dynamic_slice(token_grad[:9].reshape(-1), (me * rows,), (rows,))
    _, silu_pull = jax.vjp(jax.nn.silu, conditioning)
    grad_cond = silu_pull(silu_back[:, 0, :rows].reshape(1, D))[0]
    grad_kept = kept_grad[None, :, :slots]
    offsets = position_bias.shape[2]
    grad_table = table_grad.reshape(HEADS, 2 * GRID, 128)[:, :offsets, :offsets]
    sum_qkv = turned[:3, 0].transpose(1, 0, 2).reshape(rows, 3 * D).astype(F32)
    sum_out = turned[3, 0].astype(F32)
    sum_up = turned[:, 1].transpose(1, 0, 2).reshape(rows, FF).astype(F32)
    return (block_out, grad_kept, grad_cond, grad_ada, sum_bias, sum_qkv, sum_out, sum_up, sum_down, grad_table, sum_mask)


def solution(mesh):
    in_specs = (
        P(("wide", "narrow"), None, None, None),
        P(("wide", "narrow"), None),
        P(("wide", "narrow"), None),
        P(("wide", "narrow"), None),
        P(("wide", "narrow")),
        P(("wide", "narrow"), None),
        P(("wide", "narrow"), None),
        P(("wide", "narrow"), None),
        P(("wide", "narrow"), None),
        P(),
        P(("wide", "narrow")),
        P(("wide", "narrow"), None),
    )
    out_specs = (
        P(("wide", "narrow"), None),
        P(("wide", "narrow"), None, None, None),
        P(("wide", "narrow"), None),
        P(("wide", "narrow"), None),
        P(("wide", "narrow")),
        P(("wide", "narrow"), None),
        P(("wide", "narrow"), None),
        P(("wide", "narrow"), None),
        P(("wide", "narrow"), None),
        P(),
        P(("wide", "narrow")),
    )
    shape = dict(mesh.shape)
    rows = D // (shape["wide"] * shape["narrow"])
    fast = shape["narrow"] == 4 and shape["wide"] % 2 == 0 and rows * 4 == ROWS
    return jax.shard_map(
        per_device if fast else per_device_plain, mesh=mesh, in_specs=in_specs, out_specs=out_specs, check_vma=False
    )
```

```python
import functools
import math

import jax
import jax.numpy as jnp
from jax import lax
from jax.experimental import pallas as pl
from jax.experimental.pallas import tpu as pltpu
from jax.sharding import PartitionSpec as P

D = 1152
HEADS = 16
HEAD_DIM = 72
FF = 4608
GRID = 16
PATCHES = 256


EPSILON = 1e-06


def layer_norm(stream):
    center = stream - jnp.mean(stream, axis=-1, keepdims=True)
    variance = jnp.mean(center * center, axis=-1, keepdims=True)
    return center * lax.rsqrt(variance + EPSILON)


def modulate(stream, shift, scale):
    return layer_norm(stream) * (1.0 + scale) + shift


def offset_picker(grid):
    places = jnp.arange(grid, dtype=jnp.int32)
    spread = jnp.arange(2 * grid - 1, dtype=jnp.int32)
    return (
        places[:, None, None] - places[None, :, None] + grid - 1 == spread[None, None, :]
    ).astype(jnp.float32)


def expand_bias(table, grid):
    picker = offset_picker(grid)
    partial_rows = jnp.einsum("yka,had->hykd", picker, table, precision=lax.Precision.HIGHEST)
    expanded = jnp.einsum("hykd,xjd->hyxkj", partial_rows, picker, precision=lax.Precision.HIGHEST)
    return expanded.reshape(table.shape[0], grid * grid, grid * grid)


def bias_adjoint(grad_bias, grid):
    picker = offset_picker(grid)
    shaped = grad_bias.reshape(grad_bias.shape[0], grid, grid, grid, grid)
    partial_rows = jnp.einsum("hyxkj,xjd->hykd", shaped, picker, precision=lax.Precision.HIGHEST)
    return jnp.einsum("hykd,yka->had", partial_rows, picker, precision=lax.Precision.HIGHEST)


def gelu_tanh(value):
    return jax.nn.gelu(value, approximate=True)


MESH = pl.DeviceIdType.MESH
ROWS = 144
PARTS = (
    ((0, 80, "zxy"), (80, 64, "zyx")),
    ((0, 64, "zxy"), (64, 48, "zyx"), (112, 32, "xyz")),
    ((0, 64, "zxy"), (64, 64, "zyx"), (128, 16, "xyz")),
)
AT = {"z": 0, "y": 1, "x": 2}
F32 = jnp.float32
BF16 = jnp.bfloat16
FACTOR = 1.0 / math.sqrt(HEAD_DIM)
NT = (((1,), (1,)), ((), ()))
TN = (((0,), (0,)), ((), ()))
SPAN = 2 * PATCHES


def rels(zc):
    return [(rz, ry, rx) for rz in range(zc) for ry in range(2) for rx in range(2)]


class Place:
    def __init__(self, zc):
        wide = lax.axis_index("wide")
        narrow = lax.axis_index("narrow")
        self.zc, self.wcount = zc, 2 * zc
        self.line, self.count = wide * 4 + narrow, 8 * zc
        self.z, self.y, self.x, self.c = wide // 2, wide % 2, narrow // 2, narrow % 2
        self.hops = {"z": [(k, 0, 0) for k in range(1, zc)], "y": [(0, 1, 0)], "x": [(0, 0, 1)]}

    def shifted(self, rz, ry, rx):
        w = lax.rem(self.z + rz, self.zc) * 2 + (self.y + ry) % 2
        return w, (self.x + rx) % 2

    def device(self, rz, ry, rx, flip=0):
        w, x = self.shifted(rz, ry, rx)
        return w, x * 2 + (self.c + flip) % 2

    def greet(self):
        barrier = pltpu.get_barrier_semaphore()
        def hello(k, carry):
            t = lax.rem(self.line + k, self.count)
            pl.semaphore_signal(barrier, inc=1, device_id=(t // 4, t % 4), device_id_type=MESH)
            return carry
        lax.fori_loop(1, self.count, hello, 0)
        pl.semaphore_wait(barrier, self.count - 1)

    def turned(self, t):
        return t % 2 * (self.count // 2) + t // 2

    def exchange(self, piece, there, send, recv):
        def go(k, carry):
            t = lax.rem(self.line + k, self.count)
            pltpu.make_async_remote_copy(
                src_ref=piece(t), dst_ref=there, send_sem=send, recv_sem=recv,
                device_id=(t // 4, t % 4), device_id_type=MESH).start()
            return carry
        lax.fori_loop(1, self.count, go, 0)

    def exchange_chips(self, piece, there, send, recv):
        def go(k, carry):
            t = lax.rem(self.line + 2 * k, self.count)
            pltpu.make_async_remote_copy(
                src_ref=piece(t // 2), dst_ref=there, send_sem=send, recv_sem=recv,
                device_id=(t // 4, t % 4), device_id_type=MESH).start()
            return carry
        lax.fori_loop(1, self.count // 2, go, 0)

    def exchanged(self, got, sem):
        others = got.at[pl.ds(0, got.shape[0] - 1)]
        pltpu.make_async_copy(others, others, sem).wait()


def wait_rows(ref, total, sem):
    for blocks in range(1, ref.shape[0] + 1):
        if total % (blocks * 16) == 0 and total // blocks <= ref.shape[1]:
            some = ref.at[pl.ds(0, blocks), pl.ds(0, total // blocks)]
            pltpu.make_async_copy(some, some, sem).wait()
            return
    raise ValueError("rows")


def each_rows(total, step, body):
    def go(i, carry):
        body(pl.ds(pl.multiple_of(i * step, step), step))
        return carry
    lax.fori_loop(0, total // step, go, 0)


def each_columns(body):
    def go(i, carry):
        body(pl.ds(pl.multiple_of(i * 256, 256), 256))
        return carry
    lax.fori_loop(0, 4, go, 0)
    body(pl.ds(1024, 128))


def window(head):
    low = head * HEAD_DIM
    first, last = low // 128 * 128, -(-(low + HEAD_DIM) // 128) * 128
    lane = lax.broadcasted_iota(jnp.int32, (1, last - first), 1) + first
    mask = jnp.where((lane >= low) & (lane < low + HEAD_DIM), 1.0, 0.0).astype(F32)
    return slice(first, last), mask


class Gather:
    def __init__(self, me, src, out, sems):
        self.me, self.src, self.out = me, src, out
        self.send, self.recv, self.sib_send, self.sib_recv, self.own = sems
        self.all = rels(me.zc)
        self.index = {r: i for i, r in enumerate(self.all)}

    def block(self, g, rel, r0, rows):
        w, x = self.me.shifted(self.me.zc - rel[0], rel[1], rel[2])
        n = x * 2 + self.me.c
        b, row = (n, w * ROWS) if g < 2 else ((w * 4 + n) // self.me.wcount, lax.rem(w * 4 + n, self.me.wcount) * ROWS)
        return self.out.at[g, b, pl.ds(pl.multiple_of(row + r0, 16), rows)]

    def forward(self, g, p, rel):
        r0, rows, order = PARTS[g][p]
        at = max([i for i, d in enumerate(order) if rel[AT[d]]], default=-1)
        there = self.block(g, rel, r0, rows)
        here = there if any(rel) else self.src.at[g, pl.ds(r0, rows)]
        for d in order[at + 1:]:
            for h in self.me.hops[d]:
                seen = ((rel[0] + h[0]) % self.me.zc, (rel[1] + h[1]) % 2, (rel[2] + h[2]) % 2)
                pltpu.make_async_remote_copy(
                    src_ref=here, dst_ref=there, send_sem=self.send.at[g, p], recv_sem=self.recv.at[g, p, self.index[seen]],
                    device_id=self.me.device(*h), device_id_type=MESH).start()
        pltpu.make_async_remote_copy(
            src_ref=here, dst_ref=there, send_sem=self.sib_send.at[g, p], recv_sem=self.sib_recv.at[g, p, rel[0]],
            device_id=self.me.device(0, 0, 0, 1), device_id_type=MESH).start()

    def begin(self, g):
        for p in range(len(PARTS[g])):
            self.forward(g, p, (0, 0, 0))
        pltpu.make_async_copy(self.src.at[g], self.block(g, (0, 0, 0), 0, ROWS), self.own.at[g]).start()

    def ticks(self, g):
        soon, late = [], []
        for deep in (1, 2, 3):
            for rel in self.all:
                if sum(1 for v in rel if v) == deep:
                    now = [p for p, part in enumerate(PARTS[g]) if part[2][-1] != "z" or not rel[0]]
                    if now:
                        soon.append(functools.partial(self.tick, g, rel, now))
                    if len(now) < len(PARTS[g]):
                        late.append(functools.partial(self.tick, g, rel, [p for p in range(len(PARTS[g])) if p not in now]))
        return soon, late

    def tick(self, g, rel, parts):
        for p in parts:
            wait_rows(self.out.at[g], PARTS[g][p][1], self.recv.at[g, p, self.index[rel]])
            self.forward(g, p, rel)

    def arrived(self, g, levels):
        if 0 in levels:
            pltpu.make_async_copy(self.src.at[g], self.src.at[g], self.own.at[g]).wait()
        for p, (r0, rows, _) in enumerate(PARTS[g]):
            for rz in levels:
                wait_rows(self.out.at[g], 4 * rows, self.sib_recv.at[g, p, rz])

    def finish(self, g):
        for p, (r0, rows, _) in enumerate(PARTS[g]):
            wait_rows(self.out.at[g], (4 * self.me.zc - 1) * rows, self.send.at[g, p])
            wait_rows(self.out.at[g], 4 * self.me.zc * rows, self.sib_send.at[g, p])


class Blocks:
    def __init__(self, full, buf, sems, order):
        self.full, self.buf, self.sems, self.order = full, buf, sems, order

    def fetch(self, i):
        if i < len(self.order):
            g, b = self.order[i]
            pltpu.make_async_copy(self.full.at[g, b], self.buf.at[i % 2], self.sems.at[i % 2]).start()

    def take(self, i):
        g, b = self.order[i]
        pltpu.make_async_copy(self.full.at[g, b], self.buf.at[i % 2], self.sems.at[i % 2]).wait()
        return self.buf.at[i % 2]


def standard(v):
    center = v - jnp.mean(v, axis=-1, keepdims=True)
    spread = lax.rsqrt(jnp.mean(center * center, axis=-1, keepdims=True) + EPSILON)
    return center * spread, spread


def gelu(v):
    return 0.5 * v * (1.0 + jnp.tanh(0.7978845608 * (v + 0.044715 * v * v * v)))


def gelu_slope(v):
    t = jnp.tanh(0.7978845608 * (v + 0.044715 * v * v * v))
    return 0.5 * (1.0 + t) + 0.5 * v * (1.0 - t * t) * 0.7978845608 * (1.0 + 3.0 * 0.044715 * v * v)


def turn(ref, out):
    def body(cols):
        out[cols, :] = ref[:, cols].astype(F32).T.astype(BF16)
    each_columns(body)


def table_picker(x, entries, line):
    entry = lax.broadcasted_iota(jnp.int32, (entries, line), 0) % 128
    lane = lax.broadcasted_iota(jnp.int32, (entries, line), 1)
    return jnp.where(entry == x - lane % GRID + GRID - 1, 1.0, 0.0).astype(BF16)


def row_picker(line):
    row = lax.broadcasted_iota(jnp.int32, (2 * GRID, line), 0)
    lane = lax.broadcasted_iota(jnp.int32, (2 * GRID, line), 1)
    return jnp.where(row == 2 * GRID - 2 - lane // GRID, 1.0, 0.0).astype(F32)


def forward_kernel(zc, qkv, out, up, down, silu_out, ada, bias_row, token_row, kept, keep, table, cotangent,
                   full, one_t_out, projected_out, att_out, mixed_t_out, branch_out, stream_mid_out, two_t_out, hidden_out, sum_down_out, stream_in_out,
                   block_out, mod, silu_part, selector, gate_sum,
                   one_t, projected, att, mixed_t, branch, stream_mid, two_t, hidden, sum_down, stream_in, save_sem,
                   act_t, acts_sib, grad_down, grad_down_sib, src, pieces, landed, rows_wide, turn_send, turn_recv, pair_send, pair_recv,
                   wbuf, normed, wide_one, act, turned, silu_got, mod_rows, mod_sib, mod_got, kept_got, spread_bias,
                   send, recv, sib_send, sib_recv, own, wsem, small_send, small_recv):
    me = Place(zc)
    place = me.x * 2 + me.c
    width = out.shape[0]
    for n in range(4):
        piece = qkv[:, n * D:(n + 1) * D] if n < 3 else out[...]
        pieces[0, n] = piece.astype(BF16)
    me.greet()
    turns = {}

    def spread_rows(g):
        for k in range(1, 4):
            n = (place + k) % 4
            turns[g, k] = pltpu.make_async_remote_copy(
                src_ref=pieces.at[g, n], dst_ref=landed.at[g, place], send_sem=turn_send.at[g, k - 1], recv_sem=turn_recv.at[g, k - 1],
                device_id=(me.line // 4, n), device_id_type=MESH)
            turns[g, k].start()
        landed[g, place] = pieces[g, place]

    def join_rows(g):
        for k in range(1, 4):
            turns[g, k].wait_recv()
        for n in range(4):
            rows_wide[n * width:(n + 1) * width, :] = landed[g, n].astype(F32)
        src[g] = rows_wide[...].astype(BF16)

    spread_rows(0)
    net = Gather(me, src, full, (send, recv, sib_send, sib_recv, own))
    blocks = Blocks(full, wbuf, wsem, [(0, 0), (0, 1), (0, 2), (0, 3), (1, 0), (1, 1), (1, 2), (1, 3)])
    saves = []

    def save(here, there):
        copy = pltpu.make_async_copy(here, there, save_sem.at[len(saves)])
        copy.start()
        saves.append(copy)

    core_line = me.turned(me.line)
    me.exchange(lambda t: silu_out.at[t], silu_got.at[core_line], small_send.at[0], small_recv.at[0])
    for n in range(4):
        pieces[1, n] = up[:, n * D:(n + 1) * D].astype(BF16)
    join_rows(0)
    net.begin(0)
    spread_rows(1)
    src[2] = down[...].astype(BF16)
    me.exchange(lambda t: kept.at[t], kept_got.at[me.line], small_send.at[1], small_recv.at[1])
    silu_got[core_line] = silu_out[me.line]
    kept_got[me.line] = kept[me.line]
    ticks, _ = net.ticks(0)

    me.exchanged(silu_got, small_recv.at[0])
    silu_part[...] = silu_got[:, 0, :]
    mine = silu_part[:, : ada.shape[0]].astype(BF16)
    def mod_column(j, carry):
        lanes = pl.ds(pl.multiple_of(j * 128, 128), 128)
        v = jnp.dot(mine, ada[:, lanes].astype(BF16), preferred_element_type=F32) + bias_row[:, lanes]
        mod_rows[:, pl.ds(j, 1), :] = v[:, None, :]
        return carry
    lax.fori_loop(0, 54, mod_column, 0)
    def token_column(j, carry):
        v = jnp.broadcast_to(token_row[:, pl.ds(pl.multiple_of(j * 128, 128), 128)], (me.count, 128))
        mod_rows[:, pl.ds(54 + j, 1), :] = v[:, None, :]
        return carry
    lax.fori_loop(0, 9, token_column, 0)
    mod_rows[:, 63:64, :] = jnp.zeros((me.count, 1, 128), F32)
    half = me.count // 2
    chip = me.line // 2
    mod_swap = pltpu.make_async_remote_copy(
        src_ref=mod_rows.at[pl.ds((1 - me.c) * half, half)], dst_ref=mod_sib, send_sem=small_send.at[3], recv_sem=small_recv.at[3],
        device_id=me.device(0, 0, 0, 1), device_id_type=MESH)
    mod_swap.start()
    for _ in range(3):
        ticks.pop(0)()
    mod_swap.wait()
    def both(i, carry):
        mod_sib[i] += mod_rows[me.c * half + i]
        return carry
    lax.fori_loop(0, half, both, 0)
    me.exchange_chips(lambda t: mod_sib.at[t], mod_got.at[chip], small_send.at[2], small_recv.at[2])
    mod_got[chip] = mod_sib[chip]
    for _ in range(2):
        ticks.pop(0)()

    v = table[...]
    high = v.astype(BF16)
    rest = v - high.astype(F32)
    middle = rest.astype(BF16)
    halves = jnp.concatenate([high, middle, (rest - middle.astype(F32)).astype(BF16)], axis=1)
    picked_rows = row_picker(SPAN)
    def spread(x, carry):
        got = jnp.dot(halves, table_picker(x, 384, SPAN), preferred_element_type=F32)
        spread_bias[x] = jnp.sum(got.reshape(HEADS, 2 * GRID, SPAN) * picked_rows[None], axis=1)
        return carry
    lax.fori_loop(0, GRID // 2, spread, 0)
    for _ in range(4):
        ticks.pop(0)()
    lax.fori_loop(GRID // 2, GRID, spread, 0)

    row = lax.broadcasted_iota(jnp.int32, (PATCHES, PATCHES), 0)
    column = lax.broadcasted_iota(jnp.int32, (PATCHES, PATCHES), 1)
    kept_here = keep[...].astype(F32)
    before = jnp.where(row >= column, 1.0, 0.0).astype(BF16)
    ranks = jnp.dot(before, jnp.broadcast_to(kept_here, (PATCHES, 128)).astype(BF16), preferred_element_type=F32)
    ranks = ranks[:, :1].astype(jnp.int32) - 1
    slot = (ranks % me.count) * 8 + ranks // me.count
    selector[...] = jnp.where((keep[...] == 1) & (slot == column), 1.0, 0.0).astype(BF16)
    me.exchanged(mod_got, small_recv.at[2])
    total = mod_got[0]
    for i in range(1, half):
        total += mod_got[i]
    for i in range(63):
        mod[i // 9:i // 9 + 1, i % 9 * 128:(i % 9 + 1) * 128] = total[i:i + 1, :]
    me.exchanged(kept_got, small_recv.at[1])
    def put(cols):
        v = jnp.dot(selector[...], kept_got[:, :, cols].reshape(me.count * 8, -1), preferred_element_type=F32)
        stream_in[:, cols] = v + (1.0 - kept_here) * mod[6:7, cols]
    each_columns(put)

    def norm_one(rows):
        n, _ = standard(stream_in[rows, :])
        normed[rows, :] = (n * (1.0 + mod[1:2, :]) + mod[0:1, :]).astype(BF16)
    each_rows(PATCHES, 32, norm_one)
    turn(normed, one_t)
    def gated(rows):
        grad_down[rows, :] = (mod[5:6, :] * cotangent[rows, :].astype(F32)).astype(BF16)
    each_rows(PATCHES, 32, gated)
    def pair(here, there, i):
        copy = pltpu.make_async_remote_copy(
            src_ref=here, dst_ref=there, send_sem=pair_send.at[i], recv_sem=pair_recv.at[i], device_id=me.device(0, 0, 0, 1), device_id_type=MESH)
        copy.start()
        return copy
    grad_pair = pair(grad_down, grad_down_sib, 0)
    save(stream_in, stream_in_out)
    save(one_t, one_t_out)
    join_rows(1)
    net.begin(1)
    for tick in ticks:
        tick()
    net.arrived(0, range(zc))
    ticks, late = net.ticks(1)
    blocks.fetch(0)
    blocks.fetch(1)
    for b in range(3):
        w = blocks.take(b)
        def product(cols):
            projected[b, :, cols] = jnp.dot(normed[...], w[:, cols], preferred_element_type=F32).astype(BF16)
        each_columns(product)
        blocks.fetch(b + 2) if b + 2 < 4 else None
        ticks.pop(0)()
    save(projected, projected_out)
    wide_one[...] = jnp.zeros_like(wide_one)
    for head in range(HEADS):
        lanes, mask = window(head)
        q = projected[0, :, lanes] * mask.astype(BF16)
        scores = lax.dot_general(q, projected[1, :, lanes], NT, preferred_element_type=F32) * FACTOR
        u = spread_bias[:, head, :]
        bias = jnp.concatenate(
            [pltpu.roll(u, (SPAN - (GRID - 1 - r) * GRID) % SPAN, 1)[:, :PATCHES] for r in range(GRID)], axis=0)
        scores = scores + bias
        e = jnp.exp(scores - jnp.max(scores, axis=-1, keepdims=True))
        weights = e * (1.0 / jnp.sum(e, axis=-1, keepdims=True))
        att[head] = weights
        got = jnp.dot(weights.astype(BF16), projected[2, :, lanes], preferred_element_type=F32)
        wide_one[:, lanes] += got * mask
        if head % 2 and ticks:
            ticks.pop(0)()
        if head == 11:
            net.begin(2)
    normed[...] = wide_one[...].astype(BF16)
    turn(normed, mixed_t)
    save(att, att_out)
    save(mixed_t, mixed_t_out)
    w = blocks.take(3)
    def product(cols):
        branch[:, cols] = jnp.dot(normed[...], w[:, cols], preferred_element_type=F32)
    each_columns(product)
    def mid(rows):
        v = stream_in[rows, :] + mod[2:3, :] * branch[rows, :]
        stream_mid[rows, :] = v
        n, _ = standard(v)
        normed[rows, :] = (n * (1.0 + mod[4:5, :]) + mod[3:4, :]).astype(BF16)
    each_rows(PATCHES, 32, mid)
    turn(normed, two_t)
    save(branch, branch_out)
    save(stream_mid, stream_mid_out)
    save(two_t, two_t_out)
    for tick in ticks + late:
        tick()
    net.arrived(1, range(zc))
    ticks, late = net.ticks(2)
    def down_block(i):
        w = blocks.take(i)
        part = act.at[blocks.order[i][1]]
        def product(cols):
            v = jnp.dot(part[...], w[:, cols], preferred_element_type=F32)
            wide_one[:, cols] = v if i == 8 else wide_one[:, cols] + v
        each_columns(product)
    blocks.fetch(4)
    blocks.fetch(5)
    def turn_units(ref, b):
        turn(ref, turned)
        for i in range(8):
            unit = b * 8 + i
            w, n = unit // 4, unit % 4
            act_t[n % 2, n // 2, w * ROWS:(w + 1) * ROWS, :] = turned[i * ROWS:(i + 1) * ROWS, :]
    for b in range(4):
        w = blocks.take(4 + b)
        def product(cols):
            v = jnp.dot(normed[...], w[:, cols], preferred_element_type=F32)
            hidden[b, :, cols] = v
        each_columns(product)
        if b < 2:
            blocks.fetch(6 + b)
        def bend(rows):
            act[b, rows, :] = gelu(hidden[b, rows, :]).astype(BF16)
        each_rows(PATCHES, 32, bend)
        turn_units(act.at[b], b)
        save(hidden.at[b], hidden_out.at[b])
        for _ in range(2):
            ticks.pop(0)()
    act_pair = pair(act_t.at[1 - me.c], acts_sib, 1)
    def down_grad(j):
        def body(cols):
            v = jnp.dot(act_t[me.c, j], grad_down[:, cols], preferred_element_type=F32)
            sum_down[j, :, cols] = (v + jnp.dot(acts_sib[j], grad_down_sib[:, cols], preferred_element_type=F32)).astype(BF16)
        each_columns(body)
        save(sum_down.at[j], sum_down_out.at[j])
    for i in range(zc):
        blocks.order.append((2, lax.rem(me.z + zc - i, zc)))
    last_ticks = [[t for t in ticks + late if t.args[1][0] == i] for i in range(zc)]
    middle = [t for t in ticks if t.args[1][0] and sum(map(bool, t.args[1])) < 3]
    for i in range(zc):
        for t in last_ticks[i]:
            if t not in middle:
                t()
        if i == 0:
            for t in middle:
                t()
        if i == 0:
            grad_pair.wait_recv()
            act_pair.wait_recv()
        if i < 2:
            down_grad(i)
        net.arrived(2, [i])
        blocks.fetch(8 + i)
        if i:
            down_block(7 + i)
    down_block(7 + zc)
    gate_sum[...] = jnp.zeros_like(gate_sum)
    def last(rows):
        v = wide_one[rows, :]
        block_out[rows, :] = (stream_mid[rows, :] + mod[5:6, :] * v).astype(BF16)
        gate_sum[...] += jnp.sum(cotangent[rows, :].astype(F32) * v, axis=0, keepdims=True)
    each_rows(PATCHES, 32, last)
    for copy in saves:
        copy.wait()
    for copy in turns.values():
        copy.wait_send()
    grad_pair.wait_send()
    act_pair.wait_send()
    for g in range(3):
        net.finish(g)
    for i, got in enumerate((silu_got, kept_got, mod_got)):
        me.exchanged(got, small_send.at[i])


def run_forward(qkv, out, up, down, silu_out, ada, bias_row, token_row, kept, keep, table, cotangent, zc):
    vmem = pl.BlockSpec(memory_space=pltpu.VMEM)
    hbm = pl.BlockSpec(memory_space=pl.ANY)
    parts, count = max(map(len, PARTS)), 8 * zc
    shape = jax.ShapeDtypeStruct
    dma = pltpu.SemaphoreType.DMA
    width = out.shape[0]
    kept_on = [((D, PATCHES), BF16), ((3, PATCHES, D), BF16), ((HEADS, PATCHES, PATCHES), F32), ((D, PATCHES), BF16), ((PATCHES, D), F32),
               ((PATCHES, D), F32), ((D, PATCHES), BF16), ((4, PATCHES, D), F32), ((2, D, D), BF16), ((PATCHES, D), F32)]
    return pl.pallas_call(
        functools.partial(forward_kernel, zc),
        out_shape=[shape((3, 4, D, D), BF16)] + [shape(*k) for k in kept_on] + [
            shape((PATCHES, D), BF16), shape((8, D), F32), shape((count, 128), F32), shape((PATCHES, PATCHES), BF16), shape((1, D), F32)],
        in_specs=[vmem] * 12,
        out_specs=[hbm] * 11 + [vmem] * 5,
        scratch_shapes=[pltpu.VMEM(*k) for k in kept_on] + [
            dma((14,)),
            pltpu.VMEM((2, 2, D, PATCHES), BF16), pltpu.VMEM((2, D, PATCHES), BF16), pltpu.VMEM((PATCHES, D), BF16), pltpu.VMEM((PATCHES, D), BF16),
            pltpu.VMEM((3, ROWS, D), BF16), pltpu.VMEM((2, 4, width, D), BF16), pltpu.VMEM((2, 4, width, D), BF16), pltpu.VMEM((ROWS, D), F32),
            dma((2, 3)), dma((2, 3)), dma((2,)), dma((2,)),
            pltpu.VMEM((2, D, D), BF16), pltpu.VMEM((PATCHES, D), BF16), pltpu.VMEM((PATCHES, D), F32), pltpu.VMEM((4, PATCHES, D), BF16), pltpu.VMEM((D, PATCHES), BF16),
            pltpu.VMEM((count, 8, 128), F32), pltpu.VMEM((count, 64, 128), F32), pltpu.VMEM((count // 2, 64, 128), F32), pltpu.VMEM((count // 2, 64, 128), F32),
            pltpu.VMEM((count, 8, D), BF16), pltpu.VMEM((GRID, HEADS, SPAN), F32),
            dma((3, parts)), dma((3, parts, 4 * zc)), dma((3, parts)), dma((3, parts, zc)), dma((3,)), dma((2,)), dma((4,)), dma((4,))],
        compiler_params=pltpu.CompilerParams(collective_id=1, has_side_effects=True, vmem_limit_bytes=58 * 1024 * 1024),
        name="forward",
    )(qkv, out, up, down, silu_out, ada, bias_row, token_row, kept, keep, table, cotangent)


RPARTS = (((0, 64, "zxy"), (64, 64, "zyx"), (128, 16, "xyz")),) * 3


def reduce_plan(zc, order):
    live, slots, phases = rels(zc), {}, []
    for j, d in enumerate(order[::-1]):
        sends = [r for r in live if r[AT[d]]]
        live = [r for r in live if not r[AT[d]]]
        hops = list(range(1, zc)) if d == "z" else [1]
        for r in live:
            for k in hops:
                slots[r, j, k] = len(slots)
        phases.append((d, sends, live, hops))
    return phases, slots


class Reduce:
    def __init__(self, me, sums, landed, owned, send, recv):
        self.me, self.sums, self.landed, self.owned, self.send_sem, self.recv = me, sums, landed, owned, send, recv
        self.plans = [[reduce_plan(me.zc, part[2]) for part in parts] for parts in RPARTS]
        self.held, self.first = {}, {}
        self.items = [(g, k) for g in (2, 1, 0) for k in list(range(1, me.zc)) + [0]]

    def partial(self, g, p, rel, first=False):
        r0, rows, _ = RPARTS[g][p]
        if (g, p, rel) in self.held:
            return self.landed.at[g, self.held[g, p, rel], pl.ds(r0, rows)]
        w, x = self.me.shifted(*rel)
        return (self.first.get(g, self.sums[g]) if first else self.sums[g]).at[x, pl.ds(pl.multiple_of(w * ROWS + r0, 16), rows)]

    def send(self, g, p, j, rel):
        r0, rows, _ = RPARTS[g][p]
        d = self.plans[g][p][0][j][0]
        k = rel[AT[d]]
        hop = tuple(k if i == AT[d] else 0 for i in range(3))
        there = tuple(0 if i == AT[d] else rel[i] for i in range(3))
        slot = self.plans[g][p][1][there, j, k]
        pltpu.make_async_remote_copy(
            src_ref=self.partial(g, p, rel, j == 0), dst_ref=self.landed.at[g, slot, pl.ds(r0, rows)],
            send_sem=self.send_sem.at[g, p, min(j, 1)], recv_sem=self.recv.at[g, p, slot],
            device_id=self.me.device(*hop), device_id_type=MESH).start()

    def receive(self, g, p, j, rel, final):
        r0, rows, _ = RPARTS[g][p]
        slots = [self.plans[g][p][1][rel, j, k] for k in self.plans[g][p][0][j][3]]
        for s in slots:
            ref = self.landed.at[g, s, pl.ds(r0, rows)]
            pltpu.make_async_copy(ref, ref, self.recv.at[g, p, s]).wait()
        mine = self.partial(g, p, rel)
        def body(i, carry):
            at = pl.ds(pl.multiple_of(r0 + i * 16, 16), 16)
            total = mine[pl.ds(pl.multiple_of(i * 16, 16), 16), :].astype(F32)
            for s in slots:
                total += self.landed[g, s, at, :].astype(F32)
            if final:
                self.owned[g][at, :] = total.astype(self.owned[g].dtype)
            else:
                self.landed[g, slots[0], at, :] = total.astype(BF16)
            return carry
        lax.fori_loop(0, rows // 16, body, 0)
        self.held[g, p, rel] = slots[0]

    def stage(self, j, g, k):
        for p in range(len(RPARTS[g])):
            phases = self.plans[g][p][0]
            lowered = [r for r in phases[j - 1][2] if r[0] == k] if j else []
            sends = [r for r in phases[j][1] if r[0] == k] if j < 3 else []
            for rel in sorted(lowered, key=lambda r: r not in sends):
                self.receive(g, p, j - 1, rel, j == 3)
                if rel in sends:
                    self.send(g, p, j, rel)
            if j == 0:
                for rel in sends:
                    self.send(g, p, 0, rel)

    def step(self, t):
        for j in range(4):
            if 0 <= t - j < len(self.items):
                self.stage(j, *self.items[t - j])

    def steps(self):
        return len(self.items) + 3

    def sent(self, g, late):
        for p, (r0, rows, _) in enumerate(RPARTS[g]):
            phases = self.plans[g][p][0]
            count = sum(len(phases[j][1]) for j in ((1, 2) if late else (0,)))
            ref = self.landed.at[g, pl.ds(0, count), pl.ds(r0, rows)]
            pltpu.make_async_copy(ref, ref, self.send_sem.at[g, p, int(late)]).wait()


class Fold:
    def __init__(self, me, table, token, lands, tokens, whole, send, recv):
        self.me, self.table, self.token, self.lands, self.whole = me, table, token, lands, whole
        self.token_land, self.token_out = tokens
        self.send, self.recv, self.started = send, recv, []
        self.steps, lo, size = [], 0, table.shape[0]
        for bit, many, peers in ((me.c, 2, [(0, 0, 0, 1)]), (me.x, 2, [(0, 0, 1)]), (me.y, 2, [(0, 1, 0)]),
                                 (me.z, me.zc, [(k, 0, 0) for k in range(1, me.zc)])):
            part = size // many
            self.steps.append((lo, size, part, bit, many, peers))
            lo, size = lo + bit * part, part
        self.lo = lo

    def rows(self, ref, at, count):
        return ref.at[pl.ds(pl.multiple_of(at, 8), count)]

    def remote(self, src, dst, which, peer):
        copy = pltpu.make_async_remote_copy(
            src_ref=src, dst_ref=dst, send_sem=self.send.at[which], recv_sem=self.recv.at[which],
            device_id=self.me.device(*peer), device_id_type=MESH)
        copy.start()
        self.started.append(copy)

    def give(self, i):
        lo, size, part, bit, many, peers = self.steps[i]
        self.token_out[i] = self.token[...]
        for k, peer in enumerate(peers):
            other = lax.rem(bit + k + 1, many)
            land = self.lands[i].at[k] if many > 2 or i == 3 else self.lands[i]
            self.remote(self.rows(self.table, lo + other * part, part), land, (i, 0, k), peer)
            self.remote(self.token_out.at[i], self.token_land.at[i, k], (i, 1, k), peer)

    def take(self, i):
        lo, size, part, bit, many, peers = self.steps[i]
        mine = pl.ds(pl.multiple_of(lo + bit * part, 8), part)
        for k in range(len(peers)):
            land = self.lands[i].at[k] if many > 2 or i == 3 else self.lands[i]
            pltpu.make_async_copy(land, land, self.recv.at[i, 0, k]).wait()
            pltpu.make_async_copy(self.token_land.at[i, k], self.token_land.at[i, k], self.recv.at[i, 1, k]).wait()
            self.table[mine, :] += land[...]
            self.token[...] += self.token_land[i, k]
        if i == 3:
            self.whole[mine, :] = self.table[mine, :]

    def hand(self, i):
        lo, size, part, bit, many, peers = self.steps[i]
        mine = self.rows(self.whole, lo + bit * part, part)
        for k, peer in enumerate(peers):
            self.remote(mine, mine, (4 + i, 0, k), peer)

    def handed(self, i):
        lo, size, part, bit, many, peers = self.steps[i]
        some = self.rows(self.whole, 0, part)
        for k in range(len(peers)):
            pltpu.make_async_copy(some, some, self.recv.at[4 + i, 0, k]).wait()

    def finish(self):
        for copy in self.started:
            copy.wait_send()


def backward_kernel(zc, full, mod, cotangent, stream_in, stream_mid, branch, projected, att, hidden, one_t, mixed_t, two_t, sum_down,
                    ada, silu_part, selector, keep, gate_sum,
                    owned_down, owned_turned, grad_ada, mod_total, silu_back, kept_grad, table_grad, token_grad,
                    sum_a, sum_b, landed, wbuf, left, left_sib, grad_down, right_sib, bent, rights, grad_mixed,
                    stream, hid, att_buf, spread_grad, grad_in, small,
                    owned_out, lines, line_low, mod_got, mod_flat, ada_wide, ada_low, silu_out, kept_out, table_sum, token_sum,
                    land_core, land_x, land_y, land_z, land_token, token_out, rights_out,
                    send, recv, sib_send, sib_recv, wsem, lsem, hsem, asem, ssem, small_send, small_recv, turn_send, turn_recv, fold_send, fold_recv):
    me = Place(zc)
    me.greet()
    c = me.c
    net = Reduce(me, {2: sum_a, 1: sum_b, 0: sum_a}, landed, {2: owned_down, 1: owned_out.at[1], 0: owned_out.at[0]}, send, recv)
    blocks = Blocks(full, wbuf, wsem, [(2, 0), (2, 1), (2, 2), (2, 3), (1, 0), (1, 1), (1, 2), (1, 3), (0, 3), (0, 0), (0, 1), (0, 2)])
    swaps = []

    def swap(src, dst):
        i = len(swaps)
        swaps.append(pltpu.make_async_remote_copy(
            src_ref=src, dst_ref=dst, send_sem=sib_send.at[i], recv_sem=sib_recv.at[i],
            device_id=me.device(0, 0, 0, 1), device_id_type=MESH))
        swaps[-1].start()
        return swaps[-1]

    def load(src, dst, sem):
        copy = pltpu.make_async_copy(src, dst, sem)
        copy.start()
        return copy

    net.first[2] = sum_down
    net.step(0)
    sum_load = load(sum_down, sum_a, lsem.at[0])
    blocks.fetch(0)
    blocks.fetch(1)
    hid_load = load(hidden.at[0], hid, hsem.at[0])

    def down(rows):
        grad_down[rows, :] = (mod[5:6, :] * cotangent[rows, :].astype(F32)).astype(BF16)
    each_rows(PATCHES, 32, down)
    ada_load = load(ada, ada_wide, lsem.at[4])
    left_loads = [load(ref, left.at[i], lsem.at[1 + i]) for i, ref in enumerate((one_t, mixed_t, two_t))]
    left_swaps = [swap(ref, left_sib.at[i]) for i, ref in enumerate((one_t, mixed_t, two_t))]
    mid_load = load(stream_mid, stream.at[0], ssem.at[0])

    def weight_grad(total, mine, mine_right, theirs, their_right):
        def body(cols):
            v = jnp.dot(mine[...], mine_right[:, cols], preferred_element_type=F32)
            total[:, cols] = (v + jnp.dot(theirs[...], their_right[:, cols], preferred_element_type=F32)).astype(BF16)
        each_columns(body)

    sum_load.wait()
    for b in range(4):
        w = blocks.take(b)
        hid_load.wait()
        def bend(cols):
            v = lax.dot_general(grad_down[...], w[cols, :], NT, preferred_element_type=F32)
            bent[b, :, cols] = (v * gelu_slope(hid[:, cols])).astype(BF16)
        each_columns(bend)
        blocks.fetch(b + 2)
        if b < 3:
            hid_load = load(hidden.at[b + 1], hid, hsem.at[0])
        if b in (1, 3):
            net.step((b + 1) // 2)
    branch_load = load(branch, hid, ssem.at[1])
    bent_swaps = [swap(bent.at[1 - c], right_sib.at[0]), swap(bent.at[3 - c], right_sib.at[1])]
    for copy in left_loads:
        copy.wait()
    for copy in left_swaps + bent_swaps:
        copy.wait_recv()
    for j in range(2):
        weight_grad(sum_b.at[j], left.at[2], bent.at[2 * j + c], left_sib.at[2], right_sib.at[j])
    net.step(3)
    for b in range(4):
        w = blocks.take(4 + b)
        def back(cols):
            v = lax.dot_general(bent[b], w[cols, :], NT, preferred_element_type=F32)
            grad_in[:, cols] = v if b == 0 else grad_in[:, cols] + v
        each_columns(back)
        blocks.fetch(6 + b)
    mid_load.wait()
    branch_load.wait()
    small[...] = jnp.zeros_like(small)

    def norm_back(rows, stream_rows, scale, shift_at, scale_at):
        n, spread = standard(stream_rows)
        e = grad_in[rows, :]
        f = e * (1.0 + scale)
        small[shift_at:shift_at + 1, :] += jnp.sum(e, axis=0, keepdims=True)
        small[scale_at:scale_at + 1, :] += jnp.sum(e * n, axis=0, keepdims=True)
        return (f - jnp.mean(f, axis=-1, keepdims=True) - n * jnp.mean(f * n, axis=-1, keepdims=True)) * spread

    def back_two(rows):
        v = cotangent[rows, :].astype(F32) + norm_back(rows, stream[0, rows, :], mod[4:5, :], 3, 4)
        small[2:3, :] += jnp.sum(v * hid[rows, :], axis=0, keepdims=True)
        hid[rows, :] = v
        rights[3, rows, :] = (mod[2:3, :] * v).astype(BF16)
    each_rows(PATCHES, 32, back_two)
    in_load = load(stream_in, stream.at[0], ssem.at[0])
    net.step(4)
    att_load = load(att.at[0], att_buf.at[0], asem.at[0])
    w = blocks.take(8)
    def mixed_back(cols):
        grad_mixed[:, cols] = lax.dot_general(rights[3], w[cols, :], NT, preferred_element_type=F32).astype(BF16)
    each_columns(mixed_back)
    blocks.fetch(10)
    for b in range(3):
        rights[b] = jnp.zeros((PATCHES, D), BF16)
    net.step(5)
    for head in range(HEADS):
        att_load.wait()
        if head + 1 < HEADS:
            att_load = load(att.at[head + 1], att_buf.at[(head + 1) % 2], asem.at[(head + 1) % 2])
        lanes, mask = window(head)
        weights = att_buf[head % 2]
        low = weights.astype(BF16)
        given = grad_mixed[:, lanes]
        grad_att = lax.dot_general(given * mask.astype(BF16), projected[2, :, lanes], NT, preferred_element_type=F32)
        v = lax.dot_general(low, given, TN, preferred_element_type=F32)
        rights[2, :, lanes] += (v * mask).astype(BF16)
        scores = weights * (grad_att - jnp.sum(weights * grad_att, axis=-1, keepdims=True))
        scores_low = scores.astype(BF16)
        v = jnp.dot(scores_low, projected[1, :, lanes], preferred_element_type=F32) * FACTOR
        rights[0, :, lanes] += (v * mask).astype(BF16)
        v = lax.dot_general(scores_low, projected[0, :, lanes], TN, preferred_element_type=F32) * FACTOR
        rights[1, :, lanes] += (v * mask).astype(BF16)
        rounded = scores_low.astype(F32)
        total = jnp.zeros((GRID, SPAN), F32)
        for r in range(GRID):
            rows = jnp.concatenate([rounded[r * GRID:(r + 1) * GRID], jnp.zeros((GRID, SPAN - PATCHES), F32)], axis=1)
            total += pltpu.roll(rows, (GRID - 1 - r) * GRID, 1)
        spread_grad[:, head, :] = total
        if head in (7, 15):
            net.step(6 + head // 8)
    end_swaps = [swap(rights.at[1 - c], right_sib.at[2]), swap(rights.at[3 - c], right_sib.at[3])]
    for b in range(3):
        w = blocks.take(9 + b)
        def back(cols):
            v = lax.dot_general(rights[b], w[cols, :], NT, preferred_element_type=F32)
            grad_in[:, cols] = v if b == 0 else grad_in[:, cols] + v
        each_columns(back)
        blocks.fetch(11 + b)
    in_load.wait()
    def back_one(rows):
        v = norm_back(rows, stream[0, rows, :], mod[1:2, :], 0, 1)
        grad_in[rows, :] = hid[rows, :] + v
    each_rows(PATCHES, 32, back_one)
    for v in range(6):
        for i in range(9):
            piece = small[v:v + 1, i * 128:(i + 1) * 128] if v < 5 else gate_sum[:, i * 128:(i + 1) * 128]
            lines[v * 9 + i:v * 9 + i + 1, :] = piece
    lines[54:64, :] = jnp.zeros((10, 128), F32)
    line_low[...] = lines[...].astype(BF16)
    half, chip = me.count // 2, me.line // 2
    mine_at = c * half
    me.exchange_chips(lambda t: line_low, mod_got.at[mine_at + chip], small_send.at[0], small_recv.at[0])
    mod_got[mine_at + chip] = line_low[...]
    grad_mixed[...] = grad_in[...].astype(BF16)
    def put_back(cols):
        v = lax.dot_general(selector[...], grad_mixed[:, cols], TN, preferred_element_type=F32).astype(BF16)
        kept_out[:, :, cols] = v.reshape(me.count, 8, -1)
    each_columns(put_back)
    me.exchange(lambda t: kept_out.at[t], kept_grad.at[me.line], small_send.at[1], small_recv.at[1])
    kept_own = load(kept_out.at[me.line], kept_grad.at[me.line], ssem.at[1])
    net.sent(2, False)
    for copy in end_swaps:
        copy.wait_recv()
    weight_grad(sum_a.at[0], left.at[0], rights.at[c], left_sib.at[0], right_sib.at[2])
    weight_grad(sum_a.at[1], left.at[c], rights.at[2 + c], left_sib.at[c], right_sib.at[3])
    net.step(8)

    masked = 1.0 - keep[...].astype(F32)
    token = jnp.sum(masked * grad_in[...], axis=0, keepdims=True)
    for i in range(9):
        token_sum[i:i + 1, :] = token[:, i * 128:(i + 1) * 128]
    token_sum[9:16, :] = jnp.zeros((7, 128), F32)
    picked_rows = row_picker(SPAN)
    table_sum[...] = jnp.zeros_like(table_sum)
    def gather_table(x, carry):
        picker = table_picker(x, 128, SPAN)
        v = (spread_grad[x][:, None, :] * picked_rows[None]).reshape(HEADS * 2 * GRID, SPAN)
        high = v.astype(BF16)
        rest = v - high.astype(F32)
        middle = rest.astype(BF16)
        low = (rest - middle.astype(F32)).astype(BF16)
        for part in (high, middle, low):
            table_sum[...] += lax.dot_general(part, picker, NT, preferred_element_type=F32)
        return carry
    lax.fori_loop(0, GRID, gather_table, 0)
    fold = Fold(me, table_sum, token_sum, (land_core, land_x, land_y, land_z), (land_token, token_out), table_grad, fold_send, fold_recv)
    fold.give(0)
    net.step(9)
    fold.take(0)
    fold.give(1)

    plane = mod_got.at[pl.ds(mine_at, half)]
    me.exchanged(plane, small_recv.at[0])
    mod_swap = pltpu.make_async_remote_copy(
        src_ref=plane, dst_ref=plane, send_sem=small_send.at[2], recv_sem=small_recv.at[2],
        device_id=me.device(0, 0, 0, 1), device_id_type=MESH)
    mod_swap.start()
    ada_load.wait()
    def flat(j, carry):
        lanes = pl.ds(pl.multiple_of(j * 128, 128), 128)
        ada_low[:, lanes] = ada_wide[:, lanes].astype(BF16)
        return carry
    lax.fori_loop(0, 54, flat, 0)
    mod_swap.wait_recv()
    for j in range(54):
        mod_flat[:, j * 128:(j + 1) * 128] = mod_got[:, j, :]
    width = ada.shape[0]
    back_silu = lax.dot_general(mod_flat[...], ada_low[...], NT, preferred_element_type=F32)
    silu_out[...] = jnp.zeros_like(silu_out)
    silu_out[:, 0:1, 0:width] = back_silu[:, None, :]
    me.exchange(lambda t: silu_out.at[me.turned(t)], silu_back.at[me.line], small_send.at[3], small_recv.at[3])
    silu_back[me.line] = silu_out[me.turned(me.line)]
    net.step(10)
    fold.take(1)
    fold.give(2)
    mine = silu_part[:, :width].astype(BF16)
    def outer(j, carry):
        lanes = pl.ds(pl.multiple_of(j * 256, 256), 256)
        grad_ada[:, lanes] = lax.dot_general(mine, mod_flat[:, lanes], TN, preferred_element_type=F32)
        return carry
    lax.fori_loop(0, 27, outer, 0)
    total = jnp.zeros((64, 128), F32)
    for i in range(me.count):
        total += mod_got[i].astype(F32)
    mod_total[...] = total
    net.step(11)
    fold.take(2)
    fold.give(3)
    turns = []

    def turn_rows(g):
        for n in range(4):
            rights_out[n, g] = owned_out[g, n * width:(n + 1) * width, :].astype(BF16)
        for k in range(1, 4):
            n = (me.x * 2 + me.c + k) % 4
            copy = pltpu.make_async_remote_copy(
                src_ref=rights_out.at[n, g], dst_ref=owned_turned.at[me.x * 2 + me.c, g], send_sem=turn_send.at[g, k - 1], recv_sem=turn_recv.at[g, k - 1],
                device_id=(me.line // 4, n), device_id_type=MESH)
            copy.start()
            turns.append(copy)
        owned_turned[me.x * 2 + me.c, g] = rights_out[me.x * 2 + me.c, g]

    turn_rows(1)
    fold.take(3)
    token_grad[...] = token_sum[...]
    fold.hand(3)
    net.step(12)
    fold.handed(3)
    fold.hand(2)
    net.step(13)
    fold.handed(2)
    fold.hand(1)
    net.step(14)
    turn_rows(0)
    fold.handed(1)
    fold.hand(0)
    net.sent(1, False)
    net.sent(0, False)
    for g in range(3):
        net.sent(g, True)
    for copy in swaps:
        copy.wait_send()
    kept_own.wait()
    me.exchanged(kept_grad, small_recv.at[1])
    me.exchanged(silu_back, small_recv.at[3])
    me.exchanged(plane, small_send.at[0])
    me.exchanged(kept_grad, small_send.at[1])
    mod_swap.wait_send()
    me.exchanged(silu_back, small_send.at[3])
    fold.handed(0)
    fold.finish()
    for copy in turns:
        copy.wait()


def run_backward(full, mod, cotangent, stream_in, stream_mid, branch, projected, att, hidden, one_t, mixed_t, two_t, sum_down,
                 ada, silu_part, selector, keep, gate_sum, zc):
    vmem = pl.BlockSpec(memory_space=pltpu.VMEM)
    hbm = pl.BlockSpec(memory_space=pl.ANY)
    parts, count, width = max(map(len, RPARTS)), 8 * zc, ada.shape[0]
    table = HEADS * 2 * GRID
    shape = jax.ShapeDtypeStruct
    dma = pltpu.SemaphoreType.DMA
    return pl.pallas_call(
        functools.partial(backward_kernel, zc),
        out_shape=(shape((ROWS, D), F32), shape((4, 2, width, D), BF16), shape((width, 6 * D), F32), shape((64, 128), F32),
                   shape((count, 8, 128), F32), shape((count, 8, D), BF16), shape((HEADS * 2 * GRID, 128), F32), shape((16, 128), F32)),
        in_specs=[hbm, vmem, vmem, hbm, hbm, hbm, vmem, hbm, hbm, hbm, hbm, hbm, hbm, hbm, vmem, vmem, vmem, vmem],
        out_specs=(vmem, vmem, vmem, vmem, vmem, hbm, vmem, vmem),
        scratch_shapes=[
            pltpu.VMEM((2, D, D), BF16), pltpu.VMEM((2, D, D), BF16), pltpu.VMEM((3, 4 * zc - 1, ROWS, D), BF16),
            pltpu.VMEM((2, D, D), BF16), pltpu.VMEM((3, D, PATCHES), BF16), pltpu.VMEM((3, D, PATCHES), BF16),
            pltpu.VMEM((PATCHES, D), BF16),
            pltpu.VMEM((4, PATCHES, D), BF16), pltpu.VMEM((4, PATCHES, D), BF16), pltpu.VMEM((4, PATCHES, D), BF16),
            pltpu.VMEM((PATCHES, D), BF16), pltpu.VMEM((1, PATCHES, D), F32), pltpu.VMEM((PATCHES, D), F32),
            pltpu.VMEM((2, PATCHES, PATCHES), F32),
            pltpu.VMEM((GRID, HEADS, SPAN), F32), pltpu.VMEM((PATCHES, D), F32), pltpu.VMEM((8, D), F32),
            pltpu.VMEM((2, ROWS, D), F32), pltpu.VMEM((64, 128), F32), pltpu.VMEM((64, 128), BF16), pltpu.VMEM((count, 64, 128), BF16),
            pltpu.VMEM((count, 6 * D), BF16), pltpu.VMEM((width, 6 * D), F32), pltpu.VMEM((width, 6 * D), BF16), pltpu.VMEM((count, 8, 128), F32),
            pltpu.VMEM((count, 8, D), BF16), pltpu.VMEM((table, 128), F32), pltpu.VMEM((16, 128), F32),
            pltpu.VMEM((table // 2, 128), F32), pltpu.VMEM((table // 4, 128), F32), pltpu.VMEM((table // 8, 128), F32),
            pltpu.VMEM((zc - 1, table // 8 // zc, 128), F32), pltpu.VMEM((4, zc - 1, 16, 128), F32), pltpu.VMEM((4, 16, 128), F32), pltpu.VMEM((4, 2, width, D), BF16),
            dma((3, parts, 2)), dma((3, parts, 4 * zc - 1)), dma((7,)), dma((7,)), dma((2,)), dma((5,)), dma((1,)), dma((2,)), dma((2,)),
            dma((4,)), dma((4,)), dma((2, 3)), dma((2, 3)), dma((8, 2, zc - 1)), dma((8, 2, zc - 1))],
        compiler_params=pltpu.CompilerParams(collective_id=2, has_side_effects=True, vmem_limit_bytes=63 * 1024 * 1024),
        name="backward",
    )(full, mod, cotangent, stream_in, stream_mid, branch, projected, att, hidden, one_t, mixed_t, two_t, sum_down,
      ada, silu_part, selector, keep, gate_sum)


AXES = ("wide", "narrow")


def running_rank(keep_flat):
    count = keep_flat.shape[0]
    lower = (lax.broadcasted_iota(jnp.int32, (count, count), 0) >= lax.broadcasted_iota(jnp.int32, (count, count), 1))
    total = jnp.dot(lower.astype(jnp.bfloat16), keep_flat.astype(jnp.bfloat16)[:, None], preferred_element_type=jnp.float32)
    return total[:, 0].astype(jnp.int32) - 1


def per_device_plain(kept_tokens, keep_mask, conditioning, ada_weight, ada_bias, qkv_weight, out_weight, up_weight, down_weight, position_bias, mask_token, cotangent):
    wide_count = lax.axis_size("wide")
    narrow_count = lax.axis_size("narrow")
    devices = wide_count * narrow_count
    slots = kept_tokens.shape[2]
    images = conditioning.shape[0]
    count = images * PATCHES
    rows = qkv_weight.shape[0]
    me = lax.axis_index(AXES)
    factor = 1.0 / math.sqrt(HEAD_DIM)
    low_type = jnp.bfloat16
    wide_type = jnp.float32
    silu_cond = jax.nn.silu(conditioning).astype(low_type)
    small = jnp.concatenate([silu_cond.reshape(-1), ada_bias.astype(low_type), mask_token.astype(low_type)])
    smalls = lax.all_gather(small, AXES, axis=0, tiled=False)
    silu_all = smalls[:, : images * D].reshape(devices * images, D)
    bias_full = smalls[:, images * D : images * D + ada_bias.shape[0]].reshape(-1)
    token_full = smalls[:, images * D + ada_bias.shape[0] :].reshape(-1)
    ada_low = ada_weight.astype(low_type)
    silu_part = lax.dynamic_slice_in_dim(silu_all, me * rows, rows, axis=1)
    mod_part = jnp.dot(silu_part, ada_low, preferred_element_type=wide_type)
    mod_parts = lax.all_to_all(mod_part.reshape(devices, images, 6 * D), AXES, split_axis=0, concat_axis=0, tiled=True)
    modulation = jnp.sum(mod_parts, axis=0) + bias_full.astype(wide_type)[None, :]
    qkv_full = lax.all_gather(qkv_weight.astype(low_type), AXES, axis=0, tiled=True)
    out_full = lax.all_gather(out_weight.astype(low_type), AXES, axis=0, tiled=True)
    up_full = lax.all_gather(up_weight.astype(low_type), AXES, axis=0, tiled=True)
    down_full = lax.all_gather(down_weight.astype(low_type), AXES, axis=0, tiled=True)
    def times_qkv(v):
        return jnp.dot(v, qkv_full, preferred_element_type=wide_type)
    def times_qkv_back(v):
        return jnp.dot(v, qkv_full.T, preferred_element_type=wide_type)
    def times_up(v):
        return jnp.dot(v, up_full, preferred_element_type=wide_type)
    def times_up_back(v):
        return jnp.dot(v, up_full.T, preferred_element_type=wide_type)
    arrived = lax.all_to_all(kept_tokens, AXES, split_axis=1, concat_axis=0, tiled=True)
    received = arrived.reshape(devices * slots, D)
    keep_flat = keep_mask.reshape(count)
    keep_float = keep_flat.astype(wide_type)
    ranks = running_rank(keep_flat)
    target = ranks % devices * slots + ranks // devices
    columns = jnp.arange(devices * slots, dtype=jnp.int32)
    selector = jnp.where((keep_flat[:, None] == 1) & (target[:, None] == columns[None, :]), 1.0, 0.0).astype(wide_type)
    stream_in = jnp.dot(selector.astype(low_type), received, preferred_element_type=wide_type)
    stream_in = stream_in + (1.0 - keep_float)[:, None] * token_full.astype(wide_type)[None, :]
    stream_in = stream_in.reshape(images, PATCHES, D)
    shift_one, scale_one, gate_one, shift_two, scale_two, gate_two = jnp.split(
        modulation[:, None, :], 6, axis=-1
    )
    normed_one = modulate(stream_in, shift_one, scale_one).astype(low_type).reshape(count, D)
    projected = times_qkv(normed_one).astype(low_type)
    projected = projected.reshape(images, PATCHES, 3, HEADS, HEAD_DIM)
    queries = projected[:, :, 0]
    key_rows = projected[:, :, 1]
    value_rows = projected[:, :, 2]
    relative = expand_bias(position_bias, GRID)
    scores = (
        jnp.einsum("iqhd,ikhd->ihqk", queries, key_rows, preferred_element_type=wide_type) * factor
        + relative[None]
    )
    att_weights = jax.nn.softmax(scores, axis=-1)
    att_low = att_weights.astype(low_type)
    mixed = (
        jnp.einsum("ihqk,ikhd->iqhd", att_low, value_rows, preferred_element_type=wide_type)
        .astype(low_type)
        .reshape(count, D)
    )
    branch = jnp.dot(mixed, out_full, preferred_element_type=wide_type).reshape(images, PATCHES, D)
    stream_mid = stream_in + gate_one * branch
    normed_two = modulate(stream_mid, shift_two, scale_two).astype(low_type).reshape(count, D)
    hidden = times_up(normed_two)
    activated = gelu_tanh(hidden).astype(low_type)
    down = jnp.dot(activated, down_full, preferred_element_type=wide_type).reshape(
        images, PATCHES, D
    )
    block_out = (stream_mid + gate_two * down).reshape(count, D).astype(low_type)
    incoming = cotangent.astype(wide_type).reshape(images, PATCHES, D)
    grad_gate_two = jnp.sum(incoming * down, axis=1)
    grad_down = (gate_two * incoming).astype(low_type).reshape(count, D)
    grad_activated = jnp.dot(grad_down, down_full.T, preferred_element_type=wide_type)
    _, gelu_pull = jax.vjp(gelu_tanh, hidden)
    grad_hidden = gelu_pull(grad_activated)[0].astype(low_type)
    grad_normed_two = times_up_back(grad_hidden).reshape(
        images, PATCHES, D
    )
    _, norm_pull_two = jax.vjp(modulate, stream_mid, shift_two, scale_two)
    grad_mid_norm, grad_shift_two, grad_scale_two = norm_pull_two(grad_normed_two)
    grad_mid = incoming + grad_mid_norm
    grad_gate_one = jnp.sum(grad_mid * branch, axis=1)
    grad_branch = (gate_one * grad_mid).astype(low_type).reshape(count, D)
    grad_mixed = jnp.dot(grad_branch, out_full.T, preferred_element_type=wide_type).astype(low_type)
    grad_mixed = grad_mixed.reshape(images, PATCHES, HEADS, HEAD_DIM)
    grad_att = jnp.einsum(
        "iqhd,ikhd->ihqk", grad_mixed, value_rows, preferred_element_type=wide_type
    )
    grad_values = jnp.einsum(
        "ihqk,iqhd->ikhd", att_low, grad_mixed, preferred_element_type=wide_type
    )
    grad_scores = (
        att_weights * (grad_att - jnp.sum(att_weights * grad_att, axis=-1, keepdims=True))
    ).astype(low_type)
    grad_queries = (
        jnp.einsum("ihqk,ikhd->iqhd", grad_scores, key_rows, preferred_element_type=wide_type)
        * factor
    )
    grad_keys = (
        jnp.einsum("ihqk,iqhd->ikhd", grad_scores, queries, preferred_element_type=wide_type)
        * factor
    )
    grad_table = bias_adjoint(jnp.sum(grad_scores.astype(wide_type), axis=0), GRID)
    grad_projected = (
        jnp.stack([grad_queries, grad_keys, grad_values], axis=2)
        .astype(low_type)
        .reshape(count, 3 * D)
    )
    grad_normed_one = times_qkv_back(grad_projected).reshape(
        images, PATCHES, D
    )
    _, norm_pull_one = jax.vjp(modulate, stream_in, shift_one, scale_one)
    grad_in_norm, grad_shift_one, grad_scale_one = norm_pull_one(grad_normed_one)
    grad_in = (grad_mid + grad_in_norm).reshape(count, D)
    grad_modulation = jnp.concatenate(
        [
            grad_shift_one[:, 0],
            grad_scale_one[:, 0],
            grad_gate_one,
            grad_shift_two[:, 0],
            grad_scale_two[:, 0],
            grad_gate_two,
        ],
        axis=-1,
    ).astype(low_type)
    grad_mod_all = lax.all_gather(grad_modulation, AXES, axis=0, tiled=True)
    grad_ada = lax.dot_general(silu_part, grad_mod_all, (((0,), (0,)), ((), ())), preferred_element_type=wide_type)
    bias_share = 6 * D // devices
    sum_bias = jnp.sum(lax.dynamic_slice_in_dim(grad_mod_all, me * bias_share, bias_share, axis=1).astype(wide_type), axis=0)
    silu_parts = lax.dot_general(grad_mod_all, ada_low, (((1,), (1,)), ((), ())), preferred_element_type=wide_type)
    silu_parts = lax.all_to_all(silu_parts.reshape(devices, images, rows), AXES, split_axis=0, concat_axis=0, tiled=True)
    grad_silu = silu_parts.transpose(1, 0, 2).reshape(images, D)
    _, silu_pull = jax.vjp(jax.nn.silu, conditioning)
    grad_cond = silu_pull(grad_silu)[0]
    grad_mask = jnp.sum((1.0 - keep_float)[:, None] * grad_in, axis=0)
    grad_received = jnp.dot(
        selector.T, grad_in, precision=lax.Precision.HIGHEST, preferred_element_type=wide_type
    ).astype(low_type)
    grad_kept = lax.all_to_all(
        grad_received.reshape(devices, 1, slots, D),
        ("wide", "narrow"),
        split_axis=0,
        concat_axis=1,
        tiled=True,
    )
    def scatter(left, right):
        partial = lax.dot_general(left, right, (((0,), (0,)), ((), ())), preferred_element_type=wide_type)
        return lax.psum_scatter(partial.reshape(-1), AXES, scatter_dimension=0, tiled=True).reshape(-1, right.shape[1])
    sum_qkv = scatter(normed_one, grad_projected)
    sum_out = scatter(mixed, grad_branch)
    sum_up = scatter(normed_two, grad_hidden)
    sum_down = scatter(activated, grad_down)
    grad_table_all, mask_whole = lax.psum((grad_table, grad_mask), AXES)
    mask_share = D // devices
    sum_mask = lax.dynamic_slice_in_dim(mask_whole, me * mask_share, mask_share)
    return (block_out, grad_kept, grad_cond, grad_ada, sum_bias, sum_qkv, sum_out, sum_up, sum_down, grad_table_all, sum_mask)


def rounded(v):
    return lax.reduce_precision(v, 8, 7)


def per_device(kept_tokens, keep_mask, conditioning, ada_weight, ada_bias, qkv_weight, out_weight, up_weight, down_weight, position_bias, mask_token, cotangent):
    if kept_tokens.shape[2] > 8 or conditioning.shape[0] != 1:
        return per_device_plain(kept_tokens, keep_mask, conditioning, ada_weight, ada_bias, qkv_weight, out_weight, up_weight, down_weight, position_bias, mask_token, cotangent)
    wide_count = lax.axis_size("wide")
    devices = wide_count * lax.axis_size("narrow")
    slots = kept_tokens.shape[2]
    rows = qkv_weight.shape[0]
    share = ada_bias.shape[0]
    me = lax.axis_index(AXES)
    zc = wide_count // 2
    silu_out = jnp.pad(rounded(jax.nn.silu(conditioning)).reshape(devices, 1, rows), ((0, 0), (0, 7), (0, 128 - rows)))
    bias_row = lax.dynamic_update_slice(jnp.zeros((1, 6 * D), F32), rounded(ada_bias)[None], (0, me * share))
    token_row = lax.dynamic_update_slice(jnp.zeros((1, D), F32), rounded(mask_token)[None], (0, me * rows))
    kept = jnp.pad(kept_tokens.reshape(devices, slots, D), ((0, 0), (0, 8 - slots), (0, 0)))
    table = jnp.pad(position_bias, ((0, 0), (0, 1), (0, 128 - position_bias.shape[2]))).reshape(HEADS * 2 * GRID, 128)
    keep = keep_mask.reshape(PATCHES, 1)
    keep_float = keep.astype(F32)

    (full, one_t, projected, att, mixed_t, branch, stream_mid, two_t, hidden, sum_down_part, stream_in, block_out, mod, silu_part, selector, gate_sum) = run_forward(
        qkv_weight, out_weight, up_weight, down_weight, silu_out, ada_weight, bias_row, token_row, kept, keep, table, cotangent, zc)
    sum_down, turned, grad_ada, mod_total, silu_back, kept_grad, table_grad, token_grad = run_backward(
        full, mod, cotangent, stream_in, stream_mid, branch, projected, att, hidden, one_t, mixed_t, two_t, sum_down_part,
        ada_weight, silu_part, selector, keep, gate_sum, zc)

    sum_bias = lax.dynamic_slice(mod_total[:54].reshape(-1), (me * share,), (share,))
    sum_mask = lax.dynamic_slice(token_grad[:9].reshape(-1), (me * rows,), (rows,))
    _, silu_pull = jax.vjp(jax.nn.silu, conditioning)
    grad_cond = silu_pull(silu_back[:, 0, :rows].reshape(1, D))[0]
    grad_kept = kept_grad[None, :, :slots]
    offsets = position_bias.shape[2]
    grad_table = table_grad.reshape(HEADS, 2 * GRID, 128)[:, :offsets, :offsets]
    sum_qkv = turned[:3, 0].transpose(1, 0, 2).reshape(rows, 3 * D).astype(F32)
    sum_out = turned[3, 0].astype(F32)
    sum_up = turned[:, 1].transpose(1, 0, 2).reshape(rows, FF).astype(F32)
    return (block_out, grad_kept, grad_cond, grad_ada, sum_bias, sum_qkv, sum_out, sum_up, sum_down, grad_table, sum_mask)


def solution(mesh):
    in_specs = (
        P(("wide", "narrow"), None, None, None),
        P(("wide", "narrow"), None),
        P(("wide", "narrow"), None),
        P(("wide", "narrow"), None),
        P(("wide", "narrow")),
        P(("wide", "narrow"), None),
        P(("wide", "narrow"), None),
        P(("wide", "narrow"), None),
        P(("wide", "narrow"), None),
        P(),
        P(("wide", "narrow")),
        P(("wide", "narrow"), None),
    )
    out_specs = (
        P(("wide", "narrow"), None),
        P(("wide", "narrow"), None, None, None),
        P(("wide", "narrow"), None),
        P(("wide", "narrow"), None),
        P(("wide", "narrow")),
        P(("wide", "narrow"), None),
        P(("wide", "narrow"), None),
        P(("wide", "narrow"), None),
        P(("wide", "narrow"), None),
        P(),
        P(("wide", "narrow")),
    )
    shape = dict(mesh.shape)
    rows = D // (shape["wide"] * shape["narrow"])
    fast = shape["narrow"] == 4 and shape["wide"] % 2 == 0 and rows * 4 == ROWS
    return jax.shard_map(
        per_device if fast else per_device_plain, mesh=mesh, in_specs=in_specs, out_specs=out_specs, check_vma=False
    )
```

```python
import functools
import math

import jax
import jax.numpy as jnp
from jax import lax
from jax.experimental import pallas as pl
from jax.experimental.pallas import tpu as pltpu
from jax.sharding import PartitionSpec as P

D = 1152
HEADS = 16
HEAD_DIM = 72
FF = 4608
GRID = 16
PATCHES = 256


EPSILON = 1e-06


def layer_norm(stream):
    center = stream - jnp.mean(stream, axis=-1, keepdims=True)
    variance = jnp.mean(center * center, axis=-1, keepdims=True)
    return center * lax.rsqrt(variance + EPSILON)


def modulate(stream, shift, scale):
    return layer_norm(stream) * (1.0 + scale) + shift


def offset_picker(grid):
    places = jnp.arange(grid, dtype=jnp.int32)
    spread = jnp.arange(2 * grid - 1, dtype=jnp.int32)
    return (
        places[:, None, None] - places[None, :, None] + grid - 1 == spread[None, None, :]
    ).astype(jnp.float32)


def expand_bias(table, grid):
    picker = offset_picker(grid)
    partial_rows = jnp.einsum("yka,had->hykd", picker, table, precision=lax.Precision.HIGHEST)
    expanded = jnp.einsum("hykd,xjd->hyxkj", partial_rows, picker, precision=lax.Precision.HIGHEST)
    return expanded.reshape(table.shape[0], grid * grid, grid * grid)


def bias_adjoint(grad_bias, grid):
    picker = offset_picker(grid)
    shaped = grad_bias.reshape(grad_bias.shape[0], grid, grid, grid, grid)
    partial_rows = jnp.einsum("hyxkj,xjd->hykd", shaped, picker, precision=lax.Precision.HIGHEST)
    return jnp.einsum("hykd,yka->had", partial_rows, picker, precision=lax.Precision.HIGHEST)


def gelu_tanh(value):
    return jax.nn.gelu(value, approximate=True)


MESH = pl.DeviceIdType.MESH
ROWS = 144
PARTS = (
    ((0, 80, "zxy"), (80, 64, "zyx")),
    ((0, 64, "zxy"), (64, 48, "zyx"), (112, 32, "xyz")),
    ((0, 64, "zxy"), (64, 64, "zyx"), (128, 16, "xyz")),
)
AT = {"z": 0, "y": 1, "x": 2}
F32 = jnp.float32
BF16 = jnp.bfloat16
FACTOR = 1.0 / math.sqrt(HEAD_DIM)
NT = (((1,), (1,)), ((), ()))
TN = (((0,), (0,)), ((), ()))
SPAN = 2 * PATCHES


def rels(zc):
    return [(rz, ry, rx) for rz in range(zc) for ry in range(2) for rx in range(2)]


class Place:
    def __init__(self, zc):
        wide = lax.axis_index("wide")
        narrow = lax.axis_index("narrow")
        self.zc, self.wcount = zc, 2 * zc
        self.line, self.count = wide * 4 + narrow, 8 * zc
        self.z, self.y, self.x, self.c = wide // 2, wide % 2, narrow // 2, narrow % 2
        self.hops = {"z": [(k, 0, 0) for k in range(1, zc)], "y": [(0, 1, 0)], "x": [(0, 0, 1)]}

    def shifted(self, rz, ry, rx):
        w = lax.rem(self.z + rz, self.zc) * 2 + (self.y + ry) % 2
        return w, (self.x + rx) % 2

    def device(self, rz, ry, rx, flip=0):
        w, x = self.shifted(rz, ry, rx)
        return w, x * 2 + (self.c + flip) % 2

    def greet(self):
        barrier = pltpu.get_barrier_semaphore()
        def hello(k, carry):
            t = lax.rem(self.line + k, self.count)
            pl.semaphore_signal(barrier, inc=1, device_id=(t // 4, t % 4), device_id_type=MESH)
            return carry
        lax.fori_loop(1, self.count, hello, 0)
        pl.semaphore_wait(barrier, self.count - 1)

    def turned(self, t):
        return t % 2 * (self.count // 2) + t // 2

    def exchange(self, piece, there, send, recv):
        def go(k, carry):
            t = lax.rem(self.line + k, self.count)
            pltpu.make_async_remote_copy(
                src_ref=piece(t), dst_ref=there, send_sem=send, recv_sem=recv,
                device_id=(t // 4, t % 4), device_id_type=MESH).start()
            return carry
        lax.fori_loop(1, self.count, go, 0)

    def exchange_chips(self, piece, there, send, recv):
        def go(k, carry):
            t = lax.rem(self.line + 2 * k, self.count)
            pltpu.make_async_remote_copy(
                src_ref=piece(t // 2), dst_ref=there, send_sem=send, recv_sem=recv,
                device_id=(t // 4, t % 4), device_id_type=MESH).start()
            return carry
        lax.fori_loop(1, self.count // 2, go, 0)

    def exchanged(self, got, sem):
        others = got.at[pl.ds(0, got.shape[0] - 1)]
        pltpu.make_async_copy(others, others, sem).wait()


def wait_rows(ref, total, sem):
    for blocks in range(1, ref.shape[0] + 1):
        if total % (blocks * 16) == 0 and total // blocks <= ref.shape[1]:
            some = ref.at[pl.ds(0, blocks), pl.ds(0, total // blocks)]
            pltpu.make_async_copy(some, some, sem).wait()
            return
    raise ValueError("rows")


def each_rows(total, step, body):
    def go(i, carry):
        body(pl.ds(pl.multiple_of(i * step, step), step))
        return carry
    lax.fori_loop(0, total // step, go, 0)


def each_columns(body):
    def go(i, carry):
        body(pl.ds(pl.multiple_of(i * 256, 256), 256))
        return carry
    lax.fori_loop(0, 4, go, 0)
    body(pl.ds(1024, 128))


def window(head):
    low = head * HEAD_DIM
    first, last = low // 128 * 128, -(-(low + HEAD_DIM) // 128) * 128
    lane = lax.broadcasted_iota(jnp.int32, (1, last - first), 1) + first
    mask = jnp.where((lane >= low) & (lane < low + HEAD_DIM), 1.0, 0.0).astype(F32)
    return slice(first, last), mask


class Gather:
    def __init__(self, me, src, out, sems):
        self.me, self.src, self.out = me, src, out
        self.send, self.recv, self.sib_send, self.sib_recv, self.own = sems
        self.all = rels(me.zc)
        self.index = {r: i for i, r in enumerate(self.all)}

    def block(self, g, rel, r0, rows):
        w, x = self.me.shifted(self.me.zc - rel[0], rel[1], rel[2])
        n = x * 2 + self.me.c
        b, row = (n, w * ROWS) if g < 2 else ((w * 4 + n) // self.me.wcount, lax.rem(w * 4 + n, self.me.wcount) * ROWS)
        return self.out.at[g, b, pl.ds(pl.multiple_of(row + r0, 16), rows)]

    def forward(self, g, p, rel):
        r0, rows, order = PARTS[g][p]
        at = max([i for i, d in enumerate(order) if rel[AT[d]]], default=-1)
        there = self.block(g, rel, r0, rows)
        here = there if any(rel) else self.src.at[g, pl.ds(r0, rows)]
        for d in order[at + 1:]:
            for h in self.me.hops[d]:
                seen = ((rel[0] + h[0]) % self.me.zc, (rel[1] + h[1]) % 2, (rel[2] + h[2]) % 2)
                pltpu.make_async_remote_copy(
                    src_ref=here, dst_ref=there, send_sem=self.send.at[g, p], recv_sem=self.recv.at[g, p, self.index[seen]],
                    device_id=self.me.device(*h), device_id_type=MESH).start()
        pltpu.make_async_remote_copy(
            src_ref=here, dst_ref=there, send_sem=self.sib_send.at[g, p], recv_sem=self.sib_recv.at[g, p, rel[0]],
            device_id=self.me.device(0, 0, 0, 1), device_id_type=MESH).start()

    def begin(self, g):
        for p in range(len(PARTS[g])):
            self.forward(g, p, (0, 0, 0))
        pltpu.make_async_copy(self.src.at[g], self.block(g, (0, 0, 0), 0, ROWS), self.own.at[g]).start()

    def ticks(self, g):
        soon, late = [], []
        for deep in (1, 2, 3):
            for rel in self.all:
                if sum(1 for v in rel if v) == deep:
                    now = [p for p, part in enumerate(PARTS[g]) if part[2][-1] != "z" or not rel[0]]
                    if now:
                        soon.append(functools.partial(self.tick, g, rel, now))
                    if len(now) < len(PARTS[g]):
                        late.append(functools.partial(self.tick, g, rel, [p for p in range(len(PARTS[g])) if p not in now]))
        return soon, late

    def tick(self, g, rel, parts):
        for p in parts:
            wait_rows(self.out.at[g], PARTS[g][p][1], self.recv.at[g, p, self.index[rel]])
            self.forward(g, p, rel)

    def arrived(self, g, levels):
        if 0 in levels:
            pltpu.make_async_copy(self.src.at[g], self.src.at[g], self.own.at[g]).wait()
        for p, (r0, rows, _) in enumerate(PARTS[g]):
            for rz in levels:
                wait_rows(self.out.at[g], 4 * rows, self.sib_recv.at[g, p, rz])

    def finish(self, g):
        for p, (r0, rows, _) in enumerate(PARTS[g]):
            wait_rows(self.out.at[g], (4 * self.me.zc - 1) * rows, self.send.at[g, p])
            wait_rows(self.out.at[g], 4 * self.me.zc * rows, self.sib_send.at[g, p])


class Blocks:
    def __init__(self, full, buf, sems, order):
        self.full, self.buf, self.sems, self.order = full, buf, sems, order

    def fetch(self, i):
        if i < len(self.order):
            g, b = self.order[i]
            pltpu.make_async_copy(self.full.at[g, b], self.buf.at[i % 2], self.sems.at[i % 2]).start()

    def take(self, i):
        g, b = self.order[i]
        pltpu.make_async_copy(self.full.at[g, b], self.buf.at[i % 2], self.sems.at[i % 2]).wait()
        return self.buf.at[i % 2]


def standard(v):
    center = v - jnp.mean(v, axis=-1, keepdims=True)
    spread = lax.rsqrt(jnp.mean(center * center, axis=-1, keepdims=True) + EPSILON)
    return center * spread, spread


def gelu(v):
    return 0.5 * v * (1.0 + jnp.tanh(0.7978845608 * (v + 0.044715 * v * v * v)))


def gelu_slope(v):
    t = jnp.tanh(0.7978845608 * (v + 0.044715 * v * v * v))
    return 0.5 * (1.0 + t) + 0.5 * v * (1.0 - t * t) * 0.7978845608 * (1.0 + 3.0 * 0.044715 * v * v)


def turn(ref, out):
    def body(cols):
        out[cols, :] = ref[:, cols].astype(F32).T.astype(BF16)
    each_columns(body)


def table_picker(x, entries, line):
    entry = lax.broadcasted_iota(jnp.int32, (entries, line), 0) % 128
    lane = lax.broadcasted_iota(jnp.int32, (entries, line), 1)
    return jnp.where(entry == x - lane % GRID + GRID - 1, 1.0, 0.0).astype(BF16)


def row_picker(line):
    row = lax.broadcasted_iota(jnp.int32, (2 * GRID, line), 0)
    lane = lax.broadcasted_iota(jnp.int32, (2 * GRID, line), 1)
    return jnp.where(row == 2 * GRID - 2 - lane // GRID, 1.0, 0.0).astype(F32)


def forward_kernel(zc, qkv, out, up, down, silu_out, ada, bias_row, token_row, kept, keep, table, cotangent,
                   full, one_t_out, projected_out, att_out, mixed_t_out, branch_out, stream_mid_out, two_t_out, hidden_out, sum_down_out, stream_in_out,
                   block_out, mod, silu_part, selector, gate_sum,
                   one_t, projected, att, mixed_t, branch, stream_mid, two_t, hidden, sum_down, stream_in, save_sem,
                   act_t, acts_sib, grad_down, grad_down_sib, src, pieces, landed, rows_wide, turn_send, turn_recv, pair_send, pair_recv,
                   wbuf, normed, wide_one, act, turned, silu_got, mod_rows, mod_sib, mod_got, kept_got, spread_bias,
                   send, recv, sib_send, sib_recv, own, wsem, small_send, small_recv):
    me = Place(zc)
    place = me.x * 2 + me.c
    width = out.shape[0]
    for n in range(4):
        piece = qkv[:, n * D:(n + 1) * D] if n < 3 else out[...]
        pieces[0, n] = piece.astype(BF16)
    me.greet()
    turns = {}

    def spread_rows(g):
        for k in range(1, 4):
            n = (place + k) % 4
            turns[g, k] = pltpu.make_async_remote_copy(
                src_ref=pieces.at[g, n], dst_ref=landed.at[g, place], send_sem=turn_send.at[g, k - 1], recv_sem=turn_recv.at[g, k - 1],
                device_id=(me.line // 4, n), device_id_type=MESH)
            turns[g, k].start()
        landed[g, place] = pieces[g, place]

    def join_rows(g):
        for k in range(1, 4):
            turns[g, k].wait_recv()
        for n in range(4):
            rows_wide[n * width:(n + 1) * width, :] = landed[g, n].astype(F32)
        src[g] = rows_wide[...].astype(BF16)

    spread_rows(0)
    net = Gather(me, src, full, (send, recv, sib_send, sib_recv, own))
    blocks = Blocks(full, wbuf, wsem, [(0, 0), (0, 1), (0, 2), (0, 3), (1, 0), (1, 1), (1, 2), (1, 3)])
    saves = []

    def save(here, there):
        copy = pltpu.make_async_copy(here, there, save_sem.at[len(saves)])
        copy.start()
        saves.append(copy)

    core_line = me.turned(me.line)
    me.exchange(lambda t: silu_out.at[t], silu_got.at[core_line], small_send.at[0], small_recv.at[0])
    for n in range(4):
        pieces[1, n] = up[:, n * D:(n + 1) * D].astype(BF16)
    join_rows(0)
    net.begin(0)
    spread_rows(1)
    src[2] = down[...].astype(BF16)
    me.exchange(lambda t: kept.at[t], kept_got.at[me.line], small_send.at[1], small_recv.at[1])
    silu_got[core_line] = silu_out[me.line]
    kept_got[me.line] = kept[me.line]
    ticks, _ = net.ticks(0)

    me.exchanged(silu_got, small_recv.at[0])
    silu_part[...] = silu_got[:, 0, :]
    mine = silu_part[:, : ada.shape[0]].astype(BF16)
    def mod_column(j, carry):
        lanes = pl.ds(pl.multiple_of(j * 128, 128), 128)
        v = jnp.dot(mine, ada[:, lanes].astype(BF16), preferred_element_type=F32) + bias_row[:, lanes]
        mod_rows[:, pl.ds(j, 1), :] = v[:, None, :]
        return carry
    lax.fori_loop(0, 54, mod_column, 0)
    def token_column(j, carry):
        v = jnp.broadcast_to(token_row[:, pl.ds(pl.multiple_of(j * 128, 128), 128)], (me.count, 128))
        mod_rows[:, pl.ds(54 + j, 1), :] = v[:, None, :]
        return carry
    lax.fori_loop(0, 9, token_column, 0)
    mod_rows[:, 63:64, :] = jnp.zeros((me.count, 1, 128), F32)
    half = me.count // 2
    chip = me.line // 2
    mod_swap = pltpu.make_async_remote_copy(
        src_ref=mod_rows.at[pl.ds((1 - me.c) * half, half)], dst_ref=mod_sib, send_sem=small_send.at[3], recv_sem=small_recv.at[3],
        device_id=me.device(0, 0, 0, 1), device_id_type=MESH)
    mod_swap.start()
    for _ in range(3):
        ticks.pop(0)()
    mod_swap.wait()
    def both(i, carry):
        mod_sib[i] += mod_rows[me.c * half + i]
        return carry
    lax.fori_loop(0, half, both, 0)
    me.exchange_chips(lambda t: mod_sib.at[t], mod_got.at[chip], small_send.at[2], small_recv.at[2])
    mod_got[chip] = mod_sib[chip]
    for _ in range(2):
        ticks.pop(0)()

    v = table[...]
    high = v.astype(BF16)
    rest = v - high.astype(F32)
    middle = rest.astype(BF16)
    halves = jnp.concatenate([high, middle, (rest - middle.astype(F32)).astype(BF16)], axis=1)
    picked_rows = row_picker(SPAN)
    def spread(x, carry):
        got = jnp.dot(halves, table_picker(x, 384, SPAN), preferred_element_type=F32)
        spread_bias[x] = jnp.sum(got.reshape(HEADS, 2 * GRID, SPAN) * picked_rows[None], axis=1)
        return carry
    lax.fori_loop(0, GRID // 2, spread, 0)
    for _ in range(4):
        ticks.pop(0)()
    lax.fori_loop(GRID // 2, GRID, spread, 0)

    row = lax.broadcasted_iota(jnp.int32, (PATCHES, PATCHES), 0)
    column = lax.broadcasted_iota(jnp.int32, (PATCHES, PATCHES), 1)
    kept_here = keep[...].astype(F32)
    before = jnp.where(row >= column, 1.0, 0.0).astype(BF16)
    ranks = jnp.dot(before, jnp.broadcast_to(kept_here, (PATCHES, 128)).astype(BF16), preferred_element_type=F32)
    ranks = ranks[:, :1].astype(jnp.int32) - 1
    slot = (ranks % me.count) * 8 + ranks // me.count
    selector[...] = jnp.where((keep[...] == 1) & (slot == column), 1.0, 0.0).astype(BF16)
    me.exchanged(mod_got, small_recv.at[2])
    total = mod_got[0]
    for i in range(1, half):
        total += mod_got[i]
    for i in range(63):
        mod[i // 9:i // 9 + 1, i % 9 * 128:(i % 9 + 1) * 128] = total[i:i + 1, :]
    me.exchanged(kept_got, small_recv.at[1])
    def put(cols):
        v = jnp.dot(selector[...], kept_got[:, :, cols].reshape(me.count * 8, -1), preferred_element_type=F32)
        stream_in[:, cols] = v + (1.0 - kept_here) * mod[6:7, cols]
    each_columns(put)

    def norm_one(rows):
        n, _ = standard(stream_in[rows, :])
        normed[rows, :] = (n * (1.0 + mod[1:2, :]) + mod[0:1, :]).astype(BF16)
    each_rows(PATCHES, 32, norm_one)
    turn(normed, one_t)
    def gated(rows):
        grad_down[rows, :] = (mod[5:6, :] * cotangent[rows, :].astype(F32)).astype(BF16)
    each_rows(PATCHES, 32, gated)
    def pair(here, there, i):
        copy = pltpu.make_async_remote_copy(
            src_ref=here, dst_ref=there, send_sem=pair_send.at[i], recv_sem=pair_recv.at[i], device_id=me.device(0, 0, 0, 1), device_id_type=MESH)
        copy.start()
        return copy
    grad_pair = pair(grad_down, grad_down_sib, 0)
    save(stream_in, stream_in_out)
    save(one_t, one_t_out)
    join_rows(1)
    net.begin(1)
    for tick in ticks:
        tick()
    net.arrived(0, range(zc))
    ticks, late = net.ticks(1)
    blocks.fetch(0)
    blocks.fetch(1)
    for b in range(3):
        w = blocks.take(b)
        def product(cols):
            projected[b, :, cols] = jnp.dot(normed[...], w[:, cols], preferred_element_type=F32).astype(BF16)
        each_columns(product)
        blocks.fetch(b + 2) if b + 2 < 4 else None
        ticks.pop(0)()
    save(projected, projected_out)
    wide_one[...] = jnp.zeros_like(wide_one)
    for head in range(HEADS):
        lanes, mask = window(head)
        q = projected[0, :, lanes] * mask.astype(BF16)
        scores = lax.dot_general(q, projected[1, :, lanes], NT, preferred_element_type=F32) * FACTOR
        u = spread_bias[:, head, :]
        bias = jnp.concatenate(
            [pltpu.roll(u, (SPAN - (GRID - 1 - r) * GRID) % SPAN, 1)[:, :PATCHES] for r in range(GRID)], axis=0)
        scores = scores + bias
        e = jnp.exp(scores - jnp.max(scores, axis=-1, keepdims=True))
        weights = e * (1.0 / jnp.sum(e, axis=-1, keepdims=True))
        att[head] = weights
        got = jnp.dot(weights.astype(BF16), projected[2, :, lanes], preferred_element_type=F32)
        wide_one[:, lanes] += got * mask
        if head % 2 and ticks:
            ticks.pop(0)()
        if head == 11:
            net.begin(2)
    normed[...] = wide_one[...].astype(BF16)
    turn(normed, mixed_t)
    save(att, att_out)
    save(mixed_t, mixed_t_out)
    w = blocks.take(3)
    def product(cols):
        branch[:, cols] = jnp.dot(normed[...], w[:, cols], preferred_element_type=F32)
    each_columns(product)
    def mid(rows):
        v = stream_in[rows, :] + mod[2:3, :] * branch[rows, :]
        stream_mid[rows, :] = v
        n, _ = standard(v)
        normed[rows, :] = (n * (1.0 + mod[4:5, :]) + mod[3:4, :]).astype(BF16)
    each_rows(PATCHES, 32, mid)
    turn(normed, two_t)
    save(branch, branch_out)
    save(stream_mid, stream_mid_out)
    save(two_t, two_t_out)
    for tick in ticks + late:
        tick()
    net.arrived(1, range(zc))
    ticks, late = net.ticks(2)
    def down_block(i):
        w = blocks.take(i)
        part = act.at[blocks.order[i][1]]
        def product(cols):
            v = jnp.dot(part[...], w[:, cols], preferred_element_type=F32)
            wide_one[:, cols] = v if i == 8 else wide_one[:, cols] + v
        each_columns(product)
    blocks.fetch(4)
    blocks.fetch(5)
    def turn_units(ref, b):
        turn(ref, turned)
        for i in range(8):
            unit = b * 8 + i
            w, n = unit // 4, unit % 4
            act_t[n % 2, n // 2, w * ROWS:(w + 1) * ROWS, :] = turned[i * ROWS:(i + 1) * ROWS, :]
    for b in range(4):
        w = blocks.take(4 + b)
        def product(cols):
            v = jnp.dot(normed[...], w[:, cols], preferred_element_type=F32)
            hidden[b, :, cols] = v
        each_columns(product)
        if b < 2:
            blocks.fetch(6 + b)
        def bend(rows):
            act[b, rows, :] = gelu(hidden[b, rows, :]).astype(BF16)
        each_rows(PATCHES, 32, bend)
        turn_units(act.at[b], b)
        save(hidden.at[b], hidden_out.at[b])
        for _ in range(2):
            ticks.pop(0)()
    act_pair = pair(act_t.at[1 - me.c], acts_sib, 1)
    def down_grad(j):
        def body(cols):
            v = jnp.dot(act_t[me.c, j], grad_down[:, cols], preferred_element_type=F32)
            sum_down[j, :, cols] = (v + jnp.dot(acts_sib[j], grad_down_sib[:, cols], preferred_element_type=F32)).astype(BF16)
        each_columns(body)
        save(sum_down.at[j], sum_down_out.at[j])
    for i in range(zc):
        blocks.order.append((2, lax.rem(me.z + zc - i, zc)))
    last_ticks = [[t for t in ticks + late if t.args[1][0] == i] for i in range(zc)]
    middle = [t for t in ticks if t.args[1][0] and sum(map(bool, t.args[1])) < 3]
    for i in range(zc):
        for t in last_ticks[i]:
            if t not in middle:
                t()
        if i == 0:
            for t in middle:
                t()
        if i == 0:
            grad_pair.wait_recv()
            act_pair.wait_recv()
        if i < 2:
            down_grad(i)
        net.arrived(2, [i])
        blocks.fetch(8 + i)
        if i:
            down_block(7 + i)
    down_block(7 + zc)
    gate_sum[...] = jnp.zeros_like(gate_sum)
    def last(rows):
        v = wide_one[rows, :]
        block_out[rows, :] = (stream_mid[rows, :] + mod[5:6, :] * v).astype(BF16)
        gate_sum[...] += jnp.sum(cotangent[rows, :].astype(F32) * v, axis=0, keepdims=True)
    each_rows(PATCHES, 32, last)
    for copy in saves:
        copy.wait()
    for copy in turns.values():
        copy.wait_send()
    grad_pair.wait_send()
    act_pair.wait_send()
    for g in range(3):
        net.finish(g)
    for i, got in enumerate((silu_got, kept_got, mod_got)):
        me.exchanged(got, small_send.at[i])


def run_forward(qkv, out, up, down, silu_out, ada, bias_row, token_row, kept, keep, table, cotangent, zc):
    vmem = pl.BlockSpec(memory_space=pltpu.VMEM)
    hbm = pl.BlockSpec(memory_space=pl.ANY)
    parts, count = max(map(len, PARTS)), 8 * zc
    shape = jax.ShapeDtypeStruct
    dma = pltpu.SemaphoreType.DMA
    width = out.shape[0]
    kept_on = [((D, PATCHES), BF16), ((3, PATCHES, D), BF16), ((HEADS, PATCHES, PATCHES), F32), ((D, PATCHES), BF16), ((PATCHES, D), F32),
               ((PATCHES, D), F32), ((D, PATCHES), BF16), ((4, PATCHES, D), F32), ((2, D, D), BF16), ((PATCHES, D), F32)]
    return pl.pallas_call(
        functools.partial(forward_kernel, zc),
        out_shape=[shape((3, 4, D, D), BF16)] + [shape(*k) for k in kept_on] + [
            shape((PATCHES, D), BF16), shape((8, D), F32), shape((count, 128), F32), shape((PATCHES, PATCHES), BF16), shape((1, D), F32)],
        in_specs=[vmem] * 12,
        out_specs=[hbm] * 11 + [vmem] * 5,
        scratch_shapes=[pltpu.VMEM(*k) for k in kept_on] + [
            dma((14,)),
            pltpu.VMEM((2, 2, D, PATCHES), BF16), pltpu.VMEM((2, D, PATCHES), BF16), pltpu.VMEM((PATCHES, D), BF16), pltpu.VMEM((PATCHES, D), BF16),
            pltpu.VMEM((3, ROWS, D), BF16), pltpu.VMEM((2, 4, width, D), BF16), pltpu.VMEM((2, 4, width, D), BF16), pltpu.VMEM((ROWS, D), F32),
            dma((2, 3)), dma((2, 3)), dma((2,)), dma((2,)),
            pltpu.VMEM((2, D, D), BF16), pltpu.VMEM((PATCHES, D), BF16), pltpu.VMEM((PATCHES, D), F32), pltpu.VMEM((4, PATCHES, D), BF16), pltpu.VMEM((D, PATCHES), BF16),
            pltpu.VMEM((count, 8, 128), F32), pltpu.VMEM((count, 64, 128), F32), pltpu.VMEM((count // 2, 64, 128), F32), pltpu.VMEM((count // 2, 64, 128), F32),
            pltpu.VMEM((count, 8, D), BF16), pltpu.VMEM((GRID, HEADS, SPAN), F32),
            dma((3, parts)), dma((3, parts, 4 * zc)), dma((3, parts)), dma((3, parts, zc)), dma((3,)), dma((2,)), dma((4,)), dma((4,))],
        compiler_params=pltpu.CompilerParams(collective_id=1, has_side_effects=True, vmem_limit_bytes=58 * 1024 * 1024),
        name="forward",
    )(qkv, out, up, down, silu_out, ada, bias_row, token_row, kept, keep, table, cotangent)


RPARTS = (((0, 64, "zxy"), (64, 64, "zyx"), (128, 16, "xyz")),) * 3


def reduce_plan(zc, order):
    live, slots, phases = rels(zc), {}, []
    for j, d in enumerate(order[::-1]):
        sends = [r for r in live if r[AT[d]]]
        live = [r for r in live if not r[AT[d]]]
        hops = list(range(1, zc)) if d == "z" else [1]
        for r in live:
            for k in hops:
                slots[r, j, k] = len(slots)
        phases.append((d, sends, live, hops))
    return phases, slots


class Reduce:
    def __init__(self, me, sums, landed, owned, send, recv):
        self.me, self.sums, self.landed, self.owned, self.send_sem, self.recv = me, sums, landed, owned, send, recv
        self.plans = [[reduce_plan(me.zc, part[2]) for part in parts] for parts in RPARTS]
        self.held, self.first = {}, {}
        self.items = [(g, k) for g in (2, 1, 0) for k in list(range(1, me.zc)) + [0]]

    def partial(self, g, p, rel, first=False):
        r0, rows, _ = RPARTS[g][p]
        if (g, p, rel) in self.held:
            return self.landed.at[g, self.held[g, p, rel], pl.ds(r0, rows)]
        w, x = self.me.shifted(*rel)
        return (self.first.get(g, self.sums[g]) if first else self.sums[g]).at[x, pl.ds(pl.multiple_of(w * ROWS + r0, 16), rows)]

    def send(self, g, p, j, rel):
        r0, rows, _ = RPARTS[g][p]
        d = self.plans[g][p][0][j][0]
        k = rel[AT[d]]
        hop = tuple(k if i == AT[d] else 0 for i in range(3))
        there = tuple(0 if i == AT[d] else rel[i] for i in range(3))
        slot = self.plans[g][p][1][there, j, k]
        pltpu.make_async_remote_copy(
            src_ref=self.partial(g, p, rel, j == 0), dst_ref=self.landed.at[g, slot, pl.ds(r0, rows)],
            send_sem=self.send_sem.at[g, p, min(j, 1)], recv_sem=self.recv.at[g, p, slot],
            device_id=self.me.device(*hop), device_id_type=MESH).start()

    def receive(self, g, p, j, rel, final):
        r0, rows, _ = RPARTS[g][p]
        slots = [self.plans[g][p][1][rel, j, k] for k in self.plans[g][p][0][j][3]]
        for s in slots:
            ref = self.landed.at[g, s, pl.ds(r0, rows)]
            pltpu.make_async_copy(ref, ref, self.recv.at[g, p, s]).wait()
        mine = self.partial(g, p, rel)
        def body(i, carry):
            at = pl.ds(pl.multiple_of(r0 + i * 16, 16), 16)
            total = mine[pl.ds(pl.multiple_of(i * 16, 16), 16), :].astype(F32)
            for s in slots:
                total += self.landed[g, s, at, :].astype(F32)
            if final:
                self.owned[g][at, :] = total.astype(self.owned[g].dtype)
            else:
                self.landed[g, slots[0], at, :] = total.astype(BF16)
            return carry
        lax.fori_loop(0, rows // 16, body, 0)
        self.held[g, p, rel] = slots[0]

    def stage(self, j, g, k):
        for p in range(len(RPARTS[g])):
            phases = self.plans[g][p][0]
            lowered = [r for r in phases[j - 1][2] if r[0] == k] if j else []
            sends = [r for r in phases[j][1] if r[0] == k] if j < 3 else []
            for rel in sorted(lowered, key=lambda r: r not in sends):
                self.receive(g, p, j - 1, rel, j == 3)
                if rel in sends:
                    self.send(g, p, j, rel)
            if j == 0:
                for rel in sends:
                    self.send(g, p, 0, rel)

    def step(self, t):
        for j in range(4):
            if 0 <= t - j < len(self.items):
                self.stage(j, *self.items[t - j])

    def steps(self):
        return len(self.items) + 3

    def sent(self, g, late):
        for p, (r0, rows, _) in enumerate(RPARTS[g]):
            phases = self.plans[g][p][0]
            count = sum(len(phases[j][1]) for j in ((1, 2) if late else (0,)))
            ref = self.landed.at[g, pl.ds(0, count), pl.ds(r0, rows)]
            pltpu.make_async_copy(ref, ref, self.send_sem.at[g, p, int(late)]).wait()


class Fold:
    def __init__(self, me, table, token, lands, tokens, whole, send, recv):
        self.me, self.table, self.token, self.lands, self.whole = me, table, token, lands, whole
        self.token_land, self.token_out = tokens
        self.send, self.recv, self.started = send, recv, []
        self.steps, lo, size = [], 0, table.shape[0]
        for bit, many, peers in ((me.c, 2, [(0, 0, 0, 1)]), (me.x, 2, [(0, 0, 1)]), (me.y, 2, [(0, 1, 0)]),
                                 (me.z, me.zc, [(k, 0, 0) for k in range(1, me.zc)])):
            part = size // many
            self.steps.append((lo, size, part, bit, many, peers))
            lo, size = lo + bit * part, part
        self.lo = lo

    def rows(self, ref, at, count):
        return ref.at[pl.ds(pl.multiple_of(at, 8), count)]

    def remote(self, src, dst, which, peer):
        copy = pltpu.make_async_remote_copy(
            src_ref=src, dst_ref=dst, send_sem=self.send.at[which], recv_sem=self.recv.at[which],
            device_id=self.me.device(*peer), device_id_type=MESH)
        copy.start()
        self.started.append(copy)

    def give(self, i):
        lo, size, part, bit, many, peers = self.steps[i]
        self.token_out[i] = self.token[...]
        for k, peer in enumerate(peers):
            other = lax.rem(bit + k + 1, many)
            land = self.lands[i].at[k] if many > 2 or i == 3 else self.lands[i]
            self.remote(self.rows(self.table, lo + other * part, part), land, (i, 0, k), peer)
            self.remote(self.token_out.at[i], self.token_land.at[i, k], (i, 1, k), peer)

    def take(self, i):
        lo, size, part, bit, many, peers = self.steps[i]
        mine = pl.ds(pl.multiple_of(lo + bit * part, 8), part)
        for k in range(len(peers)):
            land = self.lands[i].at[k] if many > 2 or i == 3 else self.lands[i]
            pltpu.make_async_copy(land, land, self.recv.at[i, 0, k]).wait()
            pltpu.make_async_copy(self.token_land.at[i, k], self.token_land.at[i, k], self.recv.at[i, 1, k]).wait()
            self.table[mine, :] += land[...]
            self.token[...] += self.token_land[i, k]
        if i == 3:
            self.whole[mine, :] = self.table[mine, :]

    def hand(self, i):
        lo, size, part, bit, many, peers = self.steps[i]
        mine = self.rows(self.whole, lo + bit * part, part)
        for k, peer in enumerate(peers):
            self.remote(mine, mine, (4 + i, 0, k), peer)

    def handed(self, i):
        lo, size, part, bit, many, peers = self.steps[i]
        some = self.rows(self.whole, 0, part)
        for k in range(len(peers)):
            pltpu.make_async_copy(some, some, self.recv.at[4 + i, 0, k]).wait()

    def finish(self):
        for copy in self.started:
            copy.wait_send()


def backward_kernel(zc, full, mod, cotangent, stream_in, stream_mid, branch, projected, att, hidden, one_t, mixed_t, two_t, sum_down,
                    ada, silu_part, selector, keep, gate_sum,
                    owned_down, owned_turned, grad_ada, mod_total, silu_back, kept_grad, table_grad, token_grad,
                    sum_a, sum_b, landed, wbuf, left, left_sib, grad_down, right_sib, bent, rights, grad_mixed,
                    stream, hid, att_buf, spread_grad, grad_in, small,
                    owned_out, lines, line_low, mod_got, mod_flat, ada_wide, ada_low, silu_out, kept_out, table_sum, token_sum,
                    land_core, land_x, land_y, land_z, land_token, token_out, rights_out,
                    send, recv, sib_send, sib_recv, wsem, lsem, hsem, asem, ssem, small_send, small_recv, turn_send, turn_recv, fold_send, fold_recv):
    me = Place(zc)
    me.greet()
    c = me.c
    net = Reduce(me, {2: sum_a, 1: sum_b, 0: sum_a}, landed, {2: owned_down, 1: owned_out.at[1], 0: owned_out.at[0]}, send, recv)
    blocks = Blocks(full, wbuf, wsem, [(2, 0), (2, 1), (2, 2), (2, 3), (1, 0), (1, 1), (1, 2), (1, 3), (0, 3), (0, 0), (0, 1), (0, 2)])
    swaps = []

    def swap(src, dst):
        i = len(swaps)
        swaps.append(pltpu.make_async_remote_copy(
            src_ref=src, dst_ref=dst, send_sem=sib_send.at[i], recv_sem=sib_recv.at[i],
            device_id=me.device(0, 0, 0, 1), device_id_type=MESH))
        swaps[-1].start()
        return swaps[-1]

    def load(src, dst, sem):
        copy = pltpu.make_async_copy(src, dst, sem)
        copy.start()
        return copy

    net.first[2] = sum_down
    net.step(0)
    sum_load = load(sum_down, sum_a, lsem.at[0])
    blocks.fetch(0)
    blocks.fetch(1)
    hid_load = load(hidden.at[0], hid, hsem.at[0])

    def down(rows):
        grad_down[rows, :] = (mod[5:6, :] * cotangent[rows, :].astype(F32)).astype(BF16)
    each_rows(PATCHES, 32, down)
    ada_load = load(ada, ada_wide, lsem.at[4])
    left_loads = [load(ref, left.at[i], lsem.at[1 + i]) for i, ref in enumerate((one_t, mixed_t, two_t))]
    left_swaps = [swap(ref, left_sib.at[i]) for i, ref in enumerate((one_t, mixed_t, two_t))]
    mid_load = load(stream_mid, stream.at[0], ssem.at[0])

    def weight_grad(total, mine, mine_right, theirs, their_right):
        def body(cols):
            v = jnp.dot(mine[...], mine_right[:, cols], preferred_element_type=F32)
            total[:, cols] = (v + jnp.dot(theirs[...], their_right[:, cols], preferred_element_type=F32)).astype(BF16)
        each_columns(body)

    sum_load.wait()
    for b in range(4):
        w = blocks.take(b)
        hid_load.wait()
        def bend(cols):
            v = lax.dot_general(grad_down[...], w[cols, :], NT, preferred_element_type=F32)
            bent[b, :, cols] = (v * gelu_slope(hid[:, cols])).astype(BF16)
        each_columns(bend)
        blocks.fetch(b + 2)
        if b < 3:
            hid_load = load(hidden.at[b + 1], hid, hsem.at[0])
        if b in (1, 3):
            net.step((b + 1) // 2)
    branch_load = load(branch, hid, ssem.at[1])
    bent_swaps = [swap(bent.at[1 - c], right_sib.at[0]), swap(bent.at[3 - c], right_sib.at[1])]
    for copy in left_loads:
        copy.wait()
    for copy in left_swaps + bent_swaps:
        copy.wait_recv()
    for j in range(2):
        weight_grad(sum_b.at[j], left.at[2], bent.at[2 * j + c], left_sib.at[2], right_sib.at[j])
    net.step(3)
    for b in range(4):
        w = blocks.take(4 + b)
        def back(cols):
            v = lax.dot_general(bent[b], w[cols, :], NT, preferred_element_type=F32)
            grad_in[:, cols] = v if b == 0 else grad_in[:, cols] + v
        each_columns(back)
        blocks.fetch(6 + b)
    mid_load.wait()
    branch_load.wait()
    small[...] = jnp.zeros_like(small)

    def norm_back(rows, stream_rows, scale, shift_at, scale_at):
        n, spread = standard(stream_rows)
        e = grad_in[rows, :]
        f = e * (1.0 + scale)
        small[shift_at:shift_at + 1, :] += jnp.sum(e, axis=0, keepdims=True)
        small[scale_at:scale_at + 1, :] += jnp.sum(e * n, axis=0, keepdims=True)
        return (f - jnp.mean(f, axis=-1, keepdims=True) - n * jnp.mean(f * n, axis=-1, keepdims=True)) * spread

    def back_two(rows):
        v = cotangent[rows, :].astype(F32) + norm_back(rows, stream[0, rows, :], mod[4:5, :], 3, 4)
        small[2:3, :] += jnp.sum(v * hid[rows, :], axis=0, keepdims=True)
        hid[rows, :] = v
        rights[3, rows, :] = (mod[2:3, :] * v).astype(BF16)
    each_rows(PATCHES, 32, back_two)
    in_load = load(stream_in, stream.at[0], ssem.at[0])
    net.step(4)
    att_load = load(att.at[0], att_buf.at[0], asem.at[0])
    w = blocks.take(8)
    def mixed_back(cols):
        grad_mixed[:, cols] = lax.dot_general(rights[3], w[cols, :], NT, preferred_element_type=F32).astype(BF16)
    each_columns(mixed_back)
    blocks.fetch(10)
    for b in range(3):
        rights[b] = jnp.zeros((PATCHES, D), BF16)
    net.step(5)
    for head in range(HEADS):
        att_load.wait()
        if head + 1 < HEADS:
            att_load = load(att.at[head + 1], att_buf.at[(head + 1) % 2], asem.at[(head + 1) % 2])
        lanes, mask = window(head)
        weights = att_buf[head % 2]
        low = weights.astype(BF16)
        given = grad_mixed[:, lanes]
        grad_att = lax.dot_general(given * mask.astype(BF16), projected[2, :, lanes], NT, preferred_element_type=F32)
        v = lax.dot_general(low, given, TN, preferred_element_type=F32)
        rights[2, :, lanes] += (v * mask).astype(BF16)
        scores = weights * (grad_att - jnp.sum(weights * grad_att, axis=-1, keepdims=True))
        scores_low = scores.astype(BF16)
        v = jnp.dot(scores_low, projected[1, :, lanes], preferred_element_type=F32) * FACTOR
        rights[0, :, lanes] += (v * mask).astype(BF16)
        v = lax.dot_general(scores_low, projected[0, :, lanes], TN, preferred_element_type=F32) * FACTOR
        rights[1, :, lanes] += (v * mask).astype(BF16)
        rounded = scores_low.astype(F32)
        total = jnp.zeros((GRID, SPAN), F32)
        for r in range(GRID):
            rows = jnp.concatenate([rounded[r * GRID:(r + 1) * GRID], jnp.zeros((GRID, SPAN - PATCHES), F32)], axis=1)
            total += pltpu.roll(rows, (GRID - 1 - r) * GRID, 1)
        spread_grad[:, head, :] = total
        if head in (7, 15):
            net.step(6 + head // 8)
    end_swaps = [swap(rights.at[1 - c], right_sib.at[2]), swap(rights.at[3 - c], right_sib.at[3])]
    for b in range(3):
        w = blocks.take(9 + b)
        def back(cols):
            v = lax.dot_general(rights[b], w[cols, :], NT, preferred_element_type=F32)
            grad_in[:, cols] = v if b == 0 else grad_in[:, cols] + v
        each_columns(back)
        blocks.fetch(11 + b)
    in_load.wait()
    def back_one(rows):
        v = norm_back(rows, stream[0, rows, :], mod[1:2, :], 0, 1)
        grad_in[rows, :] = hid[rows, :] + v
    each_rows(PATCHES, 32, back_one)
    for v in range(6):
        for i in range(9):
            piece = small[v:v + 1, i * 128:(i + 1) * 128] if v < 5 else gate_sum[:, i * 128:(i + 1) * 128]
            lines[v * 9 + i:v * 9 + i + 1, :] = piece
    lines[54:64, :] = jnp.zeros((10, 128), F32)
    line_low[...] = lines[...].astype(BF16)
    half, chip = me.count // 2, me.line // 2
    mine_at = c * half
    me.exchange_chips(lambda t: line_low, mod_got.at[mine_at + chip], small_send.at[0], small_recv.at[0])
    mod_got[mine_at + chip] = line_low[...]
    grad_mixed[...] = grad_in[...].astype(BF16)
    def put_back(cols):
        v = lax.dot_general(selector[...], grad_mixed[:, cols], TN, preferred_element_type=F32).astype(BF16)
        kept_out[:, :, cols] = v.reshape(me.count, 8, -1)
    each_columns(put_back)
    kept_own = load(kept_out.at[me.line], kept_grad.at[me.line], ssem.at[1])
    net.sent(2, False)
    for copy in end_swaps:
        copy.wait_recv()
    weight_grad(sum_a.at[0], left.at[0], rights.at[c], left_sib.at[0], right_sib.at[2])
    weight_grad(sum_a.at[1], left.at[c], rights.at[2 + c], left_sib.at[c], right_sib.at[3])
    net.step(8)

    masked = 1.0 - keep[...].astype(F32)
    token = jnp.sum(masked * grad_in[...], axis=0, keepdims=True)
    for i in range(9):
        token_sum[i:i + 1, :] = token[:, i * 128:(i + 1) * 128]
    token_sum[9:16, :] = jnp.zeros((7, 128), F32)
    picked_rows = row_picker(SPAN)
    table_sum[...] = jnp.zeros_like(table_sum)
    def gather_table(x, carry):
        picker = table_picker(x, 128, SPAN)
        v = (spread_grad[x][:, None, :] * picked_rows[None]).reshape(HEADS * 2 * GRID, SPAN)
        high = v.astype(BF16)
        rest = v - high.astype(F32)
        middle = rest.astype(BF16)
        low = (rest - middle.astype(F32)).astype(BF16)
        for part in (high, middle, low):
            table_sum[...] += lax.dot_general(part, picker, NT, preferred_element_type=F32)
        return carry
    lax.fori_loop(0, GRID, gather_table, 0)
    fold = Fold(me, table_sum, token_sum, (land_core, land_x, land_y, land_z), (land_token, token_out), table_grad, fold_send, fold_recv)
    fold.give(0)
    net.step(9)
    fold.take(0)
    fold.give(1)

    plane = mod_got.at[pl.ds(mine_at, half)]
    me.exchanged(plane, small_recv.at[0])
    mod_swap = pltpu.make_async_remote_copy(
        src_ref=plane, dst_ref=plane, send_sem=small_send.at[2], recv_sem=small_recv.at[2],
        device_id=me.device(0, 0, 0, 1), device_id_type=MESH)
    mod_swap.start()
    ada_load.wait()
    def flat(j, carry):
        lanes = pl.ds(pl.multiple_of(j * 128, 128), 128)
        ada_low[:, lanes] = ada_wide[:, lanes].astype(BF16)
        return carry
    lax.fori_loop(0, 54, flat, 0)
    mod_swap.wait_recv()
    for j in range(54):
        mod_flat[:, j * 128:(j + 1) * 128] = mod_got[:, j, :]
    width = ada.shape[0]
    back_silu = lax.dot_general(mod_flat[...], ada_low[...], NT, preferred_element_type=F32)
    silu_out[...] = jnp.zeros_like(silu_out)
    silu_out[:, 0:1, 0:width] = back_silu[:, None, :]
    me.exchange(lambda t: silu_out.at[me.turned(t)], silu_back.at[me.line], small_send.at[3], small_recv.at[3])
    silu_back[me.line] = silu_out[me.turned(me.line)]
    net.step(10)
    fold.take(1)
    fold.give(2)
    mine = silu_part[:, :width].astype(BF16)
    def outer(j, carry):
        lanes = pl.ds(pl.multiple_of(j * 256, 256), 256)
        grad_ada[:, lanes] = lax.dot_general(mine, mod_flat[:, lanes], TN, preferred_element_type=F32)
        return carry
    lax.fori_loop(0, 27, outer, 0)
    total = jnp.zeros((64, 128), F32)
    for i in range(me.count):
        total += mod_got[i].astype(F32)
    mod_total[...] = total
    net.step(11)
    fold.take(2)
    fold.give(3)
    turns = []

    def turn_rows(g):
        for n in range(4):
            rights_out[n, g] = owned_out[g, n * width:(n + 1) * width, :].astype(BF16)
        for k in range(1, 4):
            n = (me.x * 2 + me.c + k) % 4
            copy = pltpu.make_async_remote_copy(
                src_ref=rights_out.at[n, g], dst_ref=owned_turned.at[me.x * 2 + me.c, g], send_sem=turn_send.at[g, k - 1], recv_sem=turn_recv.at[g, k - 1],
                device_id=(me.line // 4, n), device_id_type=MESH)
            copy.start()
            turns.append(copy)
        owned_turned[me.x * 2 + me.c, g] = rights_out[me.x * 2 + me.c, g]

    turn_rows(1)
    fold.take(3)
    token_grad[...] = token_sum[...]
    fold.hand(3)
    net.step(12)
    me.exchange(lambda t: kept_out.at[t], kept_grad.at[me.line], small_send.at[1], small_recv.at[1])
    fold.handed(3)
    fold.hand(2)
    net.step(13)
    fold.handed(2)
    fold.hand(1)
    net.step(14)
    turn_rows(0)
    fold.handed(1)
    fold.hand(0)
    net.sent(1, False)
    net.sent(0, False)
    for g in range(3):
        net.sent(g, True)
    for copy in swaps:
        copy.wait_send()
    kept_own.wait()
    me.exchanged(kept_grad, small_recv.at[1])
    me.exchanged(silu_back, small_recv.at[3])
    me.exchanged(plane, small_send.at[0])
    me.exchanged(kept_grad, small_send.at[1])
    mod_swap.wait_send()
    me.exchanged(silu_back, small_send.at[3])
    fold.handed(0)
    fold.finish()
    for copy in turns:
        copy.wait()


def run_backward(full, mod, cotangent, stream_in, stream_mid, branch, projected, att, hidden, one_t, mixed_t, two_t, sum_down,
                 ada, silu_part, selector, keep, gate_sum, zc):
    vmem = pl.BlockSpec(memory_space=pltpu.VMEM)
    hbm = pl.BlockSpec(memory_space=pl.ANY)
    parts, count, width = max(map(len, RPARTS)), 8 * zc, ada.shape[0]
    table = HEADS * 2 * GRID
    shape = jax.ShapeDtypeStruct
    dma = pltpu.SemaphoreType.DMA
    return pl.pallas_call(
        functools.partial(backward_kernel, zc),
        out_shape=(shape((ROWS, D), F32), shape((4, 2, width, D), BF16), shape((width, 6 * D), F32), shape((64, 128), F32),
                   shape((count, 8, 128), F32), shape((count, 8, D), BF16), shape((HEADS * 2 * GRID, 128), F32), shape((16, 128), F32)),
        in_specs=[hbm, vmem, vmem, hbm, hbm, hbm, vmem, hbm, hbm, hbm, hbm, hbm, hbm, hbm, vmem, vmem, vmem, vmem],
        out_specs=(vmem, vmem, vmem, vmem, vmem, hbm, vmem, vmem),
        scratch_shapes=[
            pltpu.VMEM((2, D, D), BF16), pltpu.VMEM((2, D, D), BF16), pltpu.VMEM((3, 4 * zc - 1, ROWS, D), BF16),
            pltpu.VMEM((2, D, D), BF16), pltpu.VMEM((3, D, PATCHES), BF16), pltpu.VMEM((3, D, PATCHES), BF16),
            pltpu.VMEM((PATCHES, D), BF16),
            pltpu.VMEM((4, PATCHES, D), BF16), pltpu.VMEM((4, PATCHES, D), BF16), pltpu.VMEM((4, PATCHES, D), BF16),
            pltpu.VMEM((PATCHES, D), BF16), pltpu.VMEM((1, PATCHES, D), F32), pltpu.VMEM((PATCHES, D), F32),
            pltpu.VMEM((2, PATCHES, PATCHES), F32),
            pltpu.VMEM((GRID, HEADS, SPAN), F32), pltpu.VMEM((PATCHES, D), F32), pltpu.VMEM((8, D), F32),
            pltpu.VMEM((2, ROWS, D), F32), pltpu.VMEM((64, 128), F32), pltpu.VMEM((64, 128), BF16), pltpu.VMEM((count, 64, 128), BF16),
            pltpu.VMEM((count, 6 * D), BF16), pltpu.VMEM((width, 6 * D), F32), pltpu.VMEM((width, 6 * D), BF16), pltpu.VMEM((count, 8, 128), F32),
            pltpu.VMEM((count, 8, D), BF16), pltpu.VMEM((table, 128), F32), pltpu.VMEM((16, 128), F32),
            pltpu.VMEM((table // 2, 128), F32), pltpu.VMEM((table // 4, 128), F32), pltpu.VMEM((table // 8, 128), F32),
            pltpu.VMEM((zc - 1, table // 8 // zc, 128), F32), pltpu.VMEM((4, zc - 1, 16, 128), F32), pltpu.VMEM((4, 16, 128), F32), pltpu.VMEM((4, 2, width, D), BF16),
            dma((3, parts, 2)), dma((3, parts, 4 * zc - 1)), dma((7,)), dma((7,)), dma((2,)), dma((5,)), dma((1,)), dma((2,)), dma((2,)),
            dma((4,)), dma((4,)), dma((2, 3)), dma((2, 3)), dma((8, 2, zc - 1)), dma((8, 2, zc - 1))],
        compiler_params=pltpu.CompilerParams(collective_id=2, has_side_effects=True, vmem_limit_bytes=63 * 1024 * 1024),
        name="backward",
    )(full, mod, cotangent, stream_in, stream_mid, branch, projected, att, hidden, one_t, mixed_t, two_t, sum_down,
      ada, silu_part, selector, keep, gate_sum)


AXES = ("wide", "narrow")


def running_rank(keep_flat):
    count = keep_flat.shape[0]
    lower = (lax.broadcasted_iota(jnp.int32, (count, count), 0) >= lax.broadcasted_iota(jnp.int32, (count, count), 1))
    total = jnp.dot(lower.astype(jnp.bfloat16), keep_flat.astype(jnp.bfloat16)[:, None], preferred_element_type=jnp.float32)
    return total[:, 0].astype(jnp.int32) - 1


def per_device_plain(kept_tokens, keep_mask, conditioning, ada_weight, ada_bias, qkv_weight, out_weight, up_weight, down_weight, position_bias, mask_token, cotangent):
    wide_count = lax.axis_size("wide")
    narrow_count = lax.axis_size("narrow")
    devices = wide_count * narrow_count
    slots = kept_tokens.shape[2]
    images = conditioning.shape[0]
    count = images * PATCHES
    rows = qkv_weight.shape[0]
    me = lax.axis_index(AXES)
    factor = 1.0 / math.sqrt(HEAD_DIM)
    low_type = jnp.bfloat16
    wide_type = jnp.float32
    silu_cond = jax.nn.silu(conditioning).astype(low_type)
    small = jnp.concatenate([silu_cond.reshape(-1), ada_bias.astype(low_type), mask_token.astype(low_type)])
    smalls = lax.all_gather(small, AXES, axis=0, tiled=False)
    silu_all = smalls[:, : images * D].reshape(devices * images, D)
    bias_full = smalls[:, images * D : images * D + ada_bias.shape[0]].reshape(-1)
    token_full = smalls[:, images * D + ada_bias.shape[0] :].reshape(-1)
    ada_low = ada_weight.astype(low_type)
    silu_part = lax.dynamic_slice_in_dim(silu_all, me * rows, rows, axis=1)
    mod_part = jnp.dot(silu_part, ada_low, preferred_element_type=wide_type)
    mod_parts = lax.all_to_all(mod_part.reshape(devices, images, 6 * D), AXES, split_axis=0, concat_axis=0, tiled=True)
    modulation = jnp.sum(mod_parts, axis=0) + bias_full.astype(wide_type)[None, :]
    qkv_full = lax.all_gather(qkv_weight.astype(low_type), AXES, axis=0, tiled=True)
    out_full = lax.all_gather(out_weight.astype(low_type), AXES, axis=0, tiled=True)
    up_full = lax.all_gather(up_weight.astype(low_type), AXES, axis=0, tiled=True)
    down_full = lax.all_gather(down_weight.astype(low_type), AXES, axis=0, tiled=True)
    def times_qkv(v):
        return jnp.dot(v, qkv_full, preferred_element_type=wide_type)
    def times_qkv_back(v):
        return jnp.dot(v, qkv_full.T, preferred_element_type=wide_type)
    def times_up(v):
        return jnp.dot(v, up_full, preferred_element_type=wide_type)
    def times_up_back(v):
        return jnp.dot(v, up_full.T, preferred_element_type=wide_type)
    arrived = lax.all_to_all(kept_tokens, AXES, split_axis=1, concat_axis=0, tiled=True)
    received = arrived.reshape(devices * slots, D)
    keep_flat = keep_mask.reshape(count)
    keep_float = keep_flat.astype(wide_type)
    ranks = running_rank(keep_flat)
    target = ranks % devices * slots + ranks // devices
    columns = jnp.arange(devices * slots, dtype=jnp.int32)
    selector = jnp.where((keep_flat[:, None] == 1) & (target[:, None] == columns[None, :]), 1.0, 0.0).astype(wide_type)
    stream_in = jnp.dot(selector.astype(low_type), received, preferred_element_type=wide_type)
    stream_in = stream_in + (1.0 - keep_float)[:, None] * token_full.astype(wide_type)[None, :]
    stream_in = stream_in.reshape(images, PATCHES, D)
    shift_one, scale_one, gate_one, shift_two, scale_two, gate_two = jnp.split(
        modulation[:, None, :], 6, axis=-1
    )
    normed_one = modulate(stream_in, shift_one, scale_one).astype(low_type).reshape(count, D)
    projected = times_qkv(normed_one).astype(low_type)
    projected = projected.reshape(images, PATCHES, 3, HEADS, HEAD_DIM)
    queries = projected[:, :, 0]
    key_rows = projected[:, :, 1]
    value_rows = projected[:, :, 2]
    relative = expand_bias(position_bias, GRID)
    scores = (
        jnp.einsum("iqhd,ikhd->ihqk", queries, key_rows, preferred_element_type=wide_type) * factor
        + relative[None]
    )
    att_weights = jax.nn.softmax(scores, axis=-1)
    att_low = att_weights.astype(low_type)
    mixed = (
        jnp.einsum("ihqk,ikhd->iqhd", att_low, value_rows, preferred_element_type=wide_type)
        .astype(low_type)
        .reshape(count, D)
    )
    branch = jnp.dot(mixed, out_full, preferred_element_type=wide_type).reshape(images, PATCHES, D)
    stream_mid = stream_in + gate_one * branch
    normed_two = modulate(stream_mid, shift_two, scale_two).astype(low_type).reshape(count, D)
    hidden = times_up(normed_two)
    activated = gelu_tanh(hidden).astype(low_type)
    down = jnp.dot(activated, down_full, preferred_element_type=wide_type).reshape(
        images, PATCHES, D
    )
    block_out = (stream_mid + gate_two * down).reshape(count, D).astype(low_type)
    incoming = cotangent.astype(wide_type).reshape(images, PATCHES, D)
    grad_gate_two = jnp.sum(incoming * down, axis=1)
    grad_down = (gate_two * incoming).astype(low_type).reshape(count, D)
    grad_activated = jnp.dot(grad_down, down_full.T, preferred_element_type=wide_type)
    _, gelu_pull = jax.vjp(gelu_tanh, hidden)
    grad_hidden = gelu_pull(grad_activated)[0].astype(low_type)
    grad_normed_two = times_up_back(grad_hidden).reshape(
        images, PATCHES, D
    )
    _, norm_pull_two = jax.vjp(modulate, stream_mid, shift_two, scale_two)
    grad_mid_norm, grad_shift_two, grad_scale_two = norm_pull_two(grad_normed_two)
    grad_mid = incoming + grad_mid_norm
    grad_gate_one = jnp.sum(grad_mid * branch, axis=1)
    grad_branch = (gate_one * grad_mid).astype(low_type).reshape(count, D)
    grad_mixed = jnp.dot(grad_branch, out_full.T, preferred_element_type=wide_type).astype(low_type)
    grad_mixed = grad_mixed.reshape(images, PATCHES, HEADS, HEAD_DIM)
    grad_att = jnp.einsum(
        "iqhd,ikhd->ihqk", grad_mixed, value_rows, preferred_element_type=wide_type
    )
    grad_values = jnp.einsum(
        "ihqk,iqhd->ikhd", att_low, grad_mixed, preferred_element_type=wide_type
    )
    grad_scores = (
        att_weights * (grad_att - jnp.sum(att_weights * grad_att, axis=-1, keepdims=True))
    ).astype(low_type)
    grad_queries = (
        jnp.einsum("ihqk,ikhd->iqhd", grad_scores, key_rows, preferred_element_type=wide_type)
        * factor
    )
    grad_keys = (
        jnp.einsum("ihqk,iqhd->ikhd", grad_scores, queries, preferred_element_type=wide_type)
        * factor
    )
    grad_table = bias_adjoint(jnp.sum(grad_scores.astype(wide_type), axis=0), GRID)
    grad_projected = (
        jnp.stack([grad_queries, grad_keys, grad_values], axis=2)
        .astype(low_type)
        .reshape(count, 3 * D)
    )
    grad_normed_one = times_qkv_back(grad_projected).reshape(
        images, PATCHES, D
    )
    _, norm_pull_one = jax.vjp(modulate, stream_in, shift_one, scale_one)
    grad_in_norm, grad_shift_one, grad_scale_one = norm_pull_one(grad_normed_one)
    grad_in = (grad_mid + grad_in_norm).reshape(count, D)
    grad_modulation = jnp.concatenate(
        [
            grad_shift_one[:, 0],
            grad_scale_one[:, 0],
            grad_gate_one,
            grad_shift_two[:, 0],
            grad_scale_two[:, 0],
            grad_gate_two,
        ],
        axis=-1,
    ).astype(low_type)
    grad_mod_all = lax.all_gather(grad_modulation, AXES, axis=0, tiled=True)
    grad_ada = lax.dot_general(silu_part, grad_mod_all, (((0,), (0,)), ((), ())), preferred_element_type=wide_type)
    bias_share = 6 * D // devices
    sum_bias = jnp.sum(lax.dynamic_slice_in_dim(grad_mod_all, me * bias_share, bias_share, axis=1).astype(wide_type), axis=0)
    silu_parts = lax.dot_general(grad_mod_all, ada_low, (((1,), (1,)), ((), ())), preferred_element_type=wide_type)
    silu_parts = lax.all_to_all(silu_parts.reshape(devices, images, rows), AXES, split_axis=0, concat_axis=0, tiled=True)
    grad_silu = silu_parts.transpose(1, 0, 2).reshape(images, D)
    _, silu_pull = jax.vjp(jax.nn.silu, conditioning)
    grad_cond = silu_pull(grad_silu)[0]
    grad_mask = jnp.sum((1.0 - keep_float)[:, None] * grad_in, axis=0)
    grad_received = jnp.dot(
        selector.T, grad_in, precision=lax.Precision.HIGHEST, preferred_element_type=wide_type
    ).astype(low_type)
    grad_kept = lax.all_to_all(
        grad_received.reshape(devices, 1, slots, D),
        ("wide", "narrow"),
        split_axis=0,
        concat_axis=1,
        tiled=True,
    )
    def scatter(left, right):
        partial = lax.dot_general(left, right, (((0,), (0,)), ((), ())), preferred_element_type=wide_type)
        return lax.psum_scatter(partial.reshape(-1), AXES, scatter_dimension=0, tiled=True).reshape(-1, right.shape[1])
    sum_qkv = scatter(normed_one, grad_projected)
    sum_out = scatter(mixed, grad_branch)
    sum_up = scatter(normed_two, grad_hidden)
    sum_down = scatter(activated, grad_down)
    grad_table_all, mask_whole = lax.psum((grad_table, grad_mask), AXES)
    mask_share = D // devices
    sum_mask = lax.dynamic_slice_in_dim(mask_whole, me * mask_share, mask_share)
    return (block_out, grad_kept, grad_cond, grad_ada, sum_bias, sum_qkv, sum_out, sum_up, sum_down, grad_table_all, sum_mask)


def rounded(v):
    return lax.reduce_precision(v, 8, 7)


def per_device(kept_tokens, keep_mask, conditioning, ada_weight, ada_bias, qkv_weight, out_weight, up_weight, down_weight, position_bias, mask_token, cotangent):
    if kept_tokens.shape[2] > 8 or conditioning.shape[0] != 1:
        return per_device_plain(kept_tokens, keep_mask, conditioning, ada_weight, ada_bias, qkv_weight, out_weight, up_weight, down_weight, position_bias, mask_token, cotangent)
    wide_count = lax.axis_size("wide")
    devices = wide_count * lax.axis_size("narrow")
    slots = kept_tokens.shape[2]
    rows = qkv_weight.shape[0]
    share = ada_bias.shape[0]
    me = lax.axis_index(AXES)
    zc = wide_count // 2
    silu_out = jnp.pad(rounded(jax.nn.silu(conditioning)).reshape(devices, 1, rows), ((0, 0), (0, 7), (0, 128 - rows)))
    bias_row = lax.dynamic_update_slice(jnp.zeros((1, 6 * D), F32), rounded(ada_bias)[None], (0, me * share))
    token_row = lax.dynamic_update_slice(jnp.zeros((1, D), F32), rounded(mask_token)[None], (0, me * rows))
    kept = jnp.pad(kept_tokens.reshape(devices, slots, D), ((0, 0), (0, 8 - slots), (0, 0)))
    table = jnp.pad(position_bias, ((0, 0), (0, 1), (0, 128 - position_bias.shape[2]))).reshape(HEADS * 2 * GRID, 128)
    keep = keep_mask.reshape(PATCHES, 1)
    keep_float = keep.astype(F32)

    (full, one_t, projected, att, mixed_t, branch, stream_mid, two_t, hidden, sum_down_part, stream_in, block_out, mod, silu_part, selector, gate_sum) = run_forward(
        qkv_weight, out_weight, up_weight, down_weight, silu_out, ada_weight, bias_row, token_row, kept, keep, table, cotangent, zc)
    sum_down, turned, grad_ada, mod_total, silu_back, kept_grad, table_grad, token_grad = run_backward(
        full, mod, cotangent, stream_in, stream_mid, branch, projected, att, hidden, one_t, mixed_t, two_t, sum_down_part,
        ada_weight, silu_part, selector, keep, gate_sum, zc)

    sum_bias = lax.dynamic_slice(mod_total[:54].reshape(-1), (me * share,), (share,))
    sum_mask = lax.dynamic_slice(token_grad[:9].reshape(-1), (me * rows,), (rows,))
    _, silu_pull = jax.vjp(jax.nn.silu, conditioning)
    grad_cond = silu_pull(silu_back[:, 0, :rows].reshape(1, D))[0]
    grad_kept = kept_grad[None, :, :slots]
    offsets = position_bias.shape[2]
    grad_table = table_grad.reshape(HEADS, 2 * GRID, 128)[:, :offsets, :offsets]
    sum_qkv = turned[:3, 0].transpose(1, 0, 2).reshape(rows, 3 * D).astype(F32)
    sum_out = turned[3, 0].astype(F32)
    sum_up = turned[:, 1].transpose(1, 0, 2).reshape(rows, FF).astype(F32)
    return (block_out, grad_kept, grad_cond, grad_ada, sum_bias, sum_qkv, sum_out, sum_up, sum_down, grad_table, sum_mask)


def solution(mesh):
    in_specs = (
        P(("wide", "narrow"), None, None, None),
        P(("wide", "narrow"), None),
        P(("wide", "narrow"), None),
        P(("wide", "narrow"), None),
        P(("wide", "narrow")),
        P(("wide", "narrow"), None),
        P(("wide", "narrow"), None),
        P(("wide", "narrow"), None),
        P(("wide", "narrow"), None),
        P(),
        P(("wide", "narrow")),
        P(("wide", "narrow"), None),
    )
    out_specs = (
        P(("wide", "narrow"), None),
        P(("wide", "narrow"), None, None, None),
        P(("wide", "narrow"), None),
        P(("wide", "narrow"), None),
        P(("wide", "narrow")),
        P(("wide", "narrow"), None),
        P(("wide", "narrow"), None),
        P(("wide", "narrow"), None),
        P(("wide", "narrow"), None),
        P(),
        P(("wide", "narrow")),
    )
    shape = dict(mesh.shape)
    rows = D // (shape["wide"] * shape["narrow"])
    fast = shape["narrow"] == 4 and shape["wide"] % 2 == 0 and rows * 4 == ROWS
    return jax.shard_map(
        per_device if fast else per_device_plain, mesh=mesh, in_specs=in_specs, out_specs=out_specs, check_vma=False
    )
```
